128 devices in a mesh: row: 8 (over y, x_hi), col: 8 (over z, core), slide: 2 (over x_lo).
Axes of the slice: x: 4 (x_hi: 2, x_lo: 2; x = x_hi * 2 + x_lo), y: 4, z: 4, core: 2. Of those that a mesh axis runs over, the one named last changes fastest.
Arguments:
- tokens_in: bfloat16 [2, 128, 128, 256], P('slide', 'row', 'col'), may hold values from -6 to 6
- out_cotangent: bfloat16 [2, 128, 128, 256], P('slide', 'row', 'col'), may hold values from -6 to 6
- w_inner: bfloat16 [256, 1024], replicated, may hold values from -0.375 to 0.375
- w_ssm: bfloat16 [256, 40], replicated, may hold values from -0.375 to 0.375
- dt_bias: float32 [8], replicated, may hold values from -1 to 1
- decay_rate: float32 [8], replicated, may hold values from 0.001 to 0.03
- skip_gain: float32 [8], replicated, may hold values from 0.5 to 1.5
- norm_gain: float32 [512], replicated, may hold values from 0.5 to 1.5
- w_out: bfloat16 [512, 256], replicated, may hold values from -0.25 to 0.25
Outputs:
- layer_out: bfloat16 [2, 128, 128, 256], P('slide', 'row', 'col')
- grad_tokens: bfloat16 [2, 128, 128, 256], P('slide', 'row', 'col')
- grad_inner: float32 [256, 1024], replicated
- grad_ssm: float32 [256, 40], replicated
- grad_out: float32 [512, 256], replicated
- grad_bias: float32 [8], replicated
- grad_rate: float32 [8], replicated
- grad_skip: float32 [8], replicated
- grad_gain: float32 [512], replicated
The draws below stay inside these ranges and needn't reach their ends.
All inputs are finite; a program needn't handle non-finite values.
Results may differ from the reference program's by a relative error of at most 0.0049.
Values sent between devices are 32-bit elements; how exact they have to be, the bound alone decides.
A program may use at most 128 MiB of HBM per device.

```python
import math
import jax
import jax.numpy as jnp
from jax import lax

D = 256
HEADS = 8
HDIM = 64
STATE = 16
E = 512
ROWS = 128
COLS = 128
SLIDES = 2
N_ROW = 8
N_COL = 8


def shard_levels(own_key, shape, pieces, smallest, high):
    factor_of, own = 1.0, jax.random.fold_in(own_key, 6)
    for axis_at, shards_of in pieces:
        draws = jnp.exp(jax.random.uniform(jax.random.fold_in(own, axis_at), (shards_of,), jnp.float32, smallest / len(pieces), high / len(pieces)))
        factor_of = factor_of * jnp.repeat(draws, shape[axis_at] // shards_of).reshape([-1 if axis == axis_at else 1 for axis in range(len(shape))])
    return factor_of


def centred(own_key, shape, spread, most, cuts=(), kind=jnp.bfloat16):
    gain = shard_levels(own_key, shape, cuts, -0.22, 0.18) if cuts else 1.0
    array = jax.random.normal(own_key, shape, jnp.float32) * spread * gain
    return jnp.minimum(jnp.maximum(array, -most), most).astype(kind)


def setup_inputs(seed: int = 0) -> dict:
    streams_of = jax.random.split(jax.random.key(seed), 10)
    return {
        "tokens_in": centred(streams_of[0], (SLIDES, ROWS, COLS, D), 1.0, 6.0, ((0, 2), (1, 8), (2, 8))),
        "out_cotangent": centred(streams_of[1], (SLIDES, ROWS, COLS, D), 1.0, 6.0, ((0, 2), (1, 8), (2, 8))),
        "w_inner": centred(streams_of[2], (D, 2 * E), D ** -0.5, 0.375),
        "w_ssm": centred(streams_of[3], (D, 2 * STATE + HEADS), D ** -0.5, 0.375),
        "dt_bias": jnp.clip(jax.random.uniform(streams_of[4], (HEADS,), jnp.float32, -1.0, 1.0), -1.0, 1.0),
        "decay_rate": jnp.clip(jnp.exp(jax.random.uniform(streams_of[5], (HEADS,), jnp.float32, math.log(0.001), math.log(0.03))), 0.001, 0.03),
        "skip_gain": jnp.clip(jax.random.uniform(streams_of[6], (HEADS,), jnp.float32, 0.5, 1.5), 0.5, 1.5),
        "norm_gain": jnp.clip(1.0 + 0.1 * jax.random.normal(streams_of[7], (E,), jnp.float32), 0.5, 1.5),
        "w_out": centred(streams_of[8], (E, D), E ** -0.5, 0.25),
    }


highest = lax.Precision.HIGHEST

def split_terms(projected, ssm_proj, dt_bias, decay_rate):
    leading = projected.shape[:-1]
    halfway = projected.shape[-1] // 2
    mixer_in = projected[..., :halfway].reshape(leading + (HEADS, HDIM))
    gate_in = projected[..., halfway:]
    step_size = jax.nn.softplus(ssm_proj[..., 2 * STATE:] + dt_bias)
    return (mixer_in, gate_in, step_size[..., None] * mixer_in, -step_size * decay_rate, ssm_proj[..., :STATE], ssm_proj[..., STATE:2 * STATE])

def block_out(drive, decay_log, in_map, out_map, state_in):
    cumulative = jnp.cumsum(decay_log, axis=1)
    block_len = drive.shape[1]
    causal = jnp.arange(block_len)[:, None] >= jnp.arange(block_len)[None, :]
    log_gaps = cumulative[:, :, None, :] - cumulative[:, None, :, :]
    decay_mask = jnp.exp(jnp.where(causal[None, :, :, None], log_gaps, -jnp.inf))
    scores = jnp.einsum('sin,sjn->sij', out_map, in_map, precision=highest)
    within = jnp.einsum('sijh,sij,sjhp->sihp', decay_mask, scores, drive, precision=highest)
    carried = jnp.einsum('sin,shpn->sihp', out_map, state_in, precision=highest)
    return within + jnp.exp(cumulative)[..., None] * carried

def block_terms(drive, decay_log, in_map):
    cumulative = jnp.cumsum(decay_log, axis=1)
    final_log = cumulative[:, -1]
    weight = jnp.exp(final_log[:, None, :] - cumulative)
    summary = jnp.einsum('sjh,sjn,sjhp->shpn', weight, in_map, drive, precision=highest)
    return (jnp.exp(final_log), summary)

def rows_view(tensor):
    return tensor.reshape((-1,) + tensor.shape[2:])

def cols_view(tensor):
    swapped = jnp.swapaxes(tensor, 1, 2)
    return swapped.reshape((-1,) + swapped.shape[2:])

def sweep(drive, decay_log, in_map, out_map, block_count):
    lane_count, length_all = drive.shape[:2]
    block_len = length_all // block_count

    def split_blocks(tensor):
        return jnp.moveaxis(tensor.reshape((lane_count, block_count, block_len) + tensor.shape[2:]), 1, 0)

    def advance(carry_state, blocks):
        drive_piece, decay_piece, inmap_piece, outmap_piece = blocks
        piece_out = block_out(drive_piece, decay_piece, inmap_piece, outmap_piece, carry_state)
        total_decay, fresh = block_terms(drive_piece, decay_piece, inmap_piece)
        return (total_decay[..., None, None] * carry_state + fresh, piece_out)
    initial = jnp.zeros((lane_count, HEADS, HDIM, STATE), jnp.float32)
    final_state, outputs = lax.scan(advance, initial, (split_blocks(drive), split_blocks(decay_log), split_blocks(in_map), split_blocks(out_map)))
    return jnp.moveaxis(outputs, 0, 1).reshape(drive.shape)

def inner_layer(projected, ssm_proj, dt_bias, decay_rate, skip_gain, norm_gain):
    mixer_in, gate_in, drive, decay_log, in_map, out_map = split_terms(projected, ssm_proj, dt_bias, decay_rate)
    terms = (drive, decay_log, in_map, out_map)
    row_out = sweep(*[rows_view(tensor) for tensor in terms], N_COL).reshape(drive.shape)
    col_out = sweep(*[cols_view(tensor) for tensor in terms], N_ROW)
    col_out = jnp.swapaxes(col_out.reshape((projected.shape[0], projected.shape[2], projected.shape[1]) + col_out.shape[2:]), 1, 2)
    mixed = row_out + col_out + skip_gain[:, None] * mixer_in
    gated = mixed.reshape(projected.shape[:-1] + (-1,)) * jax.nn.silu(gate_in)
    inv_rms = lax.rsqrt(lax.optimization_barrier(jnp.mean(gated * gated, axis=-1, keepdims=True)) + 1e-05)
    return gated * inv_rms * norm_gain

def outer_sum(left, right):
    return lax.dot_general(left, right, (((0,), (0,)), ((), ())), preferred_element_type=jnp.float32)

def reference(tokens_in, out_cotangent, w_inner, w_ssm, dt_bias, decay_rate, skip_gain, norm_gain, w_out):
    out_list = []
    grad_list = []
    totals = [jnp.zeros(w_inner.shape, jnp.float32), jnp.zeros(w_ssm.shape, jnp.float32), jnp.zeros(w_out.shape, jnp.float32), jnp.zeros(dt_bias.shape, jnp.float32), jnp.zeros(decay_rate.shape, jnp.float32), jnp.zeros(skip_gain.shape, jnp.float32), jnp.zeros(norm_gain.shape, jnp.float32)]
    for which_slide in range(SLIDES):
        tokens = tokens_in[which_slide].reshape(-1, D)
        cotangent = out_cotangent[which_slide].reshape(-1, D)
        projected = jnp.dot(tokens, w_inner, preferred_element_type=jnp.float32).reshape(1, ROWS, COLS, -1)
        ssm_proj = jnp.dot(tokens, w_ssm, preferred_element_type=jnp.float32).reshape(1, ROWS, COLS, -1)
        normed_f, pullback = jax.vjp(inner_layer, projected, ssm_proj, dt_bias, decay_rate, skip_gain, norm_gain)
        normed = normed_f.astype(jnp.bfloat16).reshape(-1, E)
        out_list.append(jnp.dot(normed, w_out, preferred_element_type=jnp.float32).astype(jnp.bfloat16).reshape(ROWS, COLS, D))
        d_normed = lax.dot_general(cotangent, w_out, (((1,), (1,)), ((), ())), preferred_element_type=jnp.float32)
        d_proj, d_ssm, d_bias, d_rate, d_skip, d_gain = pullback(d_normed.reshape(normed_f.shape))
        d_proj = d_proj.reshape(-1, 2 * E).astype(jnp.bfloat16)
        d_ssm = d_ssm.reshape(-1, 2 * STATE + HEADS).astype(jnp.bfloat16)
        back_proj = lax.dot_general(d_proj, w_inner, (((1,), (1,)), ((), ())), preferred_element_type=jnp.float32)
        back_proj = back_proj + lax.dot_general(d_ssm, w_ssm, (((1,), (1,)), ((), ())), preferred_element_type=jnp.float32)
        grad_list.append(back_proj.astype(jnp.bfloat16).reshape(ROWS, COLS, D))
        totals = [totals[0] + outer_sum(tokens, d_proj), totals[1] + outer_sum(tokens, d_ssm), totals[2] + outer_sum(normed, cotangent), totals[3] + d_bias, totals[4] + d_rate, totals[5] + d_skip, totals[6] + d_gain]
    factor = 1.0 / jnp.sqrt(jnp.float32(SLIDES * ROWS * COLS))
    totals = [member * factor for member in totals]
    return (jnp.stack(out_list), jnp.stack(grad_list), totals[0], totals[1], totals[2], totals[3], totals[4], totals[5], totals[6])
```

```python
import functools

import jax
import jax.numpy as jnp
from jax import lax
from jax.experimental import pallas as pl
from jax.experimental.pallas import tpu as pltpu
from jax.sharding import PartitionSpec as P

MESH = pl.DeviceIdType.MESH
F32 = jnp.float32
BF16 = jnp.bfloat16
HEADS = 8
HDIM = 64
STATE = 16
SIDE = 16
T = SIDE * SIDE
E = HEADS * HDIM
D = 256
CH = 4
CR = 128 // CH
NEG = -1e30
EARLY = 2048
LATE = 1280


def mm(a, b, ca=1, cb=0):
    return lax.dot_general(a, b, (((ca,), (cb,)), ((), ())), preferred_element_type=F32)


def split(x, terms):
    out = []
    for _ in range(terms - 1):
        hi = x.astype(BF16)
        out.append(hi)
        x = x - hi.astype(F32)
    out.append(x.astype(BF16))
    return out


def pick(mask, x, terms=3):
    return functools.reduce(lambda u, v: u + v, [mm(mask, part) for part in split(x, terms)])


def spread(x, mask, terms=2):
    return functools.reduce(lambda u, v: u + v, [mm(part, mask) for part in split(x, terms)])


def mm3(a, b, ca=1, cb=0):
    (ah, al), (bh, bl) = a, b
    return mm(ah, bh, ca, cb) + (mm(ah, bl, ca, cb) + mm(al, bh, ca, cb))


def keep(pair, where, x):
    hi, lo = split(x, 2)
    pair[(0,) + where] = hi
    pair[(1,) + where] = lo


def both(pair):
    return pair[0], pair[1]


def only(mask, pair):
    nil = jnp.zeros(mask.shape, BF16)
    return jnp.where(mask, pair[0], nil), jnp.where(mask, pair[1], nil)


def ind(cond):
    return jnp.where(cond, 1.0, 0.0).astype(BF16)


def grid2(rows, cols):
    return (
        lax.broadcasted_iota(jnp.int32, (rows, cols), 0),
        lax.broadcasted_iota(jnp.int32, (rows, cols), 1),
    )


def hi4(x):
    return lax.shift_right_logical(x, 4)


def lo4(x):
    return jnp.bitwise_and(x, 15)


def head_spread():
    r, c = grid2(128, E)
    return ind(r == lax.shift_right_logical(c, 6))


def head_sum(x):
    r, c = grid2(E, 128)
    return spread(x, ind(lax.shift_right_logical(r, 6) == c), 2)


def place():
    row, col, slide = lax.axis_index("row"), lax.axis_index("col"), lax.axis_index("slide")
    return dict(y=row // 2, xh=lax.rem(row, 2), z=col // 2, co=lax.rem(col, 2), xl=slide)


def at(pos, **change):
    p = dict(pos, **change)
    return (p["y"] * 2 + p["xh"], p["z"] * 2 + p["co"], p["xl"])


def flip(bit, by):
    return bit + by * (1 - 2 * bit)


def peers(pos, axis):
    out = []
    for d in (1, 2, 3):
        if axis == "x":
            out.append(at(pos, xh=flip(pos["xh"], d // 2), xl=flip(pos["xl"], d % 2)))
        else:
            out.append(at(pos, **{axis: xor4(pos[axis], d)}))
    return out


def xor4(q, d):
    return 2 * flip(q // 2, d // 2) + flip(lax.rem(q, 2), d % 2)


def remote(src, dst, ssem, rsem, to):
    return pltpu.make_async_remote_copy(
        src_ref=src, dst_ref=dst, send_sem=ssem, recv_sem=rsem, device_id=to, device_id_type=MESH
    )


class Chain:
    def __init__(self, pos, axis, back, own, got, into, send, ret, res, dec, deco, ssem, rsem, slot):
        self.bit, step = ("co", "z") if axis == "r" else ("xh", "y")
        b, q = pos[self.bit], pos[step]
        self.b = b
        self.first = (b == 1) if back else (b == 0)
        self.r = (3 - q) if back else q
        self.nxt = at(pos, **{step: lax.rem(q + (3 if back else 1), 4)})
        self.partner = at(pos, **{self.bit: 1 - b})
        self.own, self.got, self.into, self.send, self.ret, self.res = own, got, into, send, ret, res
        self.dec, self.deco = dec, deco
        self.ssem, self.rsem, self.slot = ssem, rsem, slot

    def half(self, mine, c):
        start = (self.b if mine else 1 - self.b) * 128 + c * CR
        return pl.ds(pl.multiple_of(start, CR), CR)

    def sems(self, stage, c):
        return self.ssem.at[self.slot, stage, c], self.rsem.at[self.slot, stage, c]

    def c_exch(self, c):
        return remote(self.own.at[self.half(False, c)], self.got.at[pl.ds(c * CR, CR)], *self.sems(0, c), self.partner)

    def c_hop(self, c):
        return remote(self.send.at[pl.ds(c * CR, CR)], self.into.at[pl.ds(c * CR, CR)], *self.sems(1, c), self.nxt)

    def c_ret(self, c):
        return remote(self.ret.at[pl.ds(c * CR, CR)], self.res.at[self.half(True, c)], *self.sems(2, c), self.partner)

    def start(self):
        @pl.when(self.r == 0)
        def _():
            self.into[...] = jnp.zeros((128, E), F32)

        for c in range(CH):
            self.c_exch(c).start()

    def pair(self, c):
        sl = pl.ds(c * CR, CR)
        self.c_exch(c).wait_recv()
        got, own = self.got[sl], self.own[self.half(True, c)]
        d_own, d_oth = self.dec[self.half(True, c)], self.deco[sl]
        lead = jnp.where(self.first, own, got)
        tail = jnp.where(self.first, got, own)
        d_tail = jnp.where(self.first, d_oth, d_own)
        self.send[sl] = tail + d_tail * lead

        @pl.when(self.r == 0)
        def _():
            self.c_hop(c).start()

    def hop(self, c):
        sl = pl.ds(c * CR, CR)

        @pl.when(self.r > 0)
        def _():
            self.c_hop(c).wait_recv()

        enter = self.into[sl]
        d_own, d_oth = self.dec[self.half(True, c)], self.deco[sl]

        @pl.when((self.r > 0) & (self.r < 3))
        def _():
            self.send[sl] = self.send[sl] + d_own * d_oth * enter
            self.c_hop(c).start()

        lead = jnp.where(self.first, self.own[self.half(True, c)], self.got[sl])
        d_lead = jnp.where(self.first, d_own, d_oth)
        after = d_lead * enter + lead
        self.ret[sl] = jnp.where(self.first, after, enter)
        self.c_ret(c).start()
        self.res[self.half(True, c)] = jnp.where(self.first, enter, after)

    def finish(self):
        for c in range(CH):
            self.c_ret(c).wait_recv()

    def drain(self):
        for c in range(CH):
            self.c_exch(c).wait_send()
            self.c_ret(c).wait_send()

            @pl.when(self.r < 3)
            def _():
                self.c_hop(c).wait_send()


def run_hops(a, c):
    @pl.when(a.r <= c.r)
    def _():
        for who, at_chunk in ((a, 0), (a, 1), (c, 0), (a, 2), (c, 1), (a, 3), (c, 2), (c, 3)):
            who.hop(at_chunk)

    @pl.when(a.r > c.r)
    def _():
        for who, at_chunk in ((c, 0), (c, 1), (a, 0), (c, 2), (a, 1), (c, 3), (a, 2), (a, 3)):
            who.hop(at_chunk)


class Total:
    def __init__(self, pos, buf, out, cbuf, xbuf, ybuf, zbuf, ssem, rsem):
        n = buf.shape[0]
        self.pos, self.buf, self.out = pos, buf, out
        self.cbuf, self.xbuf, self.ybuf, self.zbuf = cbuf, xbuf, ybuf, zbuf
        self.ssem, self.rsem = ssem, rsem
        self.nh = n // 2
        self.base = pos["co"] * self.nh
        self.other = at(pos, co=1 - pos["co"])
        index = {"x": pos["xh"] * 2 + pos["xl"], "y": pos["y"], "z": pos["z"]}
        third = -(-self.nh // 384) * 128
        sizes = (third, third, self.nh - 2 * third)
        self.parts, offset = [], 0
        for size, order in zip(sizes, ("xyz", "yzx", "zxy")):
            start = self.base + offset
            first = start + index[order[0]] * (size // 4)
            second = first + index[order[1]] * (size // 16)
            self.parts.append((order, index[order[0]], index[order[1]], size, offset, start, first, second))
            offset += size

    def rows(self, start, size):
        return pl.ds(pl.multiple_of(start, 8), size)

    def copies(self, stage):
        pos = self.pos
        if stage in (0, 6):
            src = self.buf.at[self.rows((1 - pos["co"]) * self.nh, self.nh)]
            own = self.out.at[self.rows(self.base, self.nh)]
            src, dst = (src, self.cbuf) if stage == 0 else (own, own)
            return [remote(src, dst, self.ssem.at[stage, 0], self.rsem.at[stage, 0], self.other)]
        out = []
        for p, (order, g0, g1, size, offset, start, first, second) in enumerate(self.parts):
            n0, n1 = size // 4, size // 16
            axis = order[(0, 1, 2, 1, 0)[stage - 1]]
            for d, to in enumerate(peers(pos, axis)):
                if stage == 1:
                    src = self.buf.at[self.rows(start + xor4(g0, d + 1) * n0, n0)]
                    dst = self.xbuf.at[d, pl.ds(offset // 4, n0)]
                elif stage == 2:
                    src = self.buf.at[self.rows(first + xor4(g1, d + 1) * n1, n1)]
                    dst = self.ybuf.at[d, pl.ds(offset // 16, n1)]
                elif stage == 3:
                    src, dst = self.buf.at[self.rows(second, n1)], self.zbuf.at[d, pl.ds(offset // 16, n1)]
                elif stage == 4:
                    src = dst = self.out.at[self.rows(second, n1)]
                else:
                    src = dst = self.out.at[self.rows(first, n0)]
                k = 3 * p + d
                out.append(remote(src, dst, self.ssem.at[stage, k], self.rsem.at[stage, k], to))
        return out

    def start(self, stage):
        for copy in self.copies(stage):
            copy.start()

    def finish(self, stage):
        for copy in self.copies(stage):
            copy.wait()
        if stage == 0:
            sl = self.rows(self.base, self.nh)
            self.buf[sl] = self.buf[sl] + self.cbuf[...]
        if stage not in (1, 2, 3):
            return
        came = (self.xbuf, self.ybuf, self.zbuf)[stage - 1]
        to = self.out if stage == 3 else self.buf
        for order, g0, g1, size, offset, start, first, second in self.parts:
            share = 4 if stage == 1 else 16
            sl = self.rows(first if stage == 1 else second, size // share)
            at_ = pl.ds(offset // share, size // share)
            to[sl] = (self.buf[sl] + came[0, at_]) + (came[1, at_] + came[2, at_])

    def step(self, stage):
        self.finish(stage)
        if stage < 6:
            self.start(stage + 1)


def kernel(factor, *refs):
    names_in = ["tok", "cot", "wi", "ws", "bias", "rate", "skip", "gain", "wo"]
    names_out = ["lo", "gt", "eres", "lres"]
    n_io = len(names_in) + len(names_out)
    k = dict(zip(names_in + names_out, refs[:n_io]))
    k.update(zip([name for name, _ in SCRATCH], refs[n_io:]))
    body(factor, **k)


def vm(*shape, dtype=F32):
    return pltpu.VMEM(shape, dtype)


BIG = (T, E)
SCRATCH = [
    ("x", vm(*BIG)), ("z", vm(*BIG)), ("ub", vm(2, *BIG, dtype=BF16)), ("stepe", vm(*BIG)),
    ("bt", vm(2, T, T, dtype=BF16)), ("ct", vm(2, T, T, dtype=BF16)), ("s", vm(T, T)), ("ds", vm(T, T)),
    ("wsel", vm(D, 640, dtype=BF16)), ("wpad", vm(D, 128, dtype=BF16)), ("vecs", vm(8, 128)),
    ("step", vm(T, 128)), ("sig", vm(T, 128)),
    ("cumr", vm(T, 128)), ("cumc", vm(T, 128)), ("cumrt", vm(128, T)), ("cumct", vm(128, T)),
    ("er", vm(*BIG)), ("ec", vm(*BIG)), ("wr", vm(*BIG)), ("wc", vm(*BIG)), ("dr", vm(*BIG)), ("dc", vm(*BIG)),
    ("dro", vm(128, E)), ("dco", vm(128, E)),
    ("finr", vm(SIDE, 128)), ("finc", vm(SIDE, 128)), ("finro", vm(SIDE, 128)), ("finco", vm(SIDE, 128)),
    ("wur", vm(2, *BIG, dtype=BF16)), ("wuc", vm(2, *BIG, dtype=BF16)),
    ("edr", vm(2, *BIG, dtype=BF16)), ("edc", vm(2, *BIG, dtype=BF16)),
    ("mr", vm(2, HEADS, T, T, dtype=BF16)), ("mc", vm(2, HEADS, T, T, dtype=BF16)), ("ls", vm(HEADS, T, T)),
    ("yr", vm(*BIG)), ("yc", vm(*BIG)), ("car", vm(*BIG)), ("cac", vm(*BIG)), ("dn", vm(*BIG)),
    ("dy", vm(*BIG)), ("dyb", vm(2, *BIG, dtype=BF16)), ("dzb", vm(*BIG, dtype=BF16)), ("nb", vm(*BIG, dtype=BF16)),
    ("qr", vm(*BIG)), ("qc", vm(*BIG)), ("dxb", vm(*BIG, dtype=BF16)), ("dux", vm(*BIG)),
    ("dbe", vm(T, T)), ("dce", vm(T, T)),
    ("own", pltpu.VMEM((4, T, E), F32)), ("got", pltpu.VMEM((4, 128, E), F32)), ("into", pltpu.VMEM((4, 128, E), F32)),
    ("send", pltpu.VMEM((4, 128, E), F32)), ("ret", pltpu.VMEM((4, 128, E), F32)), ("res", pltpu.VMEM((4, T, E), F32)),
    ("ebuf", vm(EARLY, 128)), ("ecb", vm(EARLY // 2, 128)), ("exb", vm(3, EARLY // 8, 128)),
    ("eyb", vm(3, EARLY // 32, 128)), ("ezb", vm(3, EARLY // 32, 128)),
    ("lbuf", vm(LATE, 128)), ("lcb", vm(LATE // 2, 128)), ("lxb", vm(3, LATE // 8, 128)),
    ("lyb", vm(3, LATE // 32, 128)), ("lzb", vm(3, LATE // 32, 128)),
    ("fsem", pltpu.SemaphoreType.DMA((2, 2))),
    ("cs", pltpu.SemaphoreType.DMA((4, 3, CH))), ("cr", pltpu.SemaphoreType.DMA((4, 3, CH))),
    ("es", pltpu.SemaphoreType.DMA((7, 9))), ("erv", pltpu.SemaphoreType.DMA((7, 9))),
    ("lsm", pltpu.SemaphoreType.DMA((7, 9))), ("lrv", pltpu.SemaphoreType.DMA((7, 9))),
]
RB = 32


def loop(rows, fn, init=0):
    def step(i, carry):
        return fn(pl.ds(pl.multiple_of(i * RB, RB), RB), i, carry)

    return lax.fori_loop(0, rows // RB, step, init)


def body(factor, tok, cot, wi, ws, bias, rate, skip, gain, wo, lo, gt, eres, lres,
         x, z, ub, stepe, bt, ct, s, ds, wsel, wpad, vecs, step, sig, cumr, cumc, cumrt, cumct,
         er, ec, wr, wc, dr, dc, dro, dco, finr, finc, finro, finco, wur, wuc, edr, edc, mr, mc, ls,
         yr, yc, car, cac, dn, dy, dyb, dzb, nb, qr, qc, dxb, dux, dbe, dce,
         own, got, into, send, ret, res, ebuf, ecb, exb, eyb, ezb, lbuf, lcb, lxb, lyb, lzb,
         fsem, cs, cr, es, erv, lsm, lrv):
    pos = place()
    barrier = pltpu.get_barrier_semaphore()
    near = [at(pos, co=1 - pos["co"])] + peers(pos, "x") + peers(pos, "y") + peers(pos, "z")
    for to in near:
        pl.semaphore_signal(barrier, inc=1, device_id=to, device_id_type=MESH)

    def chain(slot, axis, back):
        a = slot % 2
        return Chain(pos, axis, back, own.at[slot], got.at[slot], into.at[slot], send.at[slot], ret.at[slot],
                     res.at[slot], (dr, dc)[a], (dro, dco)[a], cs, cr, slot)

    fr, fc, gr_, gc_ = chain(0, "r", False), chain(1, "c", False), chain(2, "r", True), chain(3, "c", True)
    early = Total(pos, ebuf, eres, ecb, exb, eyb, ezb, es, erv)
    late = Total(pos, lbuf, lres, lcb, lxb, lyb, lzb, lsm, lrv)

    r, c = grid2(2 * STATE + HEADS, 640)
    sel = ((c < 256) & (r == lo4(c))) | ((c >= 256) & (c < 512) & (r == 16 + lo4(c))) | ((c >= 512) & (r == c - 480))
    wsel[...] = mm(ws[...], ind(sel), 0, 0).astype(BF16)
    r, c = grid2(2 * STATE + HEADS, 128)
    wpad[...] = mm(ws[...], ind(r == c), 0, 0).astype(BF16)
    vecs[...] = jnp.zeros((8, 128), F32)
    vecs[0:1, 0:HEADS] = bias[...]
    vecs[1:2, 0:HEADS] = rate[...]
    vecs[2:3, 0:HEADS] = skip[...]
    raw = mm(tok[...], wsel[:, 512:640]) + vecs[0:1, :]
    tail = jnp.exp(-jnp.abs(raw))
    stp = jnp.maximum(raw, 0.0) + jnp.log1p(tail)
    step[...] = stp
    sig[...] = jnp.where(raw >= 0, 1.0, tail) / (1.0 + tail)
    a = -stp * vecs[1:2, :]
    t, u = grid2(T, T)
    same_r, same_c = hi4(t) == hi4(u), lo4(t) == lo4(u)
    cumr[...] = pick(ind(same_r & (u <= t)), a)
    cumc[...] = pick(ind(same_c & (u <= t)), a)
    aft_r = pick(ind(same_r & (u > t)), a)
    aft_c = pick(ind(same_c & (u > t)), a)
    r, c = grid2(SIDE, T)
    finr[...] = jnp.exp(pick(ind(r == hi4(c)), a))
    finc[...] = jnp.exp(pick(ind(r == lo4(c)), a))
    hx = head_spread()
    stepe[...] = spread(stp, hx, 3)
    wr[...] = spread(jnp.exp(aft_r), hx)
    wc[...] = spread(jnp.exp(aft_c), hx)
    x[...] = mm(tok[...], wi[:, 0:E])
    keep(bt, (), mm(tok[...], wsel[:, 0:256]))

    def drive(sl, i, carry):
        u_ = stepe[sl] * x[sl]
        keep(ub, (sl,), u_)
        keep(wur, (sl,), wr[sl] * u_)
        keep(wuc, (sl,), wc[sl] * u_)
        return carry

    loop(T, drive)
    line_r, line_c = hi4(t) == hi4(u), lo4(t) == hi4(u)
    own[1] = mm3(only(line_c, bt), both(wuc), 0, 0)
    own[0] = mm3(only(line_r, bt), both(wur), 0, 0)
    pl.semaphore_wait(barrier, len(near))
    f_r = remote(finr, finro, fsem.at[0, 0], fsem.at[0, 1], fr.partner)
    f_c = remote(finc, finco, fsem.at[1, 0], fsem.at[1, 1], fc.partner)
    f_r.start()
    f_c.start()
    fr.start()
    fc.start()

    def lines(rows, first, ends):
        k, l = grid2(rows, SIDE)
        return pick(ind(hi4(k) + first == l), spread(ends, hx), 2)

    dr[...] = lines(T, 0, finr[...])
    dc[...] = lines(T, 0, finc[...])
    f_r.wait_recv()
    dro[...] = lines(128, pos["co"] * 8, finro[...])
    for q in range(CH):
        fr.pair(q)

    z[...] = mm(tok[...], wi[:, E : 2 * E])
    keep(ct, (), mm(tok[...], wsel[:, 256:512]))
    s[...] = mm3(both(ct), both(bt), 1, 1) * (1.0 / 16.0)
    er[...] = spread(jnp.exp(cumr[...]), hx)
    ec[...] = spread(jnp.exp(cumc[...]), hx)
    cumrt[...] = cumr[...].T
    cumct[...] = cumc[...].T

    def masks(sl, i, carry):
        t_, u_ = grid2(RB, T)
        t_ = t_ + i * RB
        in_r = (hi4(t_) == hi4(u_)) & (u_ <= t_)
        in_c = (lo4(t_) == lo4(u_)) & (u_ <= t_)
        s_ = s[sl]
        c_r, c_c = cumr[sl], cumc[sl]
        for h in range(HEADS):
            l_r = jnp.exp(jnp.where(in_r, c_r[:, h : h + 1] - cumrt[h : h + 1, :], NEG))
            l_c = jnp.exp(jnp.where(in_c, c_c[:, h : h + 1] - cumct[h : h + 1, :], NEG))
            keep(mr, (h, sl), l_r * s_)
            keep(mc, (h, sl), l_c * s_)
            ls[h, sl] = l_r + l_c
        return carry

    loop(T, masks)
    f_c.wait_recv()
    dco[...] = lines(128, pos["xh"] * 8, finco[...])
    for q in range(CH):
        fc.pair(q)
    low = lax.broadcasted_iota(jnp.int32, (T, 128), 1) < HDIM

    def heads(m, hp, pair, dim):
        wide = jnp.concatenate(pair, axis=1)
        part = []
        for h in (2 * hp, 2 * hp + 1):
            full = mm(m[0, h], wide, dim, 0)
            part.append(full[:, :128] + full[:, 128:] + mm(m[1, h], pair[0], dim, 0))
        return jnp.where(low, part[0], part[1])

    def within(hp, carry):
        sl = pl.ds(pl.multiple_of(hp * 128, 128), 128)
        u_ = (ub[0, :, sl], ub[1, :, sl])
        yr[:, sl] = heads(mr, hp, u_, 1)
        yc[:, sl] = heads(mc, hp, u_, 1)
        return carry

    lax.fori_loop(0, HEADS // 2, within, 0)
    dn[...] = mm(cot[...], wo[...], 1, 1)
    run_hops(fr, fc)
    fr.finish()
    car[...] = mm3(only(line_r, ct), split(res[0], 2))
    fc.finish()
    cac[...] = mm3(only(line_c, ct), split(res[1], 2))

    skipe = spread(vecs[...], hx, 3)[2:3, :]
    gain_ = gain[...]

    def middle(sl, i, carry):
        sum_gain, sum_skip = carry
        x_, z_ = x[sl], z[sl]
        c_r, c_c = er[sl] * car[sl], ec[sl] * cac[sl]
        w_r, w_c = yr[sl], yc[sl]
        y = (w_r + w_c) + (c_r + c_c) + skipe * x_
        sg = 1.0 / (1.0 + jnp.exp(-z_))
        act = z_ * sg
        gated = y * act
        inv = lax.rsqrt(jnp.mean(gated * gated, axis=-1, keepdims=True) + 1e-05)
        unit = gated * inv
        nb[sl] = (unit * gain_).astype(BF16)
        d_n = dn[sl]
        g1 = d_n * gain_
        dg = inv * (g1 - unit * jnp.mean(g1 * unit, axis=-1, keepdims=True))
        d_y = dg * act
        dzb[sl] = (dg * y * (sg * (1.0 + z_ * (1.0 - sg)))).astype(BF16)
        dy[sl] = d_y
        keep(dyb, (sl,), d_y)
        keep(edr, (sl,), er[sl] * d_y)
        keep(edc, (sl,), ec[sl] * d_y)
        qr[sl] = d_y * (c_r + w_r)
        qc[sl] = d_y * (c_c + w_c)
        fold = lambda v: functools.reduce(lambda p, q: p + q, [v[8 * j : 8 * j + 8] for j in range(RB // 8)])
        return sum_gain + fold(d_n * unit), sum_skip + fold(d_y * x_)

    nil = jnp.zeros((8, E), F32)
    sum_gain, sum_skip = loop(T, middle, (nil, nil))
    own[3] = mm3(only(line_c, ct), both(edc), 0, 0)
    gc_.start()
    own[2] = mm3(only(line_r, ct), both(edr), 0, 0)
    gr_.start()

    lg = mm(tok[...], dzb[...], 0, 0) * factor
    for j in range(4):
        ebuf[j * 256 : (j + 1) * 256] = lg[:, j * 128 : (j + 1) * 128]
    lg = mm(nb[...], cot[...], 0, 0) * factor
    for j in range(2):
        ebuf[1024 + j * 512 : 1024 + (j + 1) * 512] = lg[:, j * 128 : (j + 1) * 128]
    early.start(0)
    for q in range(CH):
        gr_.pair(q)
    early.step(0)

    def within_back(hp, carry):
        sl = pl.ds(pl.multiple_of(hp * 128, 128), 128)
        d_ = (dyb[0, :, sl], dyb[1, :, sl])
        yr[:, sl] = heads(mr, hp, d_, 0)
        yc[:, sl] = heads(mc, hp, d_, 0)
        return carry

    lax.fori_loop(0, HEADS // 2, within_back, 0)
    for q in range(CH):
        gc_.pair(q)
    ds[...] = jnp.zeros((T, T), F32)

    def scores_back(hp, carry):
        sl = pl.ds(pl.multiple_of(hp * 128, 128), 128)
        u_h, u_l = ub[0, :, sl], ub[1, :, sl]
        twice = jnp.concatenate((u_h, u_h), axis=1)
        total = ds[...]
        for j in (0, 1):
            d_h, d_l = only(low if j == 0 else ~low, (dyb[0, :, sl], dyb[1, :, sl]))
            pairs = mm(jnp.concatenate((d_h, d_l), axis=1), twice, 1, 1) + mm(d_h, u_l, 1, 1)
            total = total + ls[2 * hp + j] * pairs
        ds[...] = total
        return carry

    lax.fori_loop(0, HEADS // 2, scores_back, 0)
    head = u < STATE
    d_s = split(ds[...], 2)
    dce[...] = (
        jnp.where(line_r, mm3(both(edr), split(res[0], 2), 1, 1), 0.0)
        + jnp.where(line_c, mm3(both(edc), split(res[1], 2), 1, 1), 0.0)
        + jnp.where(head, mm3(d_s, both(bt)), 0.0)
    )
    dbe[...] = jnp.where(head, mm3(d_s, both(ct), 0, 0), 0.0)
    lo[...] = mm(nb[...], wo[...]).astype(BF16)
    run_hops(gr_, gc_)
    early.step(1)
    gr_.finish()
    g_r = split(res[2], 2)
    car[...] = mm3(only(line_r, bt), g_r)
    dbe[...] = dbe[...] + jnp.where(line_r, mm3(both(wur), g_r, 1, 1), 0.0)
    early.step(2)
    gc_.finish()
    g_c = split(res[3], 2)
    cac[...] = mm3(only(line_c, bt), g_c)
    dbe[...] = dbe[...] + jnp.where(line_c, mm3(both(wuc), g_c, 1, 1), 0.0)

    def last(sl, i, carry):
        x_, se = x[sl], stepe[sl]
        u_ = se * x_
        v_r, v_c = wr[sl] * car[sl], wc[sl] * cac[sl]
        w_r, w_c = yr[sl], yc[sl]
        qr[sl] = qr[sl] - u_ * (v_r + w_r)
        qc[sl] = qc[sl] - u_ * (v_c + w_c)
        d_u = (w_r + w_c) + (v_r + v_c)
        dux[sl] = d_u * x_
        dxb[sl] = (se * d_u + skipe * dy[sl]).astype(BF16)
        res[0, sl] = res[2, sl] * (own[0, sl] + dr[sl] * res[0, sl])
        res[1, sl] = res[3, sl] * (own[1, sl] + dc[sl] * res[1, sl])
        return carry

    loop(T, last)
    lg = mm(tok[...], dxb[...], 0, 0) * factor
    for j in range(4):
        lbuf[j * 256 : (j + 1) * 256] = lg[:, j * 128 : (j + 1) * 128]
    d_a = (
        pick(ind(same_r & (u >= t)), head_sum(qr[...]))
        + pick(ind(same_c & (u >= t)), head_sum(qc[...]))
        + pick(ind(line_r), head_sum(res[0]))
        + pick(ind(line_c), head_sum(res[1]))
    )
    d_step = head_sum(dux[...]) - vecs[1:2, :] * d_a
    d_raw = d_step * sig[...]
    r, c = grid2(T, 128)
    d_ssm = (
        spread(dbe[...], ind(c == lo4(r)))
        + spread(dce[...], ind(c == 16 + lo4(r)))
        + spread(d_raw, ind(grid2(128, 128)[1] == 32 + grid2(128, 128)[0]), 3)
    )
    d_ssm = d_ssm.astype(BF16)
    lg = mm(d_ssm, tok[...], 0, 0) * factor
    for j in range(2):
        lbuf[1024 + j * 128 : 1152 + j * 128] = lg[:, j * 128 : (j + 1) * 128]
    total_of = lambda v: jnp.sum(v, axis=0, keepdims=True)
    sum_gain = total_of(sum_gain) * factor
    for j in range(4):
        lbuf[1088 + j : 1089 + j] = sum_gain[:, j * 128 : (j + 1) * 128]
    lbuf[1092:1093] = total_of(d_raw) * factor
    lbuf[1093:1094] = -total_of(step[...] * d_a) * factor
    lbuf[1094:1095] = total_of(head_sum(sum_skip)) * factor
    late.start(0)
    early.step(3)
    late.step(0)
    back = mm(dxb[...], wi[:, 0:E], 1, 1) + mm(dzb[...], wi[:, E : 2 * E], 1, 1)
    back = back + mm(d_ssm, wpad[...], 1, 1)
    gt[...] = back.astype(BF16)
    early.step(4)
    late.step(1)
    early.step(5)
    late.step(2)
    early.step(6)
    late.step(3)
    for who in (fr, fc, gr_, gc_):
        who.drain()
    f_r.wait_send()
    f_c.wait_send()
    late.step(4)
    late.step(5)
    late.step(6)


def unpack(eres, lres, lo_in, gt_in, lo, gt, gi, gs, go, gb, gr, gk, gg):
    lo[...] = lo_in[...]
    gt[...] = gt_in[...]
    for j in range(4):
        gi[:, j * 128 : (j + 1) * 128] = lres[j * 256 : (j + 1) * 256]
        gi[:, E + j * 128 : E + (j + 1) * 128] = eres[j * 256 : (j + 1) * 256]
        gg[:, j * 128 : (j + 1) * 128] = lres[1088 + j : 1089 + j]
    for j in range(2):
        go[:, j * 128 : (j + 1) * 128] = eres[1024 + j * 512 : 1024 + (j + 1) * 512]
        gs[:, j * 128 : (j + 1) * 128] = lres[1024 + j * 128 : 1064 + j * 128]
    gb[...] = lres[1092:1093, 0:HEADS]
    gr[...] = lres[1093:1094, 0:HEADS]
    gk[...] = lres[1094:1095, 0:HEADS]


def local(tokens_in, out_cotangent, w_inner, w_ssm, dt_bias, decay_rate, skip_gain, norm_gain, w_out):
    devices = lax.axis_size("slide") * lax.axis_size("row") * lax.axis_size("col")
    factor = float(devices * T) ** -0.5
    shape = jax.ShapeDtypeStruct
    vmem = pl.BlockSpec(memory_space=pltpu.VMEM)
    lo, gt, eres, lres = pl.pallas_call(
        functools.partial(kernel, factor),
        out_shape=(shape((T, D), BF16), shape((T, D), BF16), shape((EARLY, 128), F32), shape((LATE, 128), F32)),
        in_specs=[vmem] * 9,
        out_specs=(vmem,) * 4,
        scratch_shapes=[kind for _, kind in SCRATCH],
        compiler_params=pltpu.CompilerParams(
            collective_id=0, has_side_effects=True, vmem_limit_bytes=48 * 2**20
        ),
    )(
        tokens_in.reshape(T, D),
        out_cotangent.reshape(T, D),
        w_inner,
        w_ssm.T,
        dt_bias.reshape(1, -1),
        decay_rate.reshape(1, -1),
        skip_gain.reshape(1, -1),
        norm_gain.reshape(1, -1),
        w_out,
    )
    out = pl.pallas_call(
        unpack,
        out_shape=(
            shape((T, D), BF16),
            shape((T, D), BF16),
            shape(w_inner.shape, F32),
            shape(w_ssm.shape[::-1], F32),
            shape(w_out.shape, F32),
            shape((1, HEADS), F32),
            shape((1, HEADS), F32),
            shape((1, HEADS), F32),
            shape((1, E), F32),
        ),
        in_specs=[vmem] * 4,
        out_specs=(vmem,) * 9,
        compiler_params=pltpu.CompilerParams(vmem_limit_bytes=6 * 2**20),
    )(eres, lres, lo, gt)
    return (
        out[0].reshape(tokens_in.shape),
        out[1].reshape(tokens_in.shape),
        out[2],
        out[3].T,
        out[4],
        out[5].reshape(-1),
        out[6].reshape(-1),
        out[7].reshape(-1),
        out[8].reshape(-1),
    )


def solution(mesh):
    tiles = P("slide", "row", "col", None)
    return jax.shard_map(
        local,
        mesh=mesh,
        in_specs=(tiles, tiles) + (P(),) * 7,
        out_specs=(tiles, tiles) + (P(),) * 7,
        check_vma=False,
    )
```

```python
import functools

import jax
import jax.numpy as jnp
from jax import lax
from jax.experimental import pallas as pl
from jax.experimental.pallas import tpu as pltpu
from jax.sharding import PartitionSpec as P

MESH = pl.DeviceIdType.MESH
F32 = jnp.float32
BF16 = jnp.bfloat16
HEADS = 8
HDIM = 64
STATE = 16
SIDE = 16
T = SIDE * SIDE
E = HEADS * HDIM
D = 256
CH = 4
CR = 128 // CH
NEG = -1e30
EARLY = 2048
LATE = 1280


def mm(a, b, ca=1, cb=0):
    return lax.dot_general(a, b, (((ca,), (cb,)), ((), ())), preferred_element_type=F32)


def split(x, terms):
    out = []
    for _ in range(terms - 1):
        hi = x.astype(BF16)
        out.append(hi)
        x = x - hi.astype(F32)
    out.append(x.astype(BF16))
    return out


def pick(mask, x, terms=3):
    return functools.reduce(lambda u, v: u + v, [mm(mask, part) for part in split(x, terms)])


def spread(x, mask, terms=2):
    return functools.reduce(lambda u, v: u + v, [mm(part, mask) for part in split(x, terms)])


def mm3(a, b, ca=1, cb=0):
    (ah, al), (bh, bl) = a, b
    return mm(ah, bh, ca, cb) + (mm(ah, bl, ca, cb) + mm(al, bh, ca, cb))


def keep(pair, where, x):
    hi, lo = split(x, 2)
    pair[(0,) + where] = hi
    pair[(1,) + where] = lo


def both(pair):
    return pair[0], pair[1]


def only(mask, pair):
    nil = jnp.zeros(mask.shape, BF16)
    return jnp.where(mask, pair[0], nil), jnp.where(mask, pair[1], nil)


def ind(cond):
    return jnp.where(cond, 1.0, 0.0).astype(BF16)


def grid2(rows, cols):
    return (
        lax.broadcasted_iota(jnp.int32, (rows, cols), 0),
        lax.broadcasted_iota(jnp.int32, (rows, cols), 1),
    )


def hi4(x):
    return lax.shift_right_logical(x, 4)


def lo4(x):
    return jnp.bitwise_and(x, 15)


def head_spread():
    r, c = grid2(128, E)
    return ind(r == lax.shift_right_logical(c, 6))


def head_sum(x):
    r, c = grid2(E, 128)
    return spread(x, ind(lax.shift_right_logical(r, 6) == c), 2)


def place():
    row, col, slide = lax.axis_index("row"), lax.axis_index("col"), lax.axis_index("slide")
    return dict(y=row // 2, xh=lax.rem(row, 2), z=col // 2, co=lax.rem(col, 2), xl=slide)


def at(pos, **change):
    p = dict(pos, **change)
    return (p["y"] * 2 + p["xh"], p["z"] * 2 + p["co"], p["xl"])


def flip(bit, by):
    return bit + by * (1 - 2 * bit)


def peers(pos, axis):
    out = []
    for d in (1, 2, 3):
        if axis == "x":
            out.append(at(pos, xh=flip(pos["xh"], d // 2), xl=flip(pos["xl"], d % 2)))
        else:
            out.append(at(pos, **{axis: xor4(pos[axis], d)}))
    return out


def xor4(q, d):
    return 2 * flip(q // 2, d // 2) + flip(lax.rem(q, 2), d % 2)


def remote(src, dst, ssem, rsem, to):
    return pltpu.make_async_remote_copy(
        src_ref=src, dst_ref=dst, send_sem=ssem, recv_sem=rsem, device_id=to, device_id_type=MESH
    )


class Chain:
    def __init__(self, pos, axis, back, own, got, into, send, ret, res, dec, deco, ssem, rsem, slot):
        self.bit, step = ("co", "z") if axis == "r" else ("xh", "y")
        b, q = pos[self.bit], pos[step]
        self.b = b
        self.first = (b == 1) if back else (b == 0)
        self.r = (3 - q) if back else q
        self.nxt = at(pos, **{step: lax.rem(q + (3 if back else 1), 4)})
        self.partner = at(pos, **{self.bit: 1 - b})
        self.own, self.got, self.into, self.send, self.ret, self.res = own, got, into, send, ret, res
        self.dec, self.deco = dec, deco
        self.ssem, self.rsem, self.slot = ssem, rsem, slot

    def half(self, mine, c):
        start = (self.b if mine else 1 - self.b) * 128 + c * CR
        return pl.ds(pl.multiple_of(start, CR), CR)

    def sems(self, stage, c):
        return self.ssem.at[self.slot, stage, c], self.rsem.at[self.slot, stage, c]

    def c_exch(self, c):
        return remote(self.own.at[self.half(False, c)], self.got.at[pl.ds(c * CR, CR)], *self.sems(0, c), self.partner)

    def c_hop(self, c):
        return remote(self.send.at[pl.ds(c * CR, CR)], self.into.at[pl.ds(c * CR, CR)], *self.sems(1, c), self.nxt)

    def c_ret(self, c):
        return remote(self.ret.at[pl.ds(c * CR, CR)], self.res.at[self.half(True, c)], *self.sems(2, c), self.partner)

    def start(self):
        @pl.when(self.r == 0)
        def _():
            self.into[...] = jnp.zeros((128, E), F32)

        for c in range(CH):
            self.c_exch(c).start()

    def pair(self, c):
        sl = pl.ds(c * CR, CR)
        self.c_exch(c).wait_recv()
        got, own = self.got[sl], self.own[self.half(True, c)]
        d_own, d_oth = self.dec[self.half(True, c)], self.deco[sl]
        lead = jnp.where(self.first, own, got)
        tail = jnp.where(self.first, got, own)
        d_tail = jnp.where(self.first, d_oth, d_own)
        self.send[sl] = tail + d_tail * lead

        @pl.when(self.r == 0)
        def _():
            self.c_hop(c).start()

    def hop(self, c):
        sl = pl.ds(c * CR, CR)

        @pl.when(self.r > 0)
        def _():
            self.c_hop(c).wait_recv()

        enter = self.into[sl]
        d_own, d_oth = self.dec[self.half(True, c)], self.deco[sl]

        @pl.when((self.r > 0) & (self.r < 3))
        def _():
            self.send[sl] = self.send[sl] + d_own * d_oth * enter
            self.c_hop(c).start()

        lead = jnp.where(self.first, self.own[self.half(True, c)], self.got[sl])
        d_lead = jnp.where(self.first, d_own, d_oth)
        after = d_lead * enter + lead
        self.ret[sl] = jnp.where(self.first, after, enter)
        self.c_ret(c).start()
        self.res[self.half(True, c)] = jnp.where(self.first, enter, after)

    def finish(self):
        for c in range(CH):
            self.c_ret(c).wait_recv()

    def drain(self):
        for c in range(CH):
            self.c_exch(c).wait_send()
            self.c_ret(c).wait_send()

            @pl.when(self.r < 3)
            def _():
                self.c_hop(c).wait_send()


def run_hops(a, c):
    @pl.when(a.r <= c.r)
    def _():
        for who, at_chunk in ((a, 0), (a, 1), (c, 0), (a, 2), (c, 1), (a, 3), (c, 2), (c, 3)):
            who.hop(at_chunk)

    @pl.when(a.r > c.r)
    def _():
        for who, at_chunk in ((c, 0), (c, 1), (a, 0), (c, 2), (a, 1), (c, 3), (a, 2), (a, 3)):
            who.hop(at_chunk)


class Total:
    def __init__(self, pos, buf, out, cbuf, xbuf, ybuf, zbuf, ssem, rsem):
        n = buf.shape[0]
        self.pos, self.buf, self.out = pos, buf, out
        self.cbuf, self.xbuf, self.ybuf, self.zbuf = cbuf, xbuf, ybuf, zbuf
        self.ssem, self.rsem = ssem, rsem
        self.nh = n // 2
        self.base = pos["co"] * self.nh
        self.other = at(pos, co=1 - pos["co"])
        index = {"x": pos["xh"] * 2 + pos["xl"], "y": pos["y"], "z": pos["z"]}
        third = -(-self.nh // 384) * 128
        sizes = (third, third, self.nh - 2 * third)
        self.parts, offset = [], 0
        for size, order in zip(sizes, ("xyz", "yzx", "zxy")):
            start = self.base + offset
            first = start + index[order[0]] * (size // 4)
            second = first + index[order[1]] * (size // 16)
            self.parts.append((order, index[order[0]], index[order[1]], size, offset, start, first, second))
            offset += size

    def rows(self, start, size):
        return pl.ds(pl.multiple_of(start, 8), size)

    def copies(self, stage):
        pos = self.pos
        if stage in (0, 6):
            src = self.buf.at[self.rows((1 - pos["co"]) * self.nh, self.nh)]
            own = self.out.at[self.rows(self.base, self.nh)]
            src, dst = (src, self.cbuf) if stage == 0 else (own, own)
            return [remote(src, dst, self.ssem.at[stage, 0], self.rsem.at[stage, 0], self.other)]
        out = []
        for p, (order, g0, g1, size, offset, start, first, second) in enumerate(self.parts):
            n0, n1 = size // 4, size // 16
            axis = order[(0, 1, 2, 1, 0)[stage - 1]]
            for d, to in enumerate(peers(pos, axis)):
                if stage == 1:
                    src = self.buf.at[self.rows(start + xor4(g0, d + 1) * n0, n0)]
                    dst = self.xbuf.at[d, pl.ds(offset // 4, n0)]
                elif stage == 2:
                    src = self.buf.at[self.rows(first + xor4(g1, d + 1) * n1, n1)]
                    dst = self.ybuf.at[d, pl.ds(offset // 16, n1)]
                elif stage == 3:
                    src, dst = self.buf.at[self.rows(second, n1)], self.zbuf.at[d, pl.ds(offset // 16, n1)]
                elif stage == 4:
                    src = dst = self.out.at[self.rows(second, n1)]
                else:
                    src = dst = self.out.at[self.rows(first, n0)]
                k = 3 * p + d
                out.append(remote(src, dst, self.ssem.at[stage, k], self.rsem.at[stage, k], to))
        return out

    def start(self, stage):
        for copy in self.copies(stage):
            copy.start()

    def finish(self, stage):
        for copy in self.copies(stage):
            copy.wait()
        if stage == 0:
            sl = self.rows(self.base, self.nh)
            self.buf[sl] = self.buf[sl] + self.cbuf[...]
        if stage not in (1, 2, 3):
            return
        came = (self.xbuf, self.ybuf, self.zbuf)[stage - 1]
        to = self.out if stage == 3 else self.buf
        for order, g0, g1, size, offset, start, first, second in self.parts:
            share = 4 if stage == 1 else 16
            sl = self.rows(first if stage == 1 else second, size // share)
            at_ = pl.ds(offset // share, size // share)
            to[sl] = (self.buf[sl] + came[0, at_]) + (came[1, at_] + came[2, at_])

    def step(self, stage):
        self.finish(stage)
        if stage < 6:
            self.start(stage + 1)


def kernel(factor, *refs):
    names_in = ["tok", "cot", "wi", "ws", "bias", "rate", "skip", "gain", "wo"]
    names_in = [name + "_h" for name in names_in]
    names_out = ["lo", "gt", "eres", "lres"]
    n_io = len(names_in) + len(names_out)
    k = dict(zip(names_in + names_out, refs[:n_io]))
    k.update(zip([name for name, _ in SCRATCH], refs[n_io:]))
    body(factor, **k)


def vm(*shape, dtype=F32):
    return pltpu.VMEM(shape, dtype)


BIG = (T, E)
SCRATCH = [
    ("x", vm(*BIG)), ("z", vm(*BIG)), ("ub", vm(2, *BIG, dtype=BF16)), ("stepe", vm(*BIG)),
    ("bt", vm(2, T, T, dtype=BF16)), ("ct", vm(2, T, T, dtype=BF16)), ("s", vm(T, T)), ("ds", vm(T, T)),
    ("wsel", vm(D, 640, dtype=BF16)), ("wpad", vm(D, 128, dtype=BF16)), ("vecs", vm(8, 128)),
    ("step", vm(T, 128)), ("sig", vm(T, 128)),
    ("cumr", vm(T, 128)), ("cumc", vm(T, 128)), ("cumrt", vm(128, T)), ("cumct", vm(128, T)),
    ("er", vm(*BIG)), ("ec", vm(*BIG)), ("wr", vm(*BIG)), ("wc", vm(*BIG)), ("dr", vm(*BIG)), ("dc", vm(*BIG)),
    ("dro", vm(128, E)), ("dco", vm(128, E)),
    ("finr", vm(SIDE, 128)), ("finc", vm(SIDE, 128)), ("finro", vm(SIDE, 128)), ("finco", vm(SIDE, 128)),
    ("wur", vm(2, *BIG, dtype=BF16)), ("wuc", vm(2, *BIG, dtype=BF16)),
    ("edr", vm(2, *BIG, dtype=BF16)), ("edc", vm(2, *BIG, dtype=BF16)),
    ("mr", vm(2, HEADS, T, T, dtype=BF16)), ("mc", vm(2, HEADS, T, T, dtype=BF16)), ("ls", vm(HEADS, T, T)),
    ("yr", vm(*BIG)), ("yc", vm(*BIG)), ("car", vm(*BIG)), ("cac", vm(*BIG)), ("dn", vm(*BIG)),
    ("dy", vm(*BIG)), ("dyb", vm(2, *BIG, dtype=BF16)), ("dzb", vm(*BIG, dtype=BF16)), ("nb", vm(*BIG, dtype=BF16)),
    ("qr", vm(*BIG)), ("qc", vm(*BIG)), ("dxb", vm(*BIG, dtype=BF16)), ("dux", vm(*BIG)),
    ("dbe", vm(T, T)), ("dce", vm(T, T)),
    ("own", pltpu.VMEM((4, T, E), F32)), ("got", pltpu.VMEM((4, 128, E), F32)), ("into", pltpu.VMEM((4, 128, E), F32)),
    ("send", pltpu.VMEM((4, 128, E), F32)), ("ret", pltpu.VMEM((4, 128, E), F32)), ("res", pltpu.VMEM((4, T, E), F32)),
    ("ebuf", vm(EARLY, 128)), ("ecb", vm(EARLY // 2, 128)), ("exb", vm(3, EARLY // 8, 128)),
    ("eyb", vm(3, EARLY // 32, 128)), ("ezb", vm(3, EARLY // 32, 128)),
    ("lbuf", vm(LATE, 128)), ("lcb", vm(LATE // 2, 128)), ("lxb", vm(3, LATE // 8, 128)),
    ("lyb", vm(3, LATE // 32, 128)), ("lzb", vm(3, LATE // 32, 128)),
    ("fsem", pltpu.SemaphoreType.DMA((2, 2))),
    ("cs", pltpu.SemaphoreType.DMA((4, 3, CH))), ("cr", pltpu.SemaphoreType.DMA((4, 3, CH))),
    ("es", pltpu.SemaphoreType.DMA((7, 9))), ("erv", pltpu.SemaphoreType.DMA((7, 9))),
    ("lsm", pltpu.SemaphoreType.DMA((7, 9))), ("lrv", pltpu.SemaphoreType.DMA((7, 9))),
]
SCRATCH += [
    ("tok", vm(T, D, dtype=BF16)), ("cot", vm(T, D, dtype=BF16)), ("wi", vm(D, 2 * E, dtype=BF16)),
    ("ws", vm(2 * STATE + HEADS, D, dtype=BF16)), ("bias", vm(1, HEADS)), ("rate", vm(1, HEADS)),
    ("skip", vm(1, HEADS)), ("gain", vm(1, E)), ("wo", vm(E, D, dtype=BF16)),
    ("isem", pltpu.SemaphoreType.DMA((9,))),
]
RB = 32


def loop(rows, fn, init=0):
    def step(i, carry):
        return fn(pl.ds(pl.multiple_of(i * RB, RB), RB), i, carry)

    return lax.fori_loop(0, rows // RB, step, init)


def body(factor, tok_h, cot_h, wi_h, ws_h, bias_h, rate_h, skip_h, gain_h, wo_h, lo, gt, eres, lres,
         x, z, ub, stepe, bt, ct, s, ds, wsel, wpad, vecs, step, sig, cumr, cumc, cumrt, cumct,
         er, ec, wr, wc, dr, dc, dro, dco, finr, finc, finro, finco, wur, wuc, edr, edc, mr, mc, ls,
         yr, yc, car, cac, dn, dy, dyb, dzb, nb, qr, qc, dxb, dux, dbe, dce,
         own, got, into, send, ret, res, ebuf, ecb, exb, eyb, ezb, lbuf, lcb, lxb, lyb, lzb,
         fsem, cs, cr, es, erv, lsm, lrv, tok, cot, wi, ws, bias, rate, skip, gain, wo, isem):
    pos = place()
    given = (ws_h, ws), (bias_h, bias), (rate_h, rate), (skip_h, skip), (tok_h, tok), (wi_h, wi), (cot_h, cot), (wo_h, wo), (gain_h, gain)
    fetch = [pltpu.make_async_copy(src, dst, isem.at[j]) for j, (src, dst) in enumerate(given)]
    for copy in fetch:
        copy.start()
    barrier = pltpu.get_barrier_semaphore()
    near = [at(pos, co=1 - pos["co"])] + peers(pos, "x") + peers(pos, "y") + peers(pos, "z")
    for to in near:
        pl.semaphore_signal(barrier, inc=1, device_id=to, device_id_type=MESH)

    def chain(slot, axis, back):
        a = slot % 2
        return Chain(pos, axis, back, own.at[slot], got.at[slot], into.at[slot], send.at[slot], ret.at[slot],
                     res.at[slot], (dr, dc)[a], (dro, dco)[a], cs, cr, slot)

    fr, fc, gr_, gc_ = chain(0, "r", False), chain(1, "c", False), chain(2, "r", True), chain(3, "c", True)
    early = Total(pos, ebuf, eres, ecb, exb, eyb, ezb, es, erv)
    late = Total(pos, lbuf, lres, lcb, lxb, lyb, lzb, lsm, lrv)

    for copy in fetch[:6]:
        copy.wait()
    r, c = grid2(2 * STATE + HEADS, 640)
    sel = ((c < 256) & (r == lo4(c))) | ((c >= 256) & (c < 512) & (r == 16 + lo4(c))) | ((c >= 512) & (r == c - 480))
    wsel[...] = mm(ws[...], ind(sel), 0, 0).astype(BF16)
    r, c = grid2(2 * STATE + HEADS, 128)
    wpad[...] = mm(ws[...], ind(r == c), 0, 0).astype(BF16)
    vecs[...] = jnp.zeros((8, 128), F32)
    vecs[0:1, 0:HEADS] = bias[...]
    vecs[1:2, 0:HEADS] = rate[...]
    vecs[2:3, 0:HEADS] = skip[...]
    raw = mm(tok[...], wsel[:, 512:640]) + vecs[0:1, :]
    tail = jnp.exp(-jnp.abs(raw))
    stp = jnp.maximum(raw, 0.0) + jnp.log1p(tail)
    step[...] = stp
    sig[...] = jnp.where(raw >= 0, 1.0, tail) / (1.0 + tail)
    a = -stp * vecs[1:2, :]
    t, u = grid2(T, T)
    same_r, same_c = hi4(t) == hi4(u), lo4(t) == lo4(u)
    cumr[...] = pick(ind(same_r & (u <= t)), a)
    cumc[...] = pick(ind(same_c & (u <= t)), a)
    aft_r = pick(ind(same_r & (u > t)), a)
    aft_c = pick(ind(same_c & (u > t)), a)
    r, c = grid2(SIDE, T)
    finr[...] = jnp.exp(pick(ind(r == hi4(c)), a))
    finc[...] = jnp.exp(pick(ind(r == lo4(c)), a))
    hx = head_spread()
    stepe[...] = spread(stp, hx, 3)
    wr[...] = spread(jnp.exp(aft_r), hx)
    wc[...] = spread(jnp.exp(aft_c), hx)
    x[...] = mm(tok[...], wi[:, 0:E])
    keep(bt, (), mm(tok[...], wsel[:, 0:256]))

    def drive(sl, i, carry):
        u_ = stepe[sl] * x[sl]
        keep(ub, (sl,), u_)
        keep(wur, (sl,), wr[sl] * u_)
        keep(wuc, (sl,), wc[sl] * u_)
        return carry

    loop(T, drive)
    line_r, line_c = hi4(t) == hi4(u), lo4(t) == hi4(u)
    own[1] = mm3(only(line_c, bt), both(wuc), 0, 0)
    own[0] = mm3(only(line_r, bt), both(wur), 0, 0)
    pl.semaphore_wait(barrier, len(near))
    f_r = remote(finr, finro, fsem.at[0, 0], fsem.at[0, 1], fr.partner)
    f_c = remote(finc, finco, fsem.at[1, 0], fsem.at[1, 1], fc.partner)
    f_r.start()
    f_c.start()
    fr.start()
    fc.start()

    def lines(rows, first, ends):
        k, l = grid2(rows, SIDE)
        return pick(ind(hi4(k) + first == l), spread(ends, hx), 2)

    dr[...] = lines(T, 0, finr[...])
    dc[...] = lines(T, 0, finc[...])
    f_r.wait_recv()
    dro[...] = lines(128, pos["co"] * 8, finro[...])
    for q in range(CH):
        fr.pair(q)

    z[...] = mm(tok[...], wi[:, E : 2 * E])
    keep(ct, (), mm(tok[...], wsel[:, 256:512]))
    s[...] = mm3(both(ct), both(bt), 1, 1) * (1.0 / 16.0)
    er[...] = spread(jnp.exp(cumr[...]), hx)
    ec[...] = spread(jnp.exp(cumc[...]), hx)
    cumrt[...] = cumr[...].T
    cumct[...] = cumc[...].T

    def masks(sl, i, carry):
        t_, u_ = grid2(RB, T)
        t_ = t_ + i * RB
        in_r = (hi4(t_) == hi4(u_)) & (u_ <= t_)
        in_c = (lo4(t_) == lo4(u_)) & (u_ <= t_)
        s_ = s[sl]
        c_r, c_c = cumr[sl], cumc[sl]
        for h in range(HEADS):
            l_r = jnp.exp(jnp.where(in_r, c_r[:, h : h + 1] - cumrt[h : h + 1, :], NEG))
            l_c = jnp.exp(jnp.where(in_c, c_c[:, h : h + 1] - cumct[h : h + 1, :], NEG))
            keep(mr, (h, sl), l_r * s_)
            keep(mc, (h, sl), l_c * s_)
            ls[h, sl] = l_r + l_c
        return carry

    loop(T, masks)
    f_c.wait_recv()
    dco[...] = lines(128, pos["xh"] * 8, finco[...])
    for q in range(CH):
        fc.pair(q)
    low = lax.broadcasted_iota(jnp.int32, (T, 128), 1) < HDIM

    def heads(m, hp, pair, dim):
        wide = jnp.concatenate(pair, axis=1)
        part = []
        for h in (2 * hp, 2 * hp + 1):
            full = mm(m[0, h], wide, dim, 0)
            part.append(full[:, :128] + full[:, 128:] + mm(m[1, h], pair[0], dim, 0))
        return jnp.where(low, part[0], part[1])

    def within(hp, carry):
        sl = pl.ds(pl.multiple_of(hp * 128, 128), 128)
        u_ = (ub[0, :, sl], ub[1, :, sl])
        yr[:, sl] = heads(mr, hp, u_, 1)
        yc[:, sl] = heads(mc, hp, u_, 1)
        return carry

    lax.fori_loop(0, HEADS // 2, within, 0)
    for copy in fetch[6:]:
        copy.wait()
    dn[...] = mm(cot[...], wo[...], 1, 1)
    run_hops(fr, fc)
    fr.finish()
    car[...] = mm3(only(line_r, ct), split(res[0], 2))
    fc.finish()
    cac[...] = mm3(only(line_c, ct), split(res[1], 2))

    skipe = spread(vecs[...], hx, 3)[2:3, :]
    gain_ = gain[...]

    def middle(sl, i, carry):
        sum_gain, sum_skip = carry
        x_, z_ = x[sl], z[sl]
        c_r, c_c = er[sl] * car[sl], ec[sl] * cac[sl]
        w_r, w_c = yr[sl], yc[sl]
        y = (w_r + w_c) + (c_r + c_c) + skipe * x_
        sg = 1.0 / (1.0 + jnp.exp(-z_))
        act = z_ * sg
        gated = y * act
        inv = lax.rsqrt(jnp.mean(gated * gated, axis=-1, keepdims=True) + 1e-05)
        unit = gated * inv
        nb[sl] = (unit * gain_).astype(BF16)
        d_n = dn[sl]
        g1 = d_n * gain_
        dg = inv * (g1 - unit * jnp.mean(g1 * unit, axis=-1, keepdims=True))
        d_y = dg * act
        dzb[sl] = (dg * y * (sg * (1.0 + z_ * (1.0 - sg)))).astype(BF16)
        dy[sl] = d_y
        keep(dyb, (sl,), d_y)
        keep(edr, (sl,), er[sl] * d_y)
        keep(edc, (sl,), ec[sl] * d_y)
        qr[sl] = d_y * (c_r + w_r)
        qc[sl] = d_y * (c_c + w_c)
        fold = lambda v: functools.reduce(lambda p, q: p + q, [v[8 * j : 8 * j + 8] for j in range(RB // 8)])
        return sum_gain + fold(d_n * unit), sum_skip + fold(d_y * x_)

    nil = jnp.zeros((8, E), F32)
    sum_gain, sum_skip = loop(T, middle, (nil, nil))
    own[3] = mm3(only(line_c, ct), both(edc), 0, 0)
    gc_.start()
    own[2] = mm3(only(line_r, ct), both(edr), 0, 0)
    gr_.start()

    lg = mm(tok[...], dzb[...], 0, 0) * factor
    for j in range(4):
        ebuf[j * 256 : (j + 1) * 256] = lg[:, j * 128 : (j + 1) * 128]
    lg = mm(nb[...], cot[...], 0, 0) * factor
    for j in range(2):
        ebuf[1024 + j * 512 : 1024 + (j + 1) * 512] = lg[:, j * 128 : (j + 1) * 128]
    early.start(0)
    for q in range(CH):
        gr_.pair(q)
    early.step(0)

    def within_back(hp, carry):
        sl = pl.ds(pl.multiple_of(hp * 128, 128), 128)
        d_ = (dyb[0, :, sl], dyb[1, :, sl])
        yr[:, sl] = heads(mr, hp, d_, 0)
        yc[:, sl] = heads(mc, hp, d_, 0)
        return carry

    lax.fori_loop(0, HEADS // 2, within_back, 0)
    for q in range(CH):
        gc_.pair(q)
    ds[...] = jnp.zeros((T, T), F32)

    def scores_back(hp, carry):
        sl = pl.ds(pl.multiple_of(hp * 128, 128), 128)
        u_h, u_l = ub[0, :, sl], ub[1, :, sl]
        twice = jnp.concatenate((u_h, u_h), axis=1)
        total = ds[...]
        for j in (0, 1):
            d_h, d_l = only(low if j == 0 else ~low, (dyb[0, :, sl], dyb[1, :, sl]))
            pairs = mm(jnp.concatenate((d_h, d_l), axis=1), twice, 1, 1) + mm(d_h, u_l, 1, 1)
            total = total + ls[2 * hp + j] * pairs
        ds[...] = total
        return carry

    lax.fori_loop(0, HEADS // 2, scores_back, 0)
    head = u < STATE
    d_s = split(ds[...], 2)
    dce[...] = (
        jnp.where(line_r, mm3(both(edr), split(res[0], 2), 1, 1), 0.0)
        + jnp.where(line_c, mm3(both(edc), split(res[1], 2), 1, 1), 0.0)
        + jnp.where(head, mm3(d_s, both(bt)), 0.0)
    )
    dbe[...] = jnp.where(head, mm3(d_s, both(ct), 0, 0), 0.0)
    lo[...] = mm(nb[...], wo[...]).astype(BF16)
    run_hops(gr_, gc_)
    early.step(1)
    gr_.finish()
    g_r = split(res[2], 2)
    car[...] = mm3(only(line_r, bt), g_r)
    dbe[...] = dbe[...] + jnp.where(line_r, mm3(both(wur), g_r, 1, 1), 0.0)
    early.step(2)
    gc_.finish()
    g_c = split(res[3], 2)
    cac[...] = mm3(only(line_c, bt), g_c)
    dbe[...] = dbe[...] + jnp.where(line_c, mm3(both(wuc), g_c, 1, 1), 0.0)

    def last(sl, i, carry):
        x_, se = x[sl], stepe[sl]
        u_ = se * x_
        v_r, v_c = wr[sl] * car[sl], wc[sl] * cac[sl]
        w_r, w_c = yr[sl], yc[sl]
        qr[sl] = qr[sl] - u_ * (v_r + w_r)
        qc[sl] = qc[sl] - u_ * (v_c + w_c)
        d_u = (w_r + w_c) + (v_r + v_c)
        dux[sl] = d_u * x_
        dxb[sl] = (se * d_u + skipe * dy[sl]).astype(BF16)
        res[0, sl] = res[2, sl] * (own[0, sl] + dr[sl] * res[0, sl])
        res[1, sl] = res[3, sl] * (own[1, sl] + dc[sl] * res[1, sl])
        return carry

    loop(T, last)
    lg = mm(tok[...], dxb[...], 0, 0) * factor
    for j in range(4):
        lbuf[j * 256 : (j + 1) * 256] = lg[:, j * 128 : (j + 1) * 128]
    d_a = (
        pick(ind(same_r & (u >= t)), head_sum(qr[...]))
        + pick(ind(same_c & (u >= t)), head_sum(qc[...]))
        + pick(ind(line_r), head_sum(res[0]))
        + pick(ind(line_c), head_sum(res[1]))
    )
    d_step = head_sum(dux[...]) - vecs[1:2, :] * d_a
    d_raw = d_step * sig[...]
    r, c = grid2(T, 128)
    d_ssm = (
        spread(dbe[...], ind(c == lo4(r)))
        + spread(dce[...], ind(c == 16 + lo4(r)))
        + spread(d_raw, ind(grid2(128, 128)[1] == 32 + grid2(128, 128)[0]), 3)
    )
    d_ssm = d_ssm.astype(BF16)
    lg = mm(d_ssm, tok[...], 0, 0) * factor
    for j in range(2):
        lbuf[1024 + j * 128 : 1152 + j * 128] = lg[:, j * 128 : (j + 1) * 128]
    total_of = lambda v: jnp.sum(v, axis=0, keepdims=True)
    sum_gain = total_of(sum_gain) * factor
    for j in range(4):
        lbuf[1088 + j : 1089 + j] = sum_gain[:, j * 128 : (j + 1) * 128]
    lbuf[1092:1093] = total_of(d_raw) * factor
    lbuf[1093:1094] = -total_of(step[...] * d_a) * factor
    lbuf[1094:1095] = total_of(head_sum(sum_skip)) * factor
    late.start(0)
    early.step(3)
    late.step(0)
    back = mm(dxb[...], wi[:, 0:E], 1, 1) + mm(dzb[...], wi[:, E : 2 * E], 1, 1)
    back = back + mm(d_ssm, wpad[...], 1, 1)
    gt[...] = back.astype(BF16)
    early.step(4)
    late.step(1)
    early.step(5)
    late.step(2)
    early.step(6)
    late.step(3)
    for who in (fr, fc, gr_, gc_):
        who.drain()
    f_r.wait_send()
    f_c.wait_send()
    late.step(4)
    late.step(5)
    late.step(6)


def unpack(eres, lres, lo_in, gt_in, lo, gt, gi, gs, go, gb, gr, gk, gg):
    lo[...] = lo_in[...]
    gt[...] = gt_in[...]
    for j in range(4):
        gi[:, j * 128 : (j + 1) * 128] = lres[j * 256 : (j + 1) * 256]
        gi[:, E + j * 128 : E + (j + 1) * 128] = eres[j * 256 : (j + 1) * 256]
        gg[:, j * 128 : (j + 1) * 128] = lres[1088 + j : 1089 + j]
    for j in range(2):
        go[:, j * 128 : (j + 1) * 128] = eres[1024 + j * 512 : 1024 + (j + 1) * 512]
        gs[:, j * 128 : (j + 1) * 128] = lres[1024 + j * 128 : 1064 + j * 128]
    gb[...] = lres[1092:1093, 0:HEADS]
    gr[...] = lres[1093:1094, 0:HEADS]
    gk[...] = lres[1094:1095, 0:HEADS]


def local(tokens_in, out_cotangent, w_inner, w_ssm, dt_bias, decay_rate, skip_gain, norm_gain, w_out):
    devices = lax.axis_size("slide") * lax.axis_size("row") * lax.axis_size("col")
    factor = float(devices * T) ** -0.5
    shape = jax.ShapeDtypeStruct
    vmem = pl.BlockSpec(memory_space=pltpu.VMEM)
    lo, gt, eres, lres = pl.pallas_call(
        functools.partial(kernel, factor),
        out_shape=(shape((T, D), BF16), shape((T, D), BF16), shape((EARLY, 128), F32), shape((LATE, 128), F32)),
        in_specs=[pl.BlockSpec(memory_space=pltpu.HBM)] * 9,
        out_specs=(vmem,) * 4,
        scratch_shapes=[kind for _, kind in SCRATCH],
        compiler_params=pltpu.CompilerParams(
            collective_id=0, has_side_effects=True, vmem_limit_bytes=48 * 2**20
        ),
    )(
        *[
            pltpu.with_memory_space_constraint(array, pltpu.HBM)
            for array in (
                tokens_in.reshape(T, D),
                out_cotangent.reshape(T, D),
                w_inner,
                w_ssm.T,
                dt_bias.reshape(1, -1),
                decay_rate.reshape(1, -1),
                skip_gain.reshape(1, -1),
                norm_gain.reshape(1, -1),
                w_out,
            )
        ]
    )
    out = pl.pallas_call(
        unpack,
        out_shape=(
            shape((T, D), BF16),
            shape((T, D), BF16),
            shape(w_inner.shape, F32),
            shape(w_ssm.shape[::-1], F32),
            shape(w_out.shape, F32),
            shape((1, HEADS), F32),
            shape((1, HEADS), F32),
            shape((1, HEADS), F32),
            shape((1, E), F32),
        ),
        in_specs=[vmem] * 4,
        out_specs=(vmem,) * 9,
        compiler_params=pltpu.CompilerParams(vmem_limit_bytes=6 * 2**20),
    )(eres, lres, lo, gt)
    return (
        out[0].reshape(tokens_in.shape),
        out[1].reshape(tokens_in.shape),
        out[2],
        out[3].T,
        out[4],
        out[5].reshape(-1),
        out[6].reshape(-1),
        out[7].reshape(-1),
        out[8].reshape(-1),
    )


def solution(mesh):
    tiles = P("slide", "row", "col", None)
    return jax.shard_map(
        local,
        mesh=mesh,
        in_specs=(tiles, tiles) + (P(),) * 7,
        out_specs=(tiles, tiles) + (P(),) * 7,
        check_vma=False,
    )
```

```python
import functools

import jax
import jax.numpy as jnp
from jax import lax
from jax.experimental import pallas as pl
from jax.experimental.pallas import tpu as pltpu
from jax.sharding import PartitionSpec as P

MESH = pl.DeviceIdType.MESH
F32 = jnp.float32
BF16 = jnp.bfloat16
HEADS = 8
HDIM = 64
STATE = 16
SIDE = 16
T = SIDE * SIDE
E = HEADS * HDIM
D = 256
TILES = 8
SHARE = T // TILES
NEG = -1e30
EARLY = 2048
LATE = 1280


def mm(a, b, ca=1, cb=0):
    return lax.dot_general(a, b, (((ca,), (cb,)), ((), ())), preferred_element_type=F32)


def split(x, terms):
    out = []
    for _ in range(terms - 1):
        hi = x.astype(BF16)
        out.append(hi)
        x = x - hi.astype(F32)
    out.append(x.astype(BF16))
    return out


def pick(mask, x, terms=3):
    return functools.reduce(lambda u, v: u + v, [mm(mask, part) for part in split(x, terms)])


def spread(x, mask, terms=2):
    return functools.reduce(lambda u, v: u + v, [mm(part, mask) for part in split(x, terms)])


def mm3(a, b, ca=1, cb=0):
    (ah, al), (bh, bl) = a, b
    return mm(ah, bh, ca, cb) + (mm(ah, bl, ca, cb) + mm(al, bh, ca, cb))


def keep(pair, where, x):
    hi, lo = split(x, 2)
    pair[(0,) + where] = hi
    pair[(1,) + where] = lo


def both(pair):
    return pair[0], pair[1]


def only(mask, pair):
    nil = jnp.zeros(mask.shape, BF16)
    return jnp.where(mask, pair[0], nil), jnp.where(mask, pair[1], nil)


def ind(cond):
    return jnp.where(cond, 1.0, 0.0).astype(BF16)


def grid2(rows, cols):
    return (
        lax.broadcasted_iota(jnp.int32, (rows, cols), 0),
        lax.broadcasted_iota(jnp.int32, (rows, cols), 1),
    )


def hi4(x):
    return lax.shift_right_logical(x, 4)


def lo4(x):
    return jnp.bitwise_and(x, 15)


def head_spread():
    r, c = grid2(128, E)
    return ind(r == lax.shift_right_logical(c, 6))


def head_sum(x):
    r, c = grid2(E, 128)
    return spread(x, ind(lax.shift_right_logical(r, 6) == c), 2)


def place():
    row, col, slide = lax.axis_index("row"), lax.axis_index("col"), lax.axis_index("slide")
    return dict(y=row // 2, xh=lax.rem(row, 2), z=col // 2, co=lax.rem(col, 2), xl=slide)


def at(pos, **change):
    p = dict(pos, **change)
    return (p["y"] * 2 + p["xh"], p["z"] * 2 + p["co"], p["xl"])


def flip(bit, by):
    return bit + by * (1 - 2 * bit)


def peers(pos, axis):
    out = []
    for d in (1, 2, 3):
        if axis == "x":
            out.append(at(pos, xh=flip(pos["xh"], d // 2), xl=flip(pos["xl"], d % 2)))
        else:
            out.append(at(pos, **{axis: xor4(pos[axis], d)}))
    return out


def xor4(q, d):
    return 2 * flip(q // 2, d // 2) + flip(lax.rem(q, 2), d % 2)


def remote(src, dst, ssem, rsem, to):
    return pltpu.make_async_remote_copy(
        src_ref=src, dst_ref=dst, send_sem=ssem, recv_sem=rsem, device_id=to, device_id_type=MESH
    )


class Scan:
    def __init__(self, pos, axis, back, own, got, out, res, dec, ssem, rsem, slot):
        self.me = lax.axis_index("col" if axis == "r" else "row")
        self.pos, self.axis, self.back = pos, axis, back
        self.own, self.got, self.out, self.res, self.dec = own, got, out, res, dec
        self.ssem, self.rsem, self.slot = ssem, rsem, slot

    def peer(self, d):
        k = lax.rem(self.me + d, TILES)
        if self.axis == "r":
            return k, (lax.axis_index("row"), k, self.pos["xl"])
        return k, (k, lax.axis_index("col"), self.pos["xl"])

    def lines(self, k):
        return pl.ds(pl.multiple_of(k * SHARE, SHARE), SHARE)

    def copies(self, stage):
        out = []
        for d in (4, 3, 5, 2, 6, 1, 7):
            k, to = self.peer(d)
            sems = self.ssem.at[self.slot, stage, d], self.rsem.at[self.slot, stage, d]
            if stage == 0:
                out.append(remote(self.own.at[self.lines(k)], self.got.at[self.me], *sems, to))
            else:
                out.append(remote(self.out.at[k], self.res.at[self.lines(self.me)], *sems, to))
        return out

    def start(self):
        for copy in self.copies(0):
            copy.start()
        self.got[self.me] = self.own[self.lines(self.me)]

    def turn(self):
        for copy in self.copies(0):
            copy.wait_recv()
        state = jnp.zeros((SHARE, E), F32)
        for j in range(TILES - 1, -1, -1) if self.back else range(TILES):
            self.out[j] = state
            state = self.dec[j * SHARE : (j + 1) * SHARE] * state + self.got[j]
        for copy in self.copies(1):
            copy.start()
        self.res[self.lines(self.me)] = self.out[self.me]

    def finish(self):
        for copy in self.copies(1):
            copy.wait_recv()

    def drain(self):
        for stage in (0, 1):
            for copy in self.copies(stage):
                copy.wait_send()


class Total:
    def __init__(self, pos, buf, out, cbuf, xbuf, ybuf, zbuf, ssem, rsem):
        n = buf.shape[0]
        self.pos, self.buf, self.out = pos, buf, out
        self.cbuf, self.xbuf, self.ybuf, self.zbuf = cbuf, xbuf, ybuf, zbuf
        self.ssem, self.rsem = ssem, rsem
        self.nh = n // 2
        self.base = pos["co"] * self.nh
        self.other = at(pos, co=1 - pos["co"])
        index = {"x": pos["xh"] * 2 + pos["xl"], "y": pos["y"], "z": pos["z"]}
        third = -(-self.nh // 384) * 128
        sizes = (third, third, self.nh - 2 * third)
        self.parts, offset = [], 0
        for size, order in zip(sizes, ("xyz", "yzx", "zxy")):
            start = self.base + offset
            first = start + index[order[0]] * (size // 4)
            second = first + index[order[1]] * (size // 16)
            self.parts.append((order, index[order[0]], index[order[1]], size, offset, start, first, second))
            offset += size

    def rows(self, start, size):
        return pl.ds(pl.multiple_of(start, 8), size)

    def copies(self, stage):
        pos = self.pos
        if stage in (0, 6):
            src = self.buf.at[self.rows((1 - pos["co"]) * self.nh, self.nh)]
            own = self.out.at[self.rows(self.base, self.nh)]
            src, dst = (src, self.cbuf) if stage == 0 else (own, own)
            return [remote(src, dst, self.ssem.at[stage, 0], self.rsem.at[stage, 0], self.other)]
        out = []
        for p, (order, g0, g1, size, offset, start, first, second) in enumerate(self.parts):
            n0, n1 = size // 4, size // 16
            axis = order[(0, 1, 2, 1, 0)[stage - 1]]
            for d, to in enumerate(peers(pos, axis)):
                if stage == 1:
                    src = self.buf.at[self.rows(start + xor4(g0, d + 1) * n0, n0)]
                    dst = self.xbuf.at[d, pl.ds(offset // 4, n0)]
                elif stage == 2:
                    src = self.buf.at[self.rows(first + xor4(g1, d + 1) * n1, n1)]
                    dst = self.ybuf.at[d, pl.ds(offset // 16, n1)]
                elif stage == 3:
                    src, dst = self.buf.at[self.rows(second, n1)], self.zbuf.at[d, pl.ds(offset // 16, n1)]
                elif stage == 4:
                    src = dst = self.out.at[self.rows(second, n1)]
                else:
                    src = dst = self.out.at[self.rows(first, n0)]
                k = 3 * p + d
                out.append(remote(src, dst, self.ssem.at[stage, k], self.rsem.at[stage, k], to))
        return out

    def start(self, stage):
        for copy in self.copies(stage):
            copy.start()

    def finish(self, stage):
        for copy in self.copies(stage):
            copy.wait()
        if stage == 0:
            sl = self.rows(self.base, self.nh)
            self.buf[sl] = self.buf[sl] + self.cbuf[...]
        if stage not in (1, 2, 3):
            return
        came = (self.xbuf, self.ybuf, self.zbuf)[stage - 1]
        to = self.out if stage == 3 else self.buf
        for order, g0, g1, size, offset, start, first, second in self.parts:
            share = 4 if stage == 1 else 16
            sl = self.rows(first if stage == 1 else second, size // share)
            at_ = pl.ds(offset // share, size // share)
            to[sl] = (self.buf[sl] + came[0, at_]) + (came[1, at_] + came[2, at_])

    def step(self, stage):
        self.finish(stage)
        if stage < 6:
            self.start(stage + 1)


def kernel(factor, *refs):
    names_in = ["tok", "cot", "wi", "ws", "bias", "rate", "skip", "gain", "wo"]
    names_in = [name + "_h" for name in names_in]
    names_out = ["lo", "gt", "eres", "lres"]
    n_io = len(names_in) + len(names_out)
    k = dict(zip(names_in + names_out, refs[:n_io]))
    k.update(zip([name for name, _ in SCRATCH], refs[n_io:]))
    body(factor, **k)


def vm(*shape, dtype=F32):
    return pltpu.VMEM(shape, dtype)


BIG = (T, E)
SCRATCH = [
    ("x", vm(*BIG)), ("z", vm(*BIG)), ("ub", vm(2, *BIG, dtype=BF16)), ("stepe", vm(*BIG)),
    ("bt", vm(2, T, T, dtype=BF16)), ("ct", vm(2, T, T, dtype=BF16)), ("s", vm(T, T)), ("ds", vm(T, T)),
    ("wsel", vm(D, 640, dtype=BF16)), ("wpad", vm(D, 128, dtype=BF16)), ("vecs", vm(8, 128)),
    ("step", vm(T, 128)), ("sig", vm(T, 128)),
    ("cumr", vm(T, 128)), ("cumc", vm(T, 128)), ("cumrt", vm(128, T)), ("cumct", vm(128, T)),
    ("er", vm(*BIG)), ("ec", vm(*BIG)), ("wr", vm(*BIG)), ("wc", vm(*BIG)), ("dr", vm(*BIG)), ("dc", vm(*BIG)),
    ("dxr", vm(*BIG)), ("dxc", vm(*BIG)),
    ("finr", vm(SIDE, 128)), ("finc", vm(SIDE, 128)), ("allr", vm(128, 128)), ("allc", vm(128, 128)),
    ("wur", vm(2, *BIG, dtype=BF16)), ("wuc", vm(2, *BIG, dtype=BF16)),
    ("edr", vm(2, *BIG, dtype=BF16)), ("edc", vm(2, *BIG, dtype=BF16)),
    ("mr", vm(2, HEADS, T, T, dtype=BF16)), ("mc", vm(2, HEADS, T, T, dtype=BF16)), ("ls", vm(HEADS, T, T)),
    ("yr", vm(*BIG)), ("yc", vm(*BIG)), ("car", vm(*BIG)), ("cac", vm(*BIG)), ("dn", vm(*BIG)),
    ("dy", vm(*BIG)), ("dyb", vm(2, *BIG, dtype=BF16)), ("dzb", vm(*BIG, dtype=BF16)), ("nb", vm(*BIG, dtype=BF16)),
    ("qr", vm(*BIG)), ("qc", vm(*BIG)), ("dxb", vm(*BIG, dtype=BF16)), ("dux", vm(*BIG)),
    ("dbe", vm(T, T)), ("dce", vm(T, T)),
    ("own", pltpu.VMEM((4, T, E), F32)), ("got", pltpu.VMEM((4, TILES, SHARE, E), F32)),
    ("out", pltpu.VMEM((4, TILES, SHARE, E), F32)), ("res", pltpu.VMEM((4, T, E), F32)),
    ("ebuf", vm(EARLY, 128)), ("ecb", vm(EARLY // 2, 128)), ("exb", vm(3, EARLY // 8, 128)),
    ("eyb", vm(3, EARLY // 32, 128)), ("ezb", vm(3, EARLY // 32, 128)),
    ("lbuf", vm(LATE, 128)), ("lcb", vm(LATE // 2, 128)), ("lxb", vm(3, LATE // 8, 128)),
    ("lyb", vm(3, LATE // 32, 128)), ("lzb", vm(3, LATE // 32, 128)),
    ("fsem", pltpu.SemaphoreType.DMA((2, 2, TILES))),
    ("cs", pltpu.SemaphoreType.DMA((4, 2, TILES))), ("cr", pltpu.SemaphoreType.DMA((4, 2, TILES))),
    ("es", pltpu.SemaphoreType.DMA((7, 9))), ("erv", pltpu.SemaphoreType.DMA((7, 9))),
    ("lsm", pltpu.SemaphoreType.DMA((7, 9))), ("lrv", pltpu.SemaphoreType.DMA((7, 9))),
]
SCRATCH += [
    ("tok", vm(T, D, dtype=BF16)), ("cot", vm(T, D, dtype=BF16)), ("wi", vm(D, 2 * E, dtype=BF16)),
    ("ws", vm(2 * STATE + HEADS, D, dtype=BF16)), ("bias", vm(1, HEADS)), ("rate", vm(1, HEADS)),
    ("skip", vm(1, HEADS)), ("gain", vm(1, E)), ("wo", vm(E, D, dtype=BF16)),
    ("isem", pltpu.SemaphoreType.DMA((9,))),
]
RB = 32


def loop(rows, fn, init=0):
    def step(i, carry):
        return fn(pl.ds(pl.multiple_of(i * RB, RB), RB), i, carry)

    return lax.fori_loop(0, rows // RB, step, init)


def body(factor, tok_h, cot_h, wi_h, ws_h, bias_h, rate_h, skip_h, gain_h, wo_h, lo, gt, eres, lres,
         x, z, ub, stepe, bt, ct, s, ds, wsel, wpad, vecs, step, sig, cumr, cumc, cumrt, cumct,
         er, ec, wr, wc, dr, dc, dxr, dxc, finr, finc, allr, allc, wur, wuc, edr, edc, mr, mc, ls,
         yr, yc, car, cac, dn, dy, dyb, dzb, nb, qr, qc, dxb, dux, dbe, dce,
         own, got, out, res, ebuf, ecb, exb, eyb, ezb, lbuf, lcb, lxb, lyb, lzb,
         fsem, cs, cr, es, erv, lsm, lrv, tok, cot, wi, ws, bias, rate, skip, gain, wo, isem):
    pos = place()
    given = (ws_h, ws), (bias_h, bias), (rate_h, rate), (skip_h, skip), (tok_h, tok), (wi_h, wi), (cot_h, cot), (wo_h, wo), (gain_h, gain)
    fetch = [pltpu.make_async_copy(src, dst, isem.at[j]) for j, (src, dst) in enumerate(given)]
    for copy in fetch:
        copy.start()
    barrier = pltpu.get_barrier_semaphore()

    def scan(slot, axis, back):
        return Scan(pos, axis, back, own.at[slot], got.at[slot], out.at[slot], res.at[slot], (dxr, dxc)[slot % 2],
                    cs, cr, slot)

    fr, fc, gr_, gc_ = scan(0, "r", False), scan(1, "c", False), scan(2, "r", True), scan(3, "c", True)
    near = [who.peer(d)[1] for who in (fr, fc) for d in range(1, TILES)]
    near += [at(pos, xl=1 - pos["xl"]), at(pos, xl=1 - pos["xl"], xh=1 - pos["xh"])]
    for to in near:
        pl.semaphore_signal(barrier, inc=1, device_id=to, device_id_type=MESH)
    early = Total(pos, ebuf, eres, ecb, exb, eyb, ezb, es, erv)
    late = Total(pos, lbuf, lres, lcb, lxb, lyb, lzb, lsm, lrv)

    for copy in fetch[:6]:
        copy.wait()
    r, c = grid2(2 * STATE + HEADS, 640)
    sel = ((c < 256) & (r == lo4(c))) | ((c >= 256) & (c < 512) & (r == 16 + lo4(c))) | ((c >= 512) & (r == c - 480))
    wsel[...] = mm(ws[...], ind(sel), 0, 0).astype(BF16)
    r, c = grid2(2 * STATE + HEADS, 128)
    wpad[...] = mm(ws[...], ind(r == c), 0, 0).astype(BF16)
    vecs[...] = jnp.zeros((8, 128), F32)
    vecs[0:1, 0:HEADS] = bias[...]
    vecs[1:2, 0:HEADS] = rate[...]
    vecs[2:3, 0:HEADS] = skip[...]
    raw = mm(tok[...], wsel[:, 512:640]) + vecs[0:1, :]
    tail = jnp.exp(-jnp.abs(raw))
    stp = jnp.maximum(raw, 0.0) + jnp.log1p(tail)
    step[...] = stp
    sig[...] = jnp.where(raw >= 0, 1.0, tail) / (1.0 + tail)
    a = -stp * vecs[1:2, :]
    t, u = grid2(T, T)
    same_r, same_c = hi4(t) == hi4(u), lo4(t) == lo4(u)
    cumr[...] = pick(ind(same_r & (u <= t)), a)
    cumc[...] = pick(ind(same_c & (u <= t)), a)
    aft_r = pick(ind(same_r & (u > t)), a)
    aft_c = pick(ind(same_c & (u > t)), a)
    r, c = grid2(SIDE, T)
    finr[...] = jnp.exp(pick(ind(r == hi4(c)), a))
    finc[...] = jnp.exp(pick(ind(r == lo4(c)), a))
    hx = head_spread()
    stepe[...] = spread(stp, hx, 3)
    wr[...] = spread(jnp.exp(aft_r), hx)
    wc[...] = spread(jnp.exp(aft_c), hx)
    x[...] = mm(tok[...], wi[:, 0:E])
    keep(bt, (), mm(tok[...], wsel[:, 0:256]))

    def drive(sl, i, carry):
        u_ = stepe[sl] * x[sl]
        keep(ub, (sl,), u_)
        keep(wur, (sl,), wr[sl] * u_)
        keep(wuc, (sl,), wc[sl] * u_)
        return carry

    loop(T, drive)
    line_r, line_c = hi4(t) == hi4(u), lo4(t) == hi4(u)
    own[1] = mm3(only(line_c, bt), both(wuc), 0, 0)
    own[0] = mm3(only(line_r, bt), both(wur), 0, 0)
    pl.semaphore_wait(barrier, len(near))
    ends = []
    for a_, (who, mine, all_) in enumerate(((fc, finc, allc), (fr, finr, allr))):
        place_ = pl.ds(pl.multiple_of(who.me * SIDE, SIDE), SIDE)
        all_[place_] = mine[...]
        for d in range(1, TILES):
            ends.append(remote(mine, all_.at[place_], fsem.at[a_, 0, d], fsem.at[a_, 1, d], who.peer(d)[1]))
            ends[-1].start()
    fc.start()
    fr.start()

    def lines(rows, first, ends):
        k, l = grid2(rows, SIDE)
        return pick(ind(hi4(k) + first == l), spread(ends, hx), 2)

    dr[...] = lines(T, 0, finr[...])
    dc[...] = lines(T, 0, finc[...])

    z[...] = mm(tok[...], wi[:, E : 2 * E])
    keep(ct, (), mm(tok[...], wsel[:, 256:512]))
    s[...] = mm3(both(ct), both(bt), 1, 1) * (1.0 / 16.0)
    er[...] = spread(jnp.exp(cumr[...]), hx)
    ec[...] = spread(jnp.exp(cumc[...]), hx)
    cumrt[...] = cumr[...].T
    cumct[...] = cumc[...].T

    def masks(sl, i, carry):
        t_, u_ = grid2(RB, T)
        t_ = t_ + i * RB
        in_r = (hi4(t_) == hi4(u_)) & (u_ <= t_)
        in_c = (lo4(t_) == lo4(u_)) & (u_ <= t_)
        s_ = s[sl]
        c_r, c_c = cumr[sl], cumc[sl]
        for h in range(HEADS):
            l_r = jnp.exp(jnp.where(in_r, c_r[:, h : h + 1] - cumrt[h : h + 1, :], NEG))
            l_c = jnp.exp(jnp.where(in_c, c_c[:, h : h + 1] - cumct[h : h + 1, :], NEG))
            keep(mr, (h, sl), l_r * s_)
            keep(mc, (h, sl), l_c * s_)
            ls[h, sl] = l_r + l_c
        return carry

    loop(T, masks)
    low = lax.broadcasted_iota(jnp.int32, (T, 128), 1) < HDIM

    def heads(m, hp, pair, dim):
        wide = jnp.concatenate(pair, axis=1)
        part = []
        for h in (2 * hp, 2 * hp + 1):
            full = mm(m[0, h], wide, dim, 0)
            part.append(full[:, :128] + full[:, 128:] + mm(m[1, h], pair[0], dim, 0))
        return jnp.where(low, part[0], part[1])

    def within(hp, carry):
        sl = pl.ds(pl.multiple_of(hp * 128, 128), 128)
        u_ = (ub[0, :, sl], ub[1, :, sl])
        yr[:, sl] = heads(mr, hp, u_, 1)
        yc[:, sl] = heads(mc, hp, u_, 1)
        return carry

    for copy in fetch[6:]:
        copy.wait()

    for copy in ends:
        copy.wait_recv()
    k, l = grid2(T, 128)
    line = lax.shift_right_logical(k, 5) * SIDE + jnp.bitwise_and(hi4(k), 1)
    for who, all_ in ((fr, allr), (fc, allc)):
        who.dec[...] = spread(pick(ind(l == line + 2 * who.me), all_[...], 2), hx)
    fr.turn()
    fc.turn()
    lax.fori_loop(0, HEADS // 2, within, 0)
    dn[...] = mm(cot[...], wo[...], 1, 1)
    fr.finish()
    car[...] = mm3(only(line_r, ct), split(res[0], 2))
    fc.finish()
    cac[...] = mm3(only(line_c, ct), split(res[1], 2))

    skipe = spread(vecs[...], hx, 3)[2:3, :]
    gain_ = gain[...]

    def middle(sl, i, carry):
        sum_gain, sum_skip = carry
        x_, z_ = x[sl], z[sl]
        c_r, c_c = er[sl] * car[sl], ec[sl] * cac[sl]
        w_r, w_c = yr[sl], yc[sl]
        y = (w_r + w_c) + (c_r + c_c) + skipe * x_
        sg = 1.0 / (1.0 + jnp.exp(-z_))
        act = z_ * sg
        gated = y * act
        inv = lax.rsqrt(jnp.mean(gated * gated, axis=-1, keepdims=True) + 1e-05)
        unit = gated * inv
        nb[sl] = (unit * gain_).astype(BF16)
        d_n = dn[sl]
        g1 = d_n * gain_
        dg = inv * (g1 - unit * jnp.mean(g1 * unit, axis=-1, keepdims=True))
        d_y = dg * act
        dzb[sl] = (dg * y * (sg * (1.0 + z_ * (1.0 - sg)))).astype(BF16)
        dy[sl] = d_y
        keep(dyb, (sl,), d_y)
        keep(edr, (sl,), er[sl] * d_y)
        keep(edc, (sl,), ec[sl] * d_y)
        qr[sl] = d_y * (c_r + w_r)
        qc[sl] = d_y * (c_c + w_c)
        fold = lambda v: functools.reduce(lambda p, q: p + q, [v[8 * j : 8 * j + 8] for j in range(RB // 8)])
        return sum_gain + fold(d_n * unit), sum_skip + fold(d_y * x_)

    nil = jnp.zeros((8, E), F32)
    sum_gain, sum_skip = loop(T, middle, (nil, nil))
    own[3] = mm3(only(line_c, ct), both(edc), 0, 0)
    gc_.start()
    own[2] = mm3(only(line_r, ct), both(edr), 0, 0)
    gr_.start()

    lg = mm(tok[...], dzb[...], 0, 0) * factor
    for j in range(4):
        ebuf[j * 256 : (j + 1) * 256] = lg[:, j * 128 : (j + 1) * 128]
    lg = mm(nb[...], cot[...], 0, 0) * factor
    for j in range(2):
        ebuf[1024 + j * 512 : 1024 + (j + 1) * 512] = lg[:, j * 128 : (j + 1) * 128]
    early.start(0)
    def within_back(hp, carry):
        sl = pl.ds(pl.multiple_of(hp * 128, 128), 128)
        d_ = (dyb[0, :, sl], dyb[1, :, sl])
        yr[:, sl] = heads(mr, hp, d_, 0)
        yc[:, sl] = heads(mc, hp, d_, 0)
        return carry


    def scores_back(hp, carry):
        sl = pl.ds(pl.multiple_of(hp * 128, 128), 128)
        u_h, u_l = ub[0, :, sl], ub[1, :, sl]
        twice = jnp.concatenate((u_h, u_h), axis=1)
        total = ds[...]
        for j in (0, 1):
            d_h, d_l = only(low if j == 0 else ~low, (dyb[0, :, sl], dyb[1, :, sl]))
            pairs = mm(jnp.concatenate((d_h, d_l), axis=1), twice, 1, 1) + mm(d_h, u_l, 1, 1)
            total = total + ls[2 * hp + j] * pairs
        ds[...] = total
        return carry

    lax.fori_loop(0, HEADS // 2, within_back, 0)
    gr_.turn()
    gc_.turn()
    early.step(0)
    ds[...] = jnp.zeros((T, T), F32)
    lax.fori_loop(0, HEADS // 2, scores_back, 0)
    head = u < STATE
    d_s = split(ds[...], 2)
    dce[...] = (
        jnp.where(line_r, mm3(both(edr), split(res[0], 2), 1, 1), 0.0)
        + jnp.where(line_c, mm3(both(edc), split(res[1], 2), 1, 1), 0.0)
        + jnp.where(head, mm3(d_s, both(bt)), 0.0)
    )
    dbe[...] = jnp.where(head, mm3(d_s, both(ct), 0, 0), 0.0)
    lo[...] = mm(nb[...], wo[...]).astype(BF16)
    early.step(1)
    gr_.finish()
    g_r = split(res[2], 2)
    car[...] = mm3(only(line_r, bt), g_r)
    dbe[...] = dbe[...] + jnp.where(line_r, mm3(both(wur), g_r, 1, 1), 0.0)
    early.step(2)
    gc_.finish()
    g_c = split(res[3], 2)
    cac[...] = mm3(only(line_c, bt), g_c)
    dbe[...] = dbe[...] + jnp.where(line_c, mm3(both(wuc), g_c, 1, 1), 0.0)

    def last(sl, i, carry):
        x_, se = x[sl], stepe[sl]
        u_ = se * x_
        v_r, v_c = wr[sl] * car[sl], wc[sl] * cac[sl]
        w_r, w_c = yr[sl], yc[sl]
        qr[sl] = qr[sl] - u_ * (v_r + w_r)
        qc[sl] = qc[sl] - u_ * (v_c + w_c)
        d_u = (w_r + w_c) + (v_r + v_c)
        dux[sl] = d_u * x_
        dxb[sl] = (se * d_u + skipe * dy[sl]).astype(BF16)
        res[0, sl] = res[2, sl] * (own[0, sl] + dr[sl] * res[0, sl])
        res[1, sl] = res[3, sl] * (own[1, sl] + dc[sl] * res[1, sl])
        return carry

    loop(T, last)
    lg = mm(tok[...], dxb[...], 0, 0) * factor
    for j in range(4):
        lbuf[j * 256 : (j + 1) * 256] = lg[:, j * 128 : (j + 1) * 128]
    d_a = (
        pick(ind(same_r & (u >= t)), head_sum(qr[...]))
        + pick(ind(same_c & (u >= t)), head_sum(qc[...]))
        + pick(ind(line_r), head_sum(res[0]))
        + pick(ind(line_c), head_sum(res[1]))
    )
    d_step = head_sum(dux[...]) - vecs[1:2, :] * d_a
    d_raw = d_step * sig[...]
    r, c = grid2(T, 128)
    d_ssm = (
        spread(dbe[...], ind(c == lo4(r)))
        + spread(dce[...], ind(c == 16 + lo4(r)))
        + spread(d_raw, ind(grid2(128, 128)[1] == 32 + grid2(128, 128)[0]), 3)
    )
    d_ssm = d_ssm.astype(BF16)
    lg = mm(d_ssm, tok[...], 0, 0) * factor
    for j in range(2):
        lbuf[1024 + j * 128 : 1152 + j * 128] = lg[:, j * 128 : (j + 1) * 128]
    total_of = lambda v: jnp.sum(v, axis=0, keepdims=True)
    sum_gain = total_of(sum_gain) * factor
    for j in range(4):
        lbuf[1088 + j : 1089 + j] = sum_gain[:, j * 128 : (j + 1) * 128]
    lbuf[1092:1093] = total_of(d_raw) * factor
    lbuf[1093:1094] = -total_of(step[...] * d_a) * factor
    lbuf[1094:1095] = total_of(head_sum(sum_skip)) * factor
    late.start(0)
    early.step(3)
    late.step(0)
    back = mm(dxb[...], wi[:, 0:E], 1, 1) + mm(dzb[...], wi[:, E : 2 * E], 1, 1)
    back = back + mm(d_ssm, wpad[...], 1, 1)
    gt[...] = back.astype(BF16)
    early.step(4)
    late.step(1)
    early.step(5)
    late.step(2)
    early.step(6)
    late.step(3)
    for who in (fr, fc, gr_, gc_):
        who.drain()
    for copy in ends:
        copy.wait_send()
    late.step(4)
    late.step(5)
    late.step(6)


def unpack(eres, lres, lo_in, gt_in, lo, gt, gi, gs, go, gb, gr, gk, gg):
    lo[...] = lo_in[...]
    gt[...] = gt_in[...]
    for j in range(4):
        gi[:, j * 128 : (j + 1) * 128] = lres[j * 256 : (j + 1) * 256]
        gi[:, E + j * 128 : E + (j + 1) * 128] = eres[j * 256 : (j + 1) * 256]
        gg[:, j * 128 : (j + 1) * 128] = lres[1088 + j : 1089 + j]
    for j in range(2):
        go[:, j * 128 : (j + 1) * 128] = eres[1024 + j * 512 : 1024 + (j + 1) * 512]
        gs[:, j * 128 : (j + 1) * 128] = lres[1024 + j * 128 : 1064 + j * 128]
    gb[...] = lres[1092:1093, 0:HEADS]
    gr[...] = lres[1093:1094, 0:HEADS]
    gk[...] = lres[1094:1095, 0:HEADS]


def local(tokens_in, out_cotangent, w_inner, w_ssm, dt_bias, decay_rate, skip_gain, norm_gain, w_out):
    devices = lax.axis_size("slide") * lax.axis_size("row") * lax.axis_size("col")
    factor = float(devices * T) ** -0.5
    shape = jax.ShapeDtypeStruct
    vmem = pl.BlockSpec(memory_space=pltpu.VMEM)
    lo, gt, eres, lres = pl.pallas_call(
        functools.partial(kernel, factor),
        out_shape=(shape((T, D), BF16), shape((T, D), BF16), shape((EARLY, 128), F32), shape((LATE, 128), F32)),
        in_specs=[pl.BlockSpec(memory_space=pltpu.HBM)] * 9,
        out_specs=(vmem,) * 4,
        scratch_shapes=[kind for _, kind in SCRATCH],
        compiler_params=pltpu.CompilerParams(
            collective_id=0, has_side_effects=True, vmem_limit_bytes=48 * 2**20
        ),
    )(
        *[
            pltpu.with_memory_space_constraint(array, pltpu.HBM)
            for array in (
                tokens_in.reshape(T, D),
                out_cotangent.reshape(T, D),
                w_inner,
                w_ssm.T,
                dt_bias.reshape(1, -1),
                decay_rate.reshape(1, -1),
                skip_gain.reshape(1, -1),
                norm_gain.reshape(1, -1),
                w_out,
            )
        ]
    )
    out = pl.pallas_call(
        unpack,
        out_shape=(
            shape((T, D), BF16),
            shape((T, D), BF16),
            shape(w_inner.shape, F32),
            shape(w_ssm.shape[::-1], F32),
            shape(w_out.shape, F32),
            shape((1, HEADS), F32),
            shape((1, HEADS), F32),
            shape((1, HEADS), F32),
            shape((1, E), F32),
        ),
        in_specs=[vmem] * 4,
        out_specs=(vmem,) * 9,
        compiler_params=pltpu.CompilerParams(vmem_limit_bytes=6 * 2**20),
    )(eres, lres, lo, gt)
    return (
        out[0].reshape(tokens_in.shape),
        out[1].reshape(tokens_in.shape),
        out[2],
        out[3].T,
        out[4],
        out[5].reshape(-1),
        out[6].reshape(-1),
        out[7].reshape(-1),
        out[8].reshape(-1),
    )


def solution(mesh):
    tiles = P("slide", "row", "col", None)
    return jax.shard_map(
        local,
        mesh=mesh,
        in_specs=(tiles, tiles) + (P(),) * 7,
        out_specs=(tiles, tiles) + (P(),) * 7,
        check_vma=False,
    )
```

```python
import functools

import jax
import jax.numpy as jnp
from jax import lax
from jax.experimental import pallas as pl
from jax.experimental.pallas import tpu as pltpu
from jax.sharding import PartitionSpec as P

MESH = pl.DeviceIdType.MESH
F32 = jnp.float32
BF16 = jnp.bfloat16
HEADS = 8
HDIM = 64
STATE = 16
SIDE = 16
T = SIDE * SIDE
E = HEADS * HDIM
D = 256
TILES = 8
SHARE = T // TILES
PARTS = SHARE // STATE
NEG = -1e30
EARLY = 2048
LATE = 1280
LROW = (0, 256, 640, 896)
SROW = (512, 1152)
VROW = 512 + 64


def mm(a, b, ca=1, cb=0):
    return lax.dot_general(a, b, (((ca,), (cb,)), ((), ())), preferred_element_type=F32)


def split(x, terms):
    out = []
    for _ in range(terms - 1):
        hi = x.astype(BF16)
        out.append(hi)
        x = x - hi.astype(F32)
    out.append(x.astype(BF16))
    return out


def pick(mask, x, terms=3):
    return functools.reduce(lambda u, v: u + v, [mm(mask, part) for part in split(x, terms)])


def spread(x, mask, terms=2):
    return functools.reduce(lambda u, v: u + v, [mm(part, mask) for part in split(x, terms)])


def mm3(a, b, ca=1, cb=0):
    (ah, al), (bh, bl) = a, b
    return mm(ah, bh, ca, cb) + (mm(ah, bl, ca, cb) + mm(al, bh, ca, cb))


def keep(pair, where, x):
    hi, lo = split(x, 2)
    pair[(0,) + where] = hi
    pair[(1,) + where] = lo


def both(pair):
    return pair[0], pair[1]


def only(mask, pair):
    nil = jnp.zeros(mask.shape, BF16)
    return jnp.where(mask, pair[0], nil), jnp.where(mask, pair[1], nil)


def ind(cond):
    return jnp.where(cond, 1.0, 0.0).astype(BF16)


def grid2(rows, cols):
    return (
        lax.broadcasted_iota(jnp.int32, (rows, cols), 0),
        lax.broadcasted_iota(jnp.int32, (rows, cols), 1),
    )


def hi4(x):
    return lax.shift_right_logical(x, 4)


def lo4(x):
    return jnp.bitwise_and(x, 15)


def head_spread():
    r, c = grid2(128, E)
    return ind(r == lax.shift_right_logical(c, 6))


def head_sum(x):
    r, c = grid2(E, 128)
    return spread(x, ind(lax.shift_right_logical(r, 6) == c), 2)


def place():
    row, col, slide = lax.axis_index("row"), lax.axis_index("col"), lax.axis_index("slide")
    return dict(y=row // 2, xh=lax.rem(row, 2), z=col // 2, co=lax.rem(col, 2), xl=slide)


def at(pos, **change):
    p = dict(pos, **change)
    return (p["y"] * 2 + p["xh"], p["z"] * 2 + p["co"], p["xl"])


def flip(bit, by):
    return bit + by * (1 - 2 * bit)


def peers(pos, axis):
    out = []
    for d in (1, 2, 3):
        if axis == "x":
            out.append(at(pos, xh=flip(pos["xh"], d // 2), xl=flip(pos["xl"], d % 2)))
        else:
            out.append(at(pos, **{axis: xor4(pos[axis], d)}))
    return out


def xor4(q, d):
    return 2 * flip(q // 2, d // 2) + flip(lax.rem(q, 2), d % 2)


def remote(src, dst, ssem, rsem, to):
    return pltpu.make_async_remote_copy(
        src_ref=src, dst_ref=dst, send_sem=ssem, recv_sem=rsem, device_id=to, device_id_type=MESH
    )


class Scan:
    def __init__(self, pos, axis, back, own, got, out, res, dec, ssem, rsem, slot):
        self.me = lax.axis_index("col" if axis == "r" else "row")
        self.pos, self.axis, self.back = pos, axis, back
        self.own, self.got, self.out, self.res, self.dec = own, got, out, res, dec
        self.ssem, self.rsem, self.slot = ssem, rsem, slot

    def peer(self, d):
        k = lax.rem(self.me + d, TILES)
        if self.axis == "r":
            return k, (lax.axis_index("row"), k, self.pos["xl"])
        return k, (k, lax.axis_index("col"), self.pos["xl"])

    def lines(self, k, part):
        return pl.ds(pl.multiple_of(k * SHARE + part * STATE, STATE), STATE)

    def copies(self, stage, part):
        out, piece = [], pl.ds(part * STATE, STATE)
        for d in (4, 3, 5, 2, 6, 1, 7):
            k, to = self.peer(d)
            sems = self.ssem.at[self.slot, stage, part, d], self.rsem.at[self.slot, stage, part, d]
            if stage == 0:
                out.append(remote(self.own.at[self.lines(k, part)], self.got.at[self.me, piece], *sems, to))
            else:
                out.append(remote(self.out.at[k, piece], self.res.at[self.lines(self.me, part)], *sems, to))
        return out

    def start(self, part):
        for copy in self.copies(0, part):
            copy.start()
        self.got[self.me, pl.ds(part * STATE, STATE)] = self.own[self.lines(self.me, part)]

    def turn(self, part):
        for copy in self.copies(0, part):
            copy.wait_recv()
        state, piece = jnp.zeros((STATE, E), F32), pl.ds(part * STATE, STATE)
        for j in range(TILES - 1, -1, -1) if self.back else range(TILES):
            self.out[j, piece] = state
            state = self.dec[pl.ds(j * SHARE + part * STATE, STATE)] * state + self.got[j, piece]
        for copy in self.copies(1, part):
            copy.start()
        self.res[self.lines(self.me, part)] = self.out[self.me, piece]

    def finish(self):
        for part in range(PARTS):
            for copy in self.copies(1, part):
                copy.wait_recv()

    def drain(self):
        for stage in (0, 1):
            for part in range(PARTS):
                for copy in self.copies(stage, part):
                    copy.wait_send()


class Total:
    def __init__(self, pos, buf, out, cbuf, xbuf, ybuf, zbuf, ssem, rsem):
        n = buf.shape[0]
        self.pos, self.buf, self.out = pos, buf, out
        self.cbuf, self.xbuf, self.ybuf, self.zbuf = cbuf, xbuf, ybuf, zbuf
        self.ssem, self.rsem = ssem, rsem
        self.nh = n // 2
        self.base = pos["co"] * self.nh
        self.other = at(pos, co=1 - pos["co"])
        index = {"x": pos["xh"] * 2 + pos["xl"], "y": pos["y"], "z": pos["z"]}
        third = -(-self.nh // 384) * 128
        sizes = (third, third, self.nh - 2 * third)
        self.parts, offset = [], 0
        for size, order in zip(sizes, ("xyz", "yzx", "zxy")):
            start = self.base + offset
            first = start + index[order[0]] * (size // 4)
            second = first + index[order[1]] * (size // 16)
            self.parts.append((order, index[order[0]], index[order[1]], size, offset, start, first, second))
            offset += size

    def rows(self, start, size):
        return pl.ds(pl.multiple_of(start, 8), size)

    def copies(self, stage):
        pos = self.pos
        if stage in (0, 6):
            src = self.buf.at[self.rows((1 - pos["co"]) * self.nh, self.nh)]
            own = self.out.at[self.rows(self.base, self.nh)]
            src, dst = (src, self.cbuf) if stage == 0 else (own, own)
            return [remote(src, dst, self.ssem.at[stage, 0], self.rsem.at[stage, 0], self.other)]
        out = []
        for p, (order, g0, g1, size, offset, start, first, second) in enumerate(self.parts):
            n0, n1 = size // 4, size // 16
            axis = order[(0, 1, 2, 1, 0)[stage - 1]]
            for d, to in enumerate(peers(pos, axis)):
                if stage == 1:
                    src = self.buf.at[self.rows(start + xor4(g0, d + 1) * n0, n0)]
                    dst = self.xbuf.at[d, pl.ds(offset // 4, n0)]
                elif stage == 2:
                    src = self.buf.at[self.rows(first + xor4(g1, d + 1) * n1, n1)]
                    dst = self.ybuf.at[d, pl.ds(offset // 16, n1)]
                elif stage == 3:
                    src, dst = self.buf.at[self.rows(second, n1)], self.zbuf.at[d, pl.ds(offset // 16, n1)]
                elif stage == 4:
                    src = dst = self.out.at[self.rows(second, n1)]
                else:
                    src = dst = self.out.at[self.rows(first, n0)]
                k = 3 * p + d
                out.append(remote(src, dst, self.ssem.at[stage, k], self.rsem.at[stage, k], to))
        return out

    def start(self, stage):
        for copy in self.copies(stage):
            copy.start()

    def finish(self, stage):
        for copy in self.copies(stage):
            copy.wait()
        if stage == 0:
            sl = self.rows(self.base, self.nh)
            self.buf[sl] = self.buf[sl] + self.cbuf[...]
        if stage not in (1, 2, 3):
            return
        came = (self.xbuf, self.ybuf, self.zbuf)[stage - 1]
        to = self.out if stage == 3 else self.buf
        for order, g0, g1, size, offset, start, first, second in self.parts:
            share = 4 if stage == 1 else 16
            sl = self.rows(first if stage == 1 else second, size // share)
            at_ = pl.ds(offset // share, size // share)
            to[sl] = (self.buf[sl] + came[0, at_]) + (came[1, at_] + came[2, at_])

    def step(self, stage):
        self.finish(stage)
        if stage < 6:
            self.start(stage + 1)


def kernel(factor, *refs):
    names_in = ["tok", "cot", "wi", "ws", "bias", "rate", "skip", "gain", "wo"]
    names_in = [name + "_h" for name in names_in]
    names_out = ["lo", "gt", "eres", "lres"]
    n_io = len(names_in) + len(names_out)
    k = dict(zip(names_in + names_out, refs[:n_io]))
    k.update(zip([name for name, _ in SCRATCH], refs[n_io:]))
    body(factor, **k)


def vm(*shape, dtype=F32):
    return pltpu.VMEM(shape, dtype)


BIG = (T, E)
SCRATCH = [
    ("x", vm(*BIG)), ("z", vm(*BIG)), ("ub", vm(2, *BIG, dtype=BF16)), ("stepe", vm(*BIG)),
    ("bt", vm(2, T, T, dtype=BF16)), ("ct", vm(2, T, T, dtype=BF16)), ("s", vm(T, T)), ("ds", vm(T, T)),
    ("wsel", vm(D, 640, dtype=BF16)), ("wpad", vm(D, 128, dtype=BF16)), ("vecs", vm(8, 128)),
    ("step", vm(T, 128)), ("sig", vm(T, 128)),
    ("cumr", vm(T, 128)), ("cumc", vm(T, 128)), ("cumrt", vm(128, T)), ("cumct", vm(128, T)),
    ("er", vm(*BIG)), ("ec", vm(*BIG)), ("wr", vm(*BIG)), ("wc", vm(*BIG)), ("dr", vm(*BIG)), ("dc", vm(*BIG)),
    ("dxr", vm(*BIG)), ("dxc", vm(*BIG)),
    ("finr", vm(SIDE, 128)), ("finc", vm(SIDE, 128)), ("allr", vm(128, 128)), ("allc", vm(128, 128)),
    ("wur", vm(2, *BIG, dtype=BF16)), ("wuc", vm(2, *BIG, dtype=BF16)),
    ("edr", vm(2, *BIG, dtype=BF16)), ("edc", vm(2, *BIG, dtype=BF16)),
    ("mr", vm(2, HEADS, T, T, dtype=BF16)), ("mc", vm(2, HEADS, T, T, dtype=BF16)), ("ls", vm(HEADS, T, T)),
    ("yr", vm(*BIG)), ("yc", vm(*BIG)), ("car", vm(*BIG)), ("cac", vm(*BIG)), ("dn", vm(*BIG)),
    ("dy", vm(*BIG)), ("dyb", vm(2, *BIG, dtype=BF16)), ("dzb", vm(*BIG, dtype=BF16)), ("nb", vm(*BIG, dtype=BF16)),
    ("qr", vm(*BIG)), ("qc", vm(*BIG)), ("dxb", vm(*BIG, dtype=BF16)), ("dux", vm(*BIG)),
    ("dbe", vm(T, T)), ("dce", vm(T, T)),
    ("own", pltpu.VMEM((4, T, E), F32)), ("got", pltpu.VMEM((4, TILES, SHARE, E), F32)),
    ("out", pltpu.VMEM((4, TILES, SHARE, E), F32)), ("res", pltpu.VMEM((4, T, E), F32)),
    ("ebuf", vm(EARLY, 128)), ("ecb", vm(EARLY // 2, 128)), ("exb", vm(3, EARLY // 8, 128)),
    ("eyb", vm(3, EARLY // 32, 128)), ("ezb", vm(3, EARLY // 32, 128)),
    ("lbuf", vm(LATE, 128)), ("lcb", vm(LATE // 2, 128)), ("lxb", vm(3, LATE // 8, 128)),
    ("lyb", vm(3, LATE // 32, 128)), ("lzb", vm(3, LATE // 32, 128)),
    ("fsem", pltpu.SemaphoreType.DMA((2, 2, TILES))),
    ("cs", pltpu.SemaphoreType.DMA((4, 2, PARTS, TILES))), ("cr", pltpu.SemaphoreType.DMA((4, 2, PARTS, TILES))),
    ("es", pltpu.SemaphoreType.DMA((7, 9))), ("erv", pltpu.SemaphoreType.DMA((7, 9))),
    ("lsm", pltpu.SemaphoreType.DMA((7, 9))), ("lrv", pltpu.SemaphoreType.DMA((7, 9))),
]
SCRATCH += [
    ("tok", vm(T, D, dtype=BF16)), ("cot", vm(T, D, dtype=BF16)), ("wi", vm(D, 2 * E, dtype=BF16)),
    ("ws", vm(2 * STATE + HEADS, D, dtype=BF16)), ("bias", vm(1, HEADS)), ("rate", vm(1, HEADS)),
    ("skip", vm(1, HEADS)), ("gain", vm(1, E)), ("wo", vm(E, D, dtype=BF16)),
    ("isem", pltpu.SemaphoreType.DMA((9,))),
]
RB = 32


def loop(rows, fn, init=0):
    def step(i, carry):
        return fn(pl.ds(pl.multiple_of(i * RB, RB), RB), i, carry)

    return lax.fori_loop(0, rows // RB, step, init)


def body(factor, tok_h, cot_h, wi_h, ws_h, bias_h, rate_h, skip_h, gain_h, wo_h, lo, gt, eres, lres,
         x, z, ub, stepe, bt, ct, s, ds, wsel, wpad, vecs, step, sig, cumr, cumc, cumrt, cumct,
         er, ec, wr, wc, dr, dc, dxr, dxc, finr, finc, allr, allc, wur, wuc, edr, edc, mr, mc, ls,
         yr, yc, car, cac, dn, dy, dyb, dzb, nb, qr, qc, dxb, dux, dbe, dce,
         own, got, out, res, ebuf, ecb, exb, eyb, ezb, lbuf, lcb, lxb, lyb, lzb,
         fsem, cs, cr, es, erv, lsm, lrv, tok, cot, wi, ws, bias, rate, skip, gain, wo, isem):
    pos = place()
    given = (ws_h, ws), (bias_h, bias), (rate_h, rate), (skip_h, skip), (tok_h, tok), (wi_h, wi), (cot_h, cot), (wo_h, wo), (gain_h, gain)
    fetch = [pltpu.make_async_copy(src, dst, isem.at[j]) for j, (src, dst) in enumerate(given)]
    for copy in fetch:
        copy.start()
    barrier = pltpu.get_barrier_semaphore()

    def scan(slot, axis, back):
        return Scan(pos, axis, back, own.at[slot], got.at[slot], out.at[slot], res.at[slot], (dxr, dxc)[slot % 2],
                    cs, cr, slot)

    fr, fc, gr_, gc_ = scan(0, "r", False), scan(1, "c", False), scan(2, "r", True), scan(3, "c", True)
    near = [who.peer(d)[1] for who in (fr, fc) for d in range(1, TILES)]
    near += [at(pos, xl=1 - pos["xl"]), at(pos, xl=1 - pos["xl"], xh=1 - pos["xh"])]
    for to in near:
        pl.semaphore_signal(barrier, inc=1, device_id=to, device_id_type=MESH)
    early = Total(pos, ebuf, eres, ecb, exb, eyb, ezb, es, erv)
    late = Total(pos, lbuf, lres, lcb, lxb, lyb, lzb, lsm, lrv)

    for copy in fetch[:6]:
        copy.wait()
    r, c = grid2(2 * STATE + HEADS, 640)
    sel = ((c < 256) & (r == lo4(c))) | ((c >= 256) & (c < 512) & (r == 16 + lo4(c))) | ((c >= 512) & (r == c - 480))
    wsel[...] = mm(ws[...], ind(sel), 0, 0).astype(BF16)
    r, c = grid2(2 * STATE + HEADS, 128)
    wpad[...] = mm(ws[...], ind(r == c), 0, 0).astype(BF16)
    vecs[...] = jnp.zeros((8, 128), F32)
    vecs[0:1, 0:HEADS] = bias[...]
    vecs[1:2, 0:HEADS] = rate[...]
    vecs[2:3, 0:HEADS] = skip[...]
    raw = mm(tok[...], wsel[:, 512:640]) + vecs[0:1, :]
    tail = jnp.exp(-jnp.abs(raw))
    stp = jnp.maximum(raw, 0.0) + jnp.log1p(tail)
    step[...] = stp
    sig[...] = jnp.where(raw >= 0, 1.0, tail) / (1.0 + tail)
    a = -stp * vecs[1:2, :]
    t, u = grid2(T, T)
    same_r, same_c = hi4(t) == hi4(u), lo4(t) == lo4(u)
    aft_r = pick(ind(same_r & (u > t)), a)
    aft_c = pick(ind(same_c & (u > t)), a)
    r, c = grid2(SIDE, T)
    finr[...] = jnp.exp(pick(ind(r == hi4(c)), a))
    finc[...] = jnp.exp(pick(ind(r == lo4(c)), a))
    hx = head_spread()
    stepe[...] = spread(stp, hx, 3)
    wr[...] = spread(jnp.exp(aft_r), hx)
    wc[...] = spread(jnp.exp(aft_c), hx)
    x[...] = mm(tok[...], wi[:, 0:E])
    keep(bt, (), mm(tok[...], wsel[:, 0:256]))

    def drive(sl, i, carry):
        u_ = stepe[sl] * x[sl]
        keep(ub, (sl,), u_)
        keep(wur, (sl,), wr[sl] * u_)
        keep(wuc, (sl,), wc[sl] * u_)
        return carry

    loop(T, drive)
    line_r, line_c = hi4(t) == hi4(u), lo4(t) == hi4(u)
    own[1] = mm3(only(line_c, bt), both(wuc), 0, 0)
    own[0] = mm3(only(line_r, bt), both(wur), 0, 0)
    pl.semaphore_wait(barrier, len(near))
    ends = []
    for a_, (who, mine, all_) in enumerate(((fc, finc, allc), (fr, finr, allr))):
        place_ = pl.ds(pl.multiple_of(who.me * SIDE, SIDE), SIDE)
        all_[place_] = mine[...]
        for d in range(1, TILES):
            ends.append(remote(mine, all_.at[place_], fsem.at[a_, 0, d], fsem.at[a_, 1, d], who.peer(d)[1]))
            ends[-1].start()
    for part in range(PARTS):
        fc.start(part)
        fr.start(part)

    cumr[...] = pick(ind(same_r & (u <= t)), a)
    cumc[...] = pick(ind(same_c & (u <= t)), a)

    def lines(rows, first, ends):
        k, l = grid2(rows, SIDE)
        return pick(ind(hi4(k) + first == l), spread(ends, hx), 2)

    dr[...] = lines(T, 0, finr[...])
    dc[...] = lines(T, 0, finc[...])

    z[...] = mm(tok[...], wi[:, E : 2 * E])
    keep(ct, (), mm(tok[...], wsel[:, 256:512]))
    s[...] = mm3(both(ct), both(bt), 1, 1) * (1.0 / 16.0)
    er[...] = spread(jnp.exp(cumr[...]), hx)
    ec[...] = spread(jnp.exp(cumc[...]), hx)
    cumrt[...] = cumr[...].T
    cumct[...] = cumc[...].T

    def masks(sl, i, carry):
        t_, u_ = grid2(RB, T)
        t_ = t_ + i * RB
        in_r = (hi4(t_) == hi4(u_)) & (u_ <= t_)
        in_c = (lo4(t_) == lo4(u_)) & (u_ <= t_)
        s_ = s[sl]
        c_r, c_c = cumr[sl], cumc[sl]
        for h in range(HEADS):
            l_r = jnp.exp(jnp.where(in_r, c_r[:, h : h + 1] - cumrt[h : h + 1, :], NEG))
            l_c = jnp.exp(jnp.where(in_c, c_c[:, h : h + 1] - cumct[h : h + 1, :], NEG))
            keep(mr, (h, sl), l_r * s_)
            keep(mc, (h, sl), l_c * s_)
            ls[h, sl] = l_r + l_c
        return carry

    loop(T, masks)
    low = lax.broadcasted_iota(jnp.int32, (T, 128), 1) < HDIM

    def heads(m, hp, pair, dim):
        wide = jnp.concatenate(pair, axis=1)
        part = []
        for h in (2 * hp, 2 * hp + 1):
            full = mm(m[0, h], wide, dim, 0)
            part.append(full[:, :128] + full[:, 128:] + mm(m[1, h], pair[0], dim, 0))
        return jnp.where(low, part[0], part[1])

    def within(hp, carry):
        sl = pl.ds(pl.multiple_of(hp * 128, 128), 128)
        u_ = (ub[0, :, sl], ub[1, :, sl])
        yr[:, sl] = heads(mr, hp, u_, 1)
        yc[:, sl] = heads(mc, hp, u_, 1)
        return carry

    for copy in fetch[6:]:
        copy.wait()

    for copy in ends:
        copy.wait_recv()
    k, l = grid2(T, 128)
    line = lax.shift_right_logical(k, 5) * SIDE + jnp.bitwise_and(hi4(k), 1)
    for who, all_ in ((fr, allr), (fc, allc)):
        who.dec[...] = spread(pick(ind(l == line + 2 * who.me), all_[...], 2), hx)
    for part in range(PARTS):
        fr.turn(part)
        fc.turn(part)
    lax.fori_loop(0, HEADS // 2, within, 0)
    dn[...] = mm(cot[...], wo[...], 1, 1)
    fr.finish()
    car[...] = mm3(only(line_r, ct), split(res[0], 2))
    fc.finish()
    cac[...] = mm3(only(line_c, ct), split(res[1], 2))

    skipe = spread(vecs[...], hx, 3)[2:3, :]
    gain_ = gain[...]

    def middle(sl, i, carry):
        sum_gain, sum_skip = carry
        x_, z_ = x[sl], z[sl]
        c_r, c_c = er[sl] * car[sl], ec[sl] * cac[sl]
        w_r, w_c = yr[sl], yc[sl]
        y = (w_r + w_c) + (c_r + c_c) + skipe * x_
        sg = 1.0 / (1.0 + jnp.exp(-z_))
        act = z_ * sg
        gated = y * act
        inv = lax.rsqrt(jnp.mean(gated * gated, axis=-1, keepdims=True) + 1e-05)
        unit = gated * inv
        nb[sl] = (unit * gain_).astype(BF16)
        d_n = dn[sl]
        g1 = d_n * gain_
        dg = inv * (g1 - unit * jnp.mean(g1 * unit, axis=-1, keepdims=True))
        d_y = dg * act
        dzb[sl] = (dg * y * (sg * (1.0 + z_ * (1.0 - sg)))).astype(BF16)
        dy[sl] = d_y
        keep(dyb, (sl,), d_y)
        keep(edr, (sl,), er[sl] * d_y)
        keep(edc, (sl,), ec[sl] * d_y)
        qr[sl] = d_y * (c_r + w_r)
        qc[sl] = d_y * (c_c + w_c)
        fold = lambda v: functools.reduce(lambda p, q: p + q, [v[8 * j : 8 * j + 8] for j in range(RB // 8)])
        return sum_gain + fold(d_n * unit), sum_skip + fold(d_y * x_)

    nil = jnp.zeros((8, E), F32)
    sum_gain, sum_skip = loop(T, middle, (nil, nil))
    own[3] = mm3(only(line_c, ct), both(edc), 0, 0)
    for part in range(PARTS):
        gc_.start(part)
    own[2] = mm3(only(line_r, ct), both(edr), 0, 0)
    for part in range(PARTS):
        gr_.start(part)

    lg = mm(tok[...], dzb[...], 0, 0) * factor
    for j in range(4):
        ebuf[j * 256 : (j + 1) * 256] = lg[:, j * 128 : (j + 1) * 128]
    lg = mm(nb[...], cot[...], 0, 0) * factor
    for j in range(2):
        ebuf[1024 + j * 512 : 1024 + (j + 1) * 512] = lg[:, j * 128 : (j + 1) * 128]
    early.start(0)
    def within_back(hp, carry):
        sl = pl.ds(pl.multiple_of(hp * 128, 128), 128)
        d_ = (dyb[0, :, sl], dyb[1, :, sl])
        yr[:, sl] = heads(mr, hp, d_, 0)
        yc[:, sl] = heads(mc, hp, d_, 0)
        return carry


    def scores_back(hp, carry):
        sl = pl.ds(pl.multiple_of(hp * 128, 128), 128)
        u_h, u_l = ub[0, :, sl], ub[1, :, sl]
        twice = jnp.concatenate((u_h, u_h), axis=1)
        total = ds[...]
        for j in (0, 1):
            d_h, d_l = only(low if j == 0 else ~low, (dyb[0, :, sl], dyb[1, :, sl]))
            pairs = mm(jnp.concatenate((d_h, d_l), axis=1), twice, 1, 1) + mm(d_h, u_l, 1, 1)
            total = total + ls[2 * hp + j] * pairs
        ds[...] = total
        return carry

    lax.fori_loop(0, HEADS // 2, within_back, 0)
    for part in range(PARTS):
        gr_.turn(part)
        gc_.turn(part)
    ds[...] = jnp.zeros((T, T), F32)
    lax.fori_loop(0, HEADS // 2, scores_back, 0)
    head = u < STATE
    d_s = split(ds[...], 2)
    dce[...] = (
        jnp.where(line_r, mm3(both(edr), split(res[0], 2), 1, 1), 0.0)
        + jnp.where(line_c, mm3(both(edc), split(res[1], 2), 1, 1), 0.0)
        + jnp.where(head, mm3(d_s, both(bt)), 0.0)
    )
    dbe[...] = jnp.where(head, mm3(d_s, both(ct), 0, 0), 0.0)
    lo[...] = mm(nb[...], wo[...]).astype(BF16)
    gr_.finish()
    g_r = split(res[2], 2)
    car[...] = mm3(only(line_r, bt), g_r)
    dbe[...] = dbe[...] + jnp.where(line_r, mm3(both(wur), g_r, 1, 1), 0.0)
    gc_.finish()
    early.step(0)
    g_c = split(res[3], 2)
    cac[...] = mm3(only(line_c, bt), g_c)
    dbe[...] = dbe[...] + jnp.where(line_c, mm3(both(wuc), g_c, 1, 1), 0.0)

    def last(sl, i, carry):
        x_, se = x[sl], stepe[sl]
        u_ = se * x_
        v_r, v_c = wr[sl] * car[sl], wc[sl] * cac[sl]
        w_r, w_c = yr[sl], yc[sl]
        qr[sl] = qr[sl] - u_ * (v_r + w_r)
        qc[sl] = qc[sl] - u_ * (v_c + w_c)
        d_u = (w_r + w_c) + (v_r + v_c)
        dux[sl] = d_u * x_
        dxb[sl] = (se * d_u + skipe * dy[sl]).astype(BF16)
        res[0, sl] = res[2, sl] * (own[0, sl] + dr[sl] * res[0, sl])
        res[1, sl] = res[3, sl] * (own[1, sl] + dc[sl] * res[1, sl])
        return carry

    loop(T, last)
    lg = mm(tok[...], dxb[...], 0, 0) * factor
    for j in range(4):
        lbuf[LROW[j] : LROW[j] + 256] = lg[:, j * 128 : (j + 1) * 128]
    d_a = (
        pick(ind(same_r & (u >= t)), head_sum(qr[...]))
        + pick(ind(same_c & (u >= t)), head_sum(qc[...]))
        + pick(ind(line_r), head_sum(res[0]))
        + pick(ind(line_c), head_sum(res[1]))
    )
    d_step = head_sum(dux[...]) - vecs[1:2, :] * d_a
    d_raw = d_step * sig[...]
    r, c = grid2(T, 128)
    d_ssm = (
        spread(dbe[...], ind(c == lo4(r)))
        + spread(dce[...], ind(c == 16 + lo4(r)))
        + spread(d_raw, ind(grid2(128, 128)[1] == 32 + grid2(128, 128)[0]), 3)
    )
    d_ssm = d_ssm.astype(BF16)
    lg = mm(d_ssm, tok[...], 0, 0) * factor
    for j in range(2):
        lbuf[SROW[j] : SROW[j] + 128] = lg[:, j * 128 : (j + 1) * 128]
    total_of = lambda v: jnp.sum(v, axis=0, keepdims=True)
    sum_gain = total_of(sum_gain) * factor
    for j in range(4):
        lbuf[VROW + j : VROW + j + 1] = sum_gain[:, j * 128 : (j + 1) * 128]
    lbuf[VROW + 4 : VROW + 5] = total_of(d_raw) * factor
    lbuf[VROW + 5 : VROW + 6] = -total_of(step[...] * d_a) * factor
    lbuf[VROW + 6 : VROW + 7] = total_of(head_sum(sum_skip)) * factor
    late.start(0)
    early.step(1)
    back = mm(dxb[...], wi[:, 0:E], 1, 1)
    late.step(0)
    back = back + mm(dzb[...], wi[:, E : 2 * E], 1, 1)
    back = back + mm(d_ssm, wpad[...], 1, 1)
    gt[...] = back.astype(BF16)
    early.step(2)
    late.step(1)
    early.step(3)
    late.step(2)
    early.step(4)
    late.step(3)
    early.step(5)
    for who in (fr, fc, gr_, gc_):
        who.drain()
    for copy in ends:
        copy.wait_send()
    late.step(4)
    early.finish(6)
    late.step(5)
    late.step(6)


def unpack(eres, lres, lo_in, gt_in, lo, gt, gi, gs, go, gb, gr, gk, gg):
    lo[...] = lo_in[...]
    gt[...] = gt_in[...]
    for j in range(4):
        gi[:, j * 128 : (j + 1) * 128] = lres[LROW[j] : LROW[j] + 256]
        gi[:, E + j * 128 : E + (j + 1) * 128] = eres[j * 256 : (j + 1) * 256]
        gg[:, j * 128 : (j + 1) * 128] = lres[VROW + j : VROW + j + 1]
    for j in range(2):
        go[:, j * 128 : (j + 1) * 128] = eres[1024 + j * 512 : 1024 + (j + 1) * 512]
        gs[:, j * 128 : (j + 1) * 128] = lres[SROW[j] : SROW[j] + 40]
    gb[...] = lres[VROW + 4 : VROW + 5, 0:HEADS]
    gr[...] = lres[VROW + 5 : VROW + 6, 0:HEADS]
    gk[...] = lres[VROW + 6 : VROW + 7, 0:HEADS]


def local(tokens_in, out_cotangent, w_inner, w_ssm, dt_bias, decay_rate, skip_gain, norm_gain, w_out):
    devices = lax.axis_size("slide") * lax.axis_size("row") * lax.axis_size("col")
    factor = float(devices * T) ** -0.5
    shape = jax.ShapeDtypeStruct
    vmem = pl.BlockSpec(memory_space=pltpu.VMEM)
    lo, gt, eres, lres = pl.pallas_call(
        functools.partial(kernel, factor),
        out_shape=(shape((T, D), BF16), shape((T, D), BF16), shape((EARLY, 128), F32), shape((LATE, 128), F32)),
        in_specs=[pl.BlockSpec(memory_space=pltpu.HBM)] * 9,
        out_specs=(vmem,) * 4,
        scratch_shapes=[kind for _, kind in SCRATCH],
        compiler_params=pltpu.CompilerParams(
            collective_id=0, has_side_effects=True, vmem_limit_bytes=48 * 2**20
        ),
    )(
        *[
            pltpu.with_memory_space_constraint(array, pltpu.HBM)
            for array in (
                tokens_in.reshape(T, D),
                out_cotangent.reshape(T, D),
                w_inner,
                w_ssm.T,
                dt_bias.reshape(1, -1),
                decay_rate.reshape(1, -1),
                skip_gain.reshape(1, -1),
                norm_gain.reshape(1, -1),
                w_out,
            )
        ]
    )
    out = pl.pallas_call(
        unpack,
        out_shape=(
            shape((T, D), BF16),
            shape((T, D), BF16),
            shape(w_inner.shape, F32),
            shape(w_ssm.shape[::-1], F32),
            shape(w_out.shape, F32),
            shape((1, HEADS), F32),
            shape((1, HEADS), F32),
            shape((1, HEADS), F32),
            shape((1, E), F32),
        ),
        in_specs=[vmem] * 4,
        out_specs=(vmem,) * 9,
        compiler_params=pltpu.CompilerParams(vmem_limit_bytes=6 * 2**20),
    )(eres, lres, lo, gt)
    return (
        out[0].reshape(tokens_in.shape),
        out[1].reshape(tokens_in.shape),
        out[2],
        out[3].T,
        out[4],
        out[5].reshape(-1),
        out[6].reshape(-1),
        out[7].reshape(-1),
        out[8].reshape(-1),
    )


def solution(mesh):
    tiles = P("slide", "row", "col", None)
    return jax.shard_map(
        local,
        mesh=mesh,
        in_specs=(tiles, tiles) + (P(),) * 7,
        out_specs=(tiles, tiles) + (P(),) * 7,
        check_vma=False,
    )
```

```python
import functools

import jax
import jax.numpy as jnp
from jax import lax
from jax.experimental import pallas as pl
from jax.experimental.pallas import tpu as pltpu
from jax.sharding import PartitionSpec as P

MESH = pl.DeviceIdType.MESH
F32 = jnp.float32
BF16 = jnp.bfloat16
HEADS = 8
HDIM = 64
STATE = 16
SIDE = 16
T = SIDE * SIDE
E = HEADS * HDIM
D = 256
TILES = 8
SHARE = T // TILES
PARTS = SHARE // STATE
ORDER = (4, 3, 5, 2, 6, 1, 7)
NEG = -1e30
EARLY = 2048
LATE = 1280
LROW = (0, 256, 640, 896)
SROW = (512, 1152)
VROW = 512 + 64


def mm(a, b, ca=1, cb=0):
    return lax.dot_general(a, b, (((ca,), (cb,)), ((), ())), preferred_element_type=F32)


def split(x, terms):
    out = []
    for _ in range(terms - 1):
        hi = x.astype(BF16)
        out.append(hi)
        x = x - hi.astype(F32)
    out.append(x.astype(BF16))
    return out


def pick(mask, x, terms=3):
    return functools.reduce(lambda u, v: u + v, [mm(mask, part) for part in split(x, terms)])


def spread(x, mask, terms=2):
    return functools.reduce(lambda u, v: u + v, [mm(part, mask) for part in split(x, terms)])


def mm3(a, b, ca=1, cb=0):
    (ah, al), (bh, bl) = a, b
    return mm(ah, bh, ca, cb) + (mm(ah, bl, ca, cb) + mm(al, bh, ca, cb))


def keep(pair, where, x):
    hi, lo = split(x, 2)
    pair[(0,) + where] = hi
    pair[(1,) + where] = lo


def both(pair):
    return pair[0], pair[1]


def only(mask, pair):
    nil = jnp.zeros(mask.shape, BF16)
    return jnp.where(mask, pair[0], nil), jnp.where(mask, pair[1], nil)


def ind(cond):
    return jnp.where(cond, 1.0, 0.0).astype(BF16)


def grid2(rows, cols):
    return (
        lax.broadcasted_iota(jnp.int32, (rows, cols), 0),
        lax.broadcasted_iota(jnp.int32, (rows, cols), 1),
    )


def hi4(x):
    return lax.shift_right_logical(x, 4)


def lo4(x):
    return jnp.bitwise_and(x, 15)


def head_spread():
    r, c = grid2(128, E)
    return ind(r == lax.shift_right_logical(c, 6))


def head_sum(x):
    r, c = grid2(E, 128)
    return spread(x, ind(lax.shift_right_logical(r, 6) == c), 2)


def place():
    row, col, slide = lax.axis_index("row"), lax.axis_index("col"), lax.axis_index("slide")
    return dict(y=row // 2, xh=lax.rem(row, 2), z=col // 2, co=lax.rem(col, 2), xl=slide)


def at(pos, **change):
    p = dict(pos, **change)
    return (p["y"] * 2 + p["xh"], p["z"] * 2 + p["co"], p["xl"])


def flip(bit, by):
    return bit + by * (1 - 2 * bit)


def peers(pos, axis):
    out = []
    for d in (1, 2, 3):
        if axis == "x":
            out.append(at(pos, xh=flip(pos["xh"], d // 2), xl=flip(pos["xl"], d % 2)))
        else:
            out.append(at(pos, **{axis: xor4(pos[axis], d)}))
    return out


def xor4(q, d):
    return 2 * flip(q // 2, d // 2) + flip(lax.rem(q, 2), d % 2)


def remote(src, dst, ssem, rsem, to):
    return pltpu.make_async_remote_copy(
        src_ref=src, dst_ref=dst, send_sem=ssem, recv_sem=rsem, device_id=to, device_id_type=MESH
    )


class Scan:
    def __init__(self, pos, axis, back, own, got, out, res, dec, ssem, rsem, slot):
        self.me = lax.axis_index("col" if axis == "r" else "row")
        self.pos, self.axis, self.back = pos, axis, back
        self.head, self.last = (TILES - 1, 0) if back else (0, TILES - 1)
        self.own, self.got, self.out, self.res, self.dec = own, got, out, res, dec
        self.ssem, self.rsem, self.slot = ssem, rsem, slot

    def peer(self, d):
        k = lax.rem(self.me + d, TILES)
        if self.axis == "r":
            return k, (lax.axis_index("row"), k, self.pos["xl"])
        return k, (k, lax.axis_index("col"), self.pos["xl"])

    def lines(self, k, part):
        return pl.ds(pl.multiple_of(k * SHARE + part * STATE, STATE), STATE)

    def copies(self, stage, part):
        out, piece = [], pl.ds(part * STATE, STATE)
        for d in ORDER:
            k, to = self.peer(d)
            sems = self.ssem.at[self.slot, stage, part, d], self.rsem.at[self.slot, stage, part, d]
            if stage == 0:
                out.append(remote(self.own.at[self.lines(k, part)], self.got.at[self.me, piece], *sems, to))
            else:
                out.append(remote(self.out.at[k, piece], self.res.at[self.lines(self.me, part)], *sems, to))
        return out

    def start(self, part):
        @pl.when(self.me != self.last)
        def _():
            for copy in self.copies(0, part):
                copy.start()

        self.got[self.me, pl.ds(part * STATE, STATE)] = self.own[self.lines(self.me, part)]

    def turn(self, part):
        for d, copy in zip(ORDER, self.copies(0, part)):
            pl.when(lax.rem(self.me - d + TILES, TILES) != self.last)(copy.wait_recv)
        state, piece = jnp.zeros((STATE, E), F32), pl.ds(part * STATE, STATE)
        for j in range(TILES - 1, -1, -1) if self.back else range(TILES):
            self.out[j, piece] = state
            if j != self.last:
                state = self.dec[pl.ds(j * SHARE + part * STATE, STATE)] * state + self.got[j, piece]
        for d, copy in zip(ORDER, self.copies(1, part)):
            pl.when(self.peer(d)[0] != self.head)(copy.start)

    def finish(self):
        @pl.when(self.me == self.head)
        def _():
            self.res[...] = jnp.zeros((T, E), F32)

        @pl.when(self.me != self.head)
        def _():
            for part in range(PARTS):
                self.res[self.lines(self.me, part)] = self.out[self.me, pl.ds(part * STATE, STATE)]
                for copy in self.copies(1, part):
                    copy.wait_recv()

    def drain(self):
        for part in range(PARTS):
            @pl.when(self.me != self.last)
            def _():
                for copy in self.copies(0, part):
                    copy.wait_send()

            for d, copy in zip(ORDER, self.copies(1, part)):
                pl.when(self.peer(d)[0] != self.head)(copy.wait_send)


class Total:
    def __init__(self, pos, buf, out, cbuf, xbuf, ybuf, zbuf, ssem, rsem, cuts):
        n = buf.shape[0]
        self.cuts = cuts
        self.pos, self.buf, self.out = pos, buf, out
        self.cbuf, self.xbuf, self.ybuf, self.zbuf = cbuf, xbuf, ybuf, zbuf
        self.ssem, self.rsem = ssem, rsem
        self.nh = n // 2
        self.base = pos["co"] * self.nh
        self.other = at(pos, co=1 - pos["co"])
        index = {"x": pos["xh"] * 2 + pos["xl"], "y": pos["y"], "z": pos["z"]}
        third = -(-self.nh // 384) * 128
        sizes = (third, third, self.nh - 2 * third)
        self.parts, offset = [], 0
        for size, order in zip(sizes, ("xyz", "yzx", "zxy")):
            start = self.base + offset
            first = start + index[order[0]] * (size // 4)
            second = first + index[order[1]] * (size // 16)
            self.parts.append((order, index[order[0]], index[order[1]], size, offset, start, first, second))
            offset += size

    def rows(self, start, size):
        return pl.ds(pl.multiple_of(start, 8), size)

    def copies(self, stage):
        pos = self.pos
        if stage == 0:
            out, offset = [], 0
            for k, size in enumerate(self.cuts):
                src = self.buf.at[self.rows((1 - pos["co"]) * self.nh + offset, size)]
                sems = self.ssem.at[0, k], self.rsem.at[0, k]
                out.append(remote(src, self.cbuf.at[pl.ds(offset, size)], *sems, self.other))
                offset += size
            return out
        if stage == 6:
            own = self.out.at[self.rows(self.base, self.nh)]
            return [remote(own, own, self.ssem.at[6, 0], self.rsem.at[6, 0], self.other)]
        out = []
        for p, (order, g0, g1, size, offset, start, first, second) in enumerate(self.parts):
            n0, n1 = size // 4, size // 16
            axis = order[(0, 1, 2, 1, 0)[stage - 1]]
            for d, to in enumerate(peers(pos, axis)):
                if stage == 1:
                    src = self.buf.at[self.rows(start + xor4(g0, d + 1) * n0, n0)]
                    dst = self.xbuf.at[d, pl.ds(offset // 4, n0)]
                elif stage == 2:
                    src = self.buf.at[self.rows(first + xor4(g1, d + 1) * n1, n1)]
                    dst = self.ybuf.at[d, pl.ds(offset // 16, n1)]
                elif stage == 3:
                    src, dst = self.buf.at[self.rows(second, n1)], self.zbuf.at[d, pl.ds(offset // 16, n1)]
                elif stage == 4:
                    src = dst = self.out.at[self.rows(second, n1)]
                else:
                    src = dst = self.out.at[self.rows(first, n0)]
                k = 3 * p + d
                out.append(remote(src, dst, self.ssem.at[stage, k], self.rsem.at[stage, k], to))
        return out

    def start(self, stage):
        for copy in self.copies(stage):
            copy.start()

    def finish(self, stage):
        for copy in self.copies(stage):
            copy.wait()
        if stage == 0:
            sl = self.rows(self.base, self.nh)
            self.buf[sl] = self.buf[sl] + self.cbuf[...]
        if stage not in (1, 2, 3):
            return
        came = (self.xbuf, self.ybuf, self.zbuf)[stage - 1]
        to = self.out if stage == 3 else self.buf
        for order, g0, g1, size, offset, start, first, second in self.parts:
            share = 4 if stage == 1 else 16
            sl = self.rows(first if stage == 1 else second, size // share)
            at_ = pl.ds(offset // share, size // share)
            to[sl] = (self.buf[sl] + came[0, at_]) + (came[1, at_] + came[2, at_])

    def step(self, stage):
        self.finish(stage)
        if stage < 6:
            self.start(stage + 1)


def kernel(factor, *refs):
    names_in = ["tok", "cot", "wi", "ws", "bias", "rate", "skip", "gain", "wo"]
    names_in = [name + "_h" for name in names_in]
    names_out = ["lo", "gt", "eres", "lres"]
    n_io = len(names_in) + len(names_out)
    k = dict(zip(names_in + names_out, refs[:n_io]))
    k.update(zip([name for name, _ in SCRATCH], refs[n_io:]))
    body(factor, **k)


def vm(*shape, dtype=F32):
    return pltpu.VMEM(shape, dtype)


BIG = (T, E)
SCRATCH = [
    ("x", vm(*BIG)), ("z", vm(*BIG)), ("ub", vm(2, *BIG, dtype=BF16)), ("stepe", vm(*BIG)),
    ("bt", vm(2, T, T, dtype=BF16)), ("ct", vm(2, T, T, dtype=BF16)), ("s", vm(T, T)), ("ds", vm(T, T)),
    ("wsel", vm(D, 640, dtype=BF16)), ("wpad", vm(D, 128, dtype=BF16)), ("vecs", vm(8, 128)),
    ("step", vm(T, 128)), ("sig", vm(T, 128)),
    ("cumr", vm(T, 128)), ("cumc", vm(T, 128)), ("cumrt", vm(128, T)), ("cumct", vm(128, T)),
    ("er", vm(*BIG)), ("ec", vm(*BIG)), ("wr", vm(*BIG)), ("wc", vm(*BIG)), ("dr", vm(*BIG)), ("dc", vm(*BIG)),
    ("dxr", vm(*BIG)), ("dxc", vm(*BIG)),
    ("finr", vm(SIDE, 128)), ("finc", vm(SIDE, 128)), ("allr", vm(128, 128)), ("allc", vm(128, 128)),
    ("wur", vm(2, *BIG, dtype=BF16)), ("wuc", vm(2, *BIG, dtype=BF16)),
    ("edr", vm(2, *BIG, dtype=BF16)), ("edc", vm(2, *BIG, dtype=BF16)),
    ("mr", vm(2, HEADS, T, T, dtype=BF16)), ("mc", vm(2, HEADS, T, T, dtype=BF16)), ("ls", vm(HEADS, T, T)),
    ("yr", vm(*BIG)), ("yc", vm(*BIG)), ("car", vm(*BIG)), ("cac", vm(*BIG)), ("dn", vm(*BIG)),
    ("dy", vm(*BIG)), ("dyb", vm(2, *BIG, dtype=BF16)), ("dzb", vm(*BIG, dtype=BF16)), ("nb", vm(*BIG, dtype=BF16)),
    ("qr", vm(*BIG)), ("qc", vm(*BIG)), ("dxb", vm(*BIG, dtype=BF16)), ("act", vm(*BIG)), ("hd", vm(T, 128)), ("dux", vm(*BIG)),
    ("dbe", vm(T, T)), ("dce", vm(T, T)),
    ("own", pltpu.VMEM((4, T, E), F32)), ("got", pltpu.VMEM((4, TILES, SHARE, E), F32)),
    ("out", pltpu.VMEM((4, TILES, SHARE, E), F32)), ("res", pltpu.VMEM((4, T, E), F32)),
    ("ebuf", vm(EARLY, 128)), ("ecb", vm(EARLY // 2, 128)), ("exb", vm(3, EARLY // 8, 128)),
    ("eyb", vm(3, EARLY // 32, 128)), ("ezb", vm(3, EARLY // 32, 128)),
    ("lbuf", vm(LATE, 128)), ("lcb", vm(LATE // 2, 128)), ("lxb", vm(3, LATE // 8, 128)),
    ("lyb", vm(3, LATE // 32, 128)), ("lzb", vm(3, LATE // 32, 128)),
    ("fsem", pltpu.SemaphoreType.DMA((2, 2, TILES))),
    ("cs", pltpu.SemaphoreType.DMA((4, 2, PARTS, TILES))), ("cr", pltpu.SemaphoreType.DMA((4, 2, PARTS, TILES))),
    ("es", pltpu.SemaphoreType.DMA((7, 9))), ("erv", pltpu.SemaphoreType.DMA((7, 9))),
    ("lsm", pltpu.SemaphoreType.DMA((7, 9))), ("lrv", pltpu.SemaphoreType.DMA((7, 9))),
]
SCRATCH += [
    ("tok", vm(T, D, dtype=BF16)), ("cot", vm(T, D, dtype=BF16)), ("wi", vm(D, 2 * E, dtype=BF16)),
    ("ws", vm(2 * STATE + HEADS, D, dtype=BF16)), ("bias", vm(1, HEADS)), ("rate", vm(1, HEADS)),
    ("skip", vm(1, HEADS)), ("gain", vm(1, E)), ("wo", vm(E, D, dtype=BF16)),
    ("isem", pltpu.SemaphoreType.DMA((9,))),
]
RB = 32


def loop(rows, fn, init=0):
    def step(i, carry):
        return fn(pl.ds(pl.multiple_of(i * RB, RB), RB), i, carry)

    return lax.fori_loop(0, rows // RB, step, init)


def body(factor, tok_h, cot_h, wi_h, ws_h, bias_h, rate_h, skip_h, gain_h, wo_h, lo, gt, eres, lres,
         x, z, ub, stepe, bt, ct, s, ds, wsel, wpad, vecs, step, sig, cumr, cumc, cumrt, cumct,
         er, ec, wr, wc, dr, dc, dxr, dxc, finr, finc, allr, allc, wur, wuc, edr, edc, mr, mc, ls,
         yr, yc, car, cac, dn, dy, dyb, dzb, nb, qr, qc, dxb, act, hd, dux, dbe, dce,
         own, got, out, res, ebuf, ecb, exb, eyb, ezb, lbuf, lcb, lxb, lyb, lzb,
         fsem, cs, cr, es, erv, lsm, lrv, tok, cot, wi, ws, bias, rate, skip, gain, wo, isem):
    pos = place()
    given = (ws_h, ws), (bias_h, bias), (rate_h, rate), (skip_h, skip), (tok_h, tok), (wi_h, wi), (cot_h, cot), (wo_h, wo), (gain_h, gain)
    fetch = [pltpu.make_async_copy(src, dst, isem.at[j]) for j, (src, dst) in enumerate(given)]
    for copy in fetch:
        copy.start()
    barrier = pltpu.get_barrier_semaphore()

    def scan(slot, axis, back):
        return Scan(pos, axis, back, own.at[slot], got.at[slot], out.at[slot], res.at[slot], (dxr, dxc)[slot % 2],
                    cs, cr, slot)

    fr, fc, gr_, gc_ = scan(0, "r", False), scan(1, "c", False), scan(2, "r", True), scan(3, "c", True)
    near = [who.peer(d)[1] for who in (fr, fc) for d in range(1, TILES)]
    near += [at(pos, xl=1 - pos["xl"]), at(pos, xl=1 - pos["xl"], xh=1 - pos["xh"])]
    for to in near:
        pl.semaphore_signal(barrier, inc=1, device_id=to, device_id_type=MESH)
    early = Total(pos, ebuf, eres, ecb, exb, eyb, ezb, es, erv, (EARLY // 2,))
    late = Total(pos, lbuf, lres, lcb, lxb, lyb, lzb, lsm, lrv, (512, 128))

    for copy in fetch[:5]:
        copy.wait()
    r, c = grid2(2 * STATE + HEADS, 640)
    sel = ((c < 256) & (r == lo4(c))) | ((c >= 256) & (c < 512) & (r == 16 + lo4(c))) | ((c >= 512) & (r == c - 480))
    wsel[...] = mm(ws[...], ind(sel), 0, 0).astype(BF16)
    r, c = grid2(2 * STATE + HEADS, 128)
    wpad[...] = mm(ws[...], ind(r == c), 0, 0).astype(BF16)
    vecs[...] = jnp.zeros((8, 128), F32)
    vecs[0:1, 0:HEADS] = bias[...]
    vecs[1:2, 0:HEADS] = rate[...]
    vecs[2:3, 0:HEADS] = skip[...]
    raw = mm(tok[...], wsel[:, 512:640]) + vecs[0:1, :]
    tail = jnp.exp(-jnp.abs(raw))
    stp = jnp.maximum(raw, 0.0) + jnp.log1p(tail)
    step[...] = stp
    sig[...] = jnp.where(raw >= 0, 1.0, tail) / (1.0 + tail)
    a = -stp * vecs[1:2, :]
    t, u = grid2(T, T)
    same_r, same_c = hi4(t) == hi4(u), lo4(t) == lo4(u)
    aft_r = pick(ind(same_r & (u > t)), a)
    aft_c = pick(ind(same_c & (u > t)), a)
    r, c = grid2(SIDE, T)
    finr[...] = jnp.exp(pick(ind(r == hi4(c)), a))
    finc[...] = jnp.exp(pick(ind(r == lo4(c)), a))
    hx = head_spread()
    stepe[...] = spread(stp, hx, 3)
    wr[...] = spread(jnp.exp(aft_r), hx)
    wc[...] = spread(jnp.exp(aft_c), hx)
    fetch[5].wait()
    x[...] = mm(tok[...], wi[:, 0:E])
    keep(bt, (), mm(tok[...], wsel[:, 0:256]))

    def drive(sl, i, carry):
        u_ = stepe[sl] * x[sl]
        keep(ub, (sl,), u_)
        keep(wur, (sl,), wr[sl] * u_)
        keep(wuc, (sl,), wc[sl] * u_)
        return carry

    loop(T, drive)
    line_r, line_c = hi4(t) == hi4(u), lo4(t) == hi4(u)
    own[1] = mm3(only(line_c, bt), both(wuc), 0, 0)
    own[0] = mm3(only(line_r, bt), both(wur), 0, 0)
    pl.semaphore_wait(barrier, len(near))
    ends = []
    for a_, (who, mine, all_) in enumerate(((fc, finc, allc), (fr, finr, allr))):
        place_ = pl.ds(pl.multiple_of(who.me * SIDE, SIDE), SIDE)
        all_[place_] = mine[...]
        for d in range(1, TILES):
            ends.append(remote(mine, all_.at[place_], fsem.at[a_, 0, d], fsem.at[a_, 1, d], who.peer(d)[1]))
            ends[-1].start()
    for part in range(PARTS):
        fc.start(part)
        fr.start(part)

    cumr[...] = pick(ind(same_r & (u <= t)), a)
    cumc[...] = pick(ind(same_c & (u <= t)), a)

    def lines(rows, first, ends):
        k, l = grid2(rows, SIDE)
        return pick(ind(hi4(k) + first == l), spread(ends, hx), 2)

    dr[...] = lines(T, 0, finr[...])
    dc[...] = lines(T, 0, finc[...])

    z[...] = mm(tok[...], wi[:, E : 2 * E])
    keep(ct, (), mm(tok[...], wsel[:, 256:512]))
    s[...] = mm3(both(ct), both(bt), 1, 1) * (1.0 / 16.0)
    er[...] = spread(jnp.exp(cumr[...]), hx)
    ec[...] = spread(jnp.exp(cumc[...]), hx)
    cumrt[...] = cumr[...].T
    cumct[...] = cumc[...].T

    def masks(sl, i, carry):
        t_, u_ = grid2(RB, T)
        t_ = t_ + i * RB
        in_r = (hi4(t_) == hi4(u_)) & (u_ <= t_)
        in_c = (lo4(t_) == lo4(u_)) & (u_ <= t_)
        s_ = s[sl]
        c_r, c_c = cumr[sl], cumc[sl]
        for h in range(HEADS):
            l_r = jnp.exp(jnp.where(in_r, c_r[:, h : h + 1] - cumrt[h : h + 1, :], NEG))
            l_c = jnp.exp(jnp.where(in_c, c_c[:, h : h + 1] - cumct[h : h + 1, :], NEG))
            keep(mr, (h, sl), l_r * s_)
            keep(mc, (h, sl), l_c * s_)
            ls[h, sl] = l_r + l_c
        return carry

    loop(T, masks)
    low = lax.broadcasted_iota(jnp.int32, (T, 128), 1) < HDIM

    def heads(m, hp, pair, dim):
        wide = jnp.concatenate(pair, axis=1)
        part = []
        for h in (2 * hp, 2 * hp + 1):
            full = mm(m[0, h], wide, dim, 0)
            part.append(full[:, :128] + full[:, 128:] + mm(m[1, h], pair[0], dim, 0))
        return jnp.where(low, part[0], part[1])

    def within(hp, carry):
        sl = pl.ds(pl.multiple_of(hp * 128, 128), 128)
        u_ = (ub[0, :, sl], ub[1, :, sl])
        yr[:, sl] = heads(mr, hp, u_, 1)
        yc[:, sl] = heads(mc, hp, u_, 1)
        return carry

    for copy in fetch[6:]:
        copy.wait()

    for copy in ends:
        copy.wait_recv()
    k, l = grid2(T, 128)
    line = lax.shift_right_logical(k, 5) * SIDE + jnp.bitwise_and(hi4(k), 1)
    for who, all_ in ((fr, allr), (fc, allc)):
        who.dec[...] = spread(pick(ind(l == line + 2 * who.me), all_[...], 2), hx)
    for part in range(PARTS):
        fr.turn(part)
        fc.turn(part)
    lax.fori_loop(0, HEADS // 2, within, 0)
    dn[...] = mm(cot[...], wo[...], 1, 1)

    def gate(sl, i, carry):
        z_ = z[sl]
        sg = 1.0 / (1.0 + jnp.exp(-z_))
        act[sl] = z_ * sg
        z[sl] = sg * (1.0 + z_ * (1.0 - sg))
        return carry

    loop(T, gate)
    fr.finish()
    car[...] = mm3(only(line_r, ct), split(res[0], 2))
    fc.finish()
    cac[...] = mm3(only(line_c, ct), split(res[1], 2))

    skipe = spread(vecs[...], hx, 3)[2:3, :]
    gain_ = gain[...]

    def middle(sl, i, carry):
        sum_gain, sum_skip = carry
        x_, act_ = x[sl], act[sl]
        c_r, c_c = er[sl] * car[sl], ec[sl] * cac[sl]
        w_r, w_c = yr[sl], yc[sl]
        y = (w_r + w_c) + (c_r + c_c) + skipe * x_
        gated = y * act_
        inv = lax.rsqrt(jnp.mean(gated * gated, axis=-1, keepdims=True) + 1e-05)
        unit = gated * inv
        nb[sl] = (unit * gain_).astype(BF16)
        d_n = dn[sl]
        g1 = d_n * gain_
        dg = inv * (g1 - unit * jnp.mean(g1 * unit, axis=-1, keepdims=True))
        d_y = dg * act_
        dzb[sl] = (dg * y * z[sl]).astype(BF16)
        dy[sl] = d_y
        keep(dyb, (sl,), d_y)
        keep(edr, (sl,), er[sl] * d_y)
        keep(edc, (sl,), ec[sl] * d_y)
        qr[sl] = d_y * (c_r + w_r)
        qc[sl] = d_y * (c_c + w_c)
        fold = lambda v: functools.reduce(lambda p, q: p + q, [v[8 * j : 8 * j + 8] for j in range(RB // 8)])
        return sum_gain + fold(d_n * unit), sum_skip + fold(d_y * x_)

    nil = jnp.zeros((8, E), F32)
    sum_gain, sum_skip = loop(T, middle, (nil, nil))
    own[3] = mm3(only(line_c, ct), both(edc), 0, 0)
    for part in range(PARTS):
        gc_.start(part)
    own[2] = mm3(only(line_r, ct), both(edr), 0, 0)
    for part in range(PARTS):
        gr_.start(part)

    lg = mm(tok[...], dzb[...], 0, 0) * factor
    for j in range(4):
        ebuf[j * 256 : (j + 1) * 256] = lg[:, j * 128 : (j + 1) * 128]
    lg = mm(nb[...], cot[...], 0, 0) * factor
    for j in range(2):
        ebuf[1024 + j * 512 : 1024 + (j + 1) * 512] = lg[:, j * 128 : (j + 1) * 128]
    early.start(0)
    def within_back(hp, carry):
        sl = pl.ds(pl.multiple_of(hp * 128, 128), 128)
        d_ = (dyb[0, :, sl], dyb[1, :, sl])
        yr[:, sl] = heads(mr, hp, d_, 0)
        yc[:, sl] = heads(mc, hp, d_, 0)
        return carry


    def scores_back(hp, carry):
        sl = pl.ds(pl.multiple_of(hp * 128, 128), 128)
        u_h, u_l = ub[0, :, sl], ub[1, :, sl]
        twice = jnp.concatenate((u_h, u_h), axis=1)
        total = ds[...]
        for j in (0, 1):
            d_h, d_l = only(low if j == 0 else ~low, (dyb[0, :, sl], dyb[1, :, sl]))
            pairs = mm(jnp.concatenate((d_h, d_l), axis=1), twice, 1, 1) + mm(d_h, u_l, 1, 1)
            total = total + ls[2 * hp + j] * pairs
        ds[...] = total
        return carry

    lax.fori_loop(0, HEADS // 2, within_back, 0)
    for part in range(PARTS):
        gr_.turn(part)
        gc_.turn(part)
    ds[...] = jnp.zeros((T, T), F32)
    lax.fori_loop(0, HEADS // 2, scores_back, 0)
    head = u < STATE
    d_s = split(ds[...], 2)
    dce[...] = (
        jnp.where(line_r, mm3(both(edr), split(res[0], 2), 1, 1), 0.0)
        + jnp.where(line_c, mm3(both(edc), split(res[1], 2), 1, 1), 0.0)
        + jnp.where(head, mm3(d_s, both(bt)), 0.0)
    )
    dbe[...] = jnp.where(head, mm3(d_s, both(ct), 0, 0), 0.0)
    lo[...] = mm(nb[...], wo[...]).astype(BF16)

    def ahead(sl, i, carry):
        x_, se = x[sl], stepe[sl]
        u_ = se * x_
        w_r, w_c = yr[sl], yc[sl]
        w_ = w_r + w_c
        qr[sl] = qr[sl] - u_ * w_r
        qc[sl] = qc[sl] - u_ * w_c
        dux[sl] = w_ * x_
        dy[sl] = se * w_ + skipe * dy[sl]
        res[0, sl] = own[0, sl] + dr[sl] * res[0, sl]
        res[1, sl] = own[1, sl] + dc[sl] * res[1, sl]
        return carry

    loop(T, ahead)
    cumr[...] = head_sum(qr[...])
    cumc[...] = head_sum(qc[...])
    hd[...] = head_sum(dux[...])
    early.step(0)
    gr_.finish()
    g_r = split(res[2], 2)
    car[...] = mm3(only(line_r, bt), g_r)
    dbe[...] = dbe[...] + jnp.where(line_r, mm3(both(wur), g_r, 1, 1), 0.0)
    gc_.finish()
    g_c = split(res[3], 2)
    cac[...] = mm3(only(line_c, bt), g_c)
    dbe[...] = dbe[...] + jnp.where(line_c, mm3(both(wuc), g_c, 1, 1), 0.0)

    def last(sl, i, carry):
        x_ = x[sl]
        v_r, v_c = wr[sl] * car[sl], wc[sl] * cac[sl]
        qr[sl] = x_ * v_r
        qc[sl] = x_ * v_c
        dxb[sl] = (dy[sl] + stepe[sl] * (v_r + v_c)).astype(BF16)
        res[0, sl] = res[2, sl] * res[0, sl]
        res[1, sl] = res[3, sl] * res[1, sl]
        return carry

    loop(T, last)
    lg = mm(tok[...], dxb[...], 0, 0) * factor
    for j in range(4):
        lbuf[LROW[j] : LROW[j] + 256] = lg[:, j * 128 : (j + 1) * 128]
    late_core = late.copies(0)
    late_core[0].start()
    h_r, h_c = head_sum(qr[...]), head_sum(qc[...])
    d_a = (
        pick(ind(same_r & (u >= t)), cumr[...] - step[...] * h_r)
        + pick(ind(same_c & (u >= t)), cumc[...] - step[...] * h_c)
        + pick(ind(line_r), head_sum(res[0]))
        + pick(ind(line_c), head_sum(res[1]))
    )
    d_step = hd[...] + (h_r + h_c) - vecs[1:2, :] * d_a
    d_raw = d_step * sig[...]
    r, c = grid2(T, 128)
    d_ssm = (
        spread(dbe[...], ind(c == lo4(r)))
        + spread(dce[...], ind(c == 16 + lo4(r)))
        + spread(d_raw, ind(grid2(128, 128)[1] == 32 + grid2(128, 128)[0]), 3)
    )
    d_ssm = d_ssm.astype(BF16)
    lg = mm(d_ssm, tok[...], 0, 0) * factor
    for j in range(2):
        lbuf[SROW[j] : SROW[j] + 128] = lg[:, j * 128 : (j + 1) * 128]
    total_of = lambda v: jnp.sum(v, axis=0, keepdims=True)
    sum_gain = total_of(sum_gain) * factor
    for j in range(4):
        lbuf[VROW + j : VROW + j + 1] = sum_gain[:, j * 128 : (j + 1) * 128]
    lbuf[VROW + 4 : VROW + 5] = total_of(d_raw) * factor
    lbuf[VROW + 5 : VROW + 6] = -total_of(step[...] * d_a) * factor
    lbuf[VROW + 6 : VROW + 7] = total_of(head_sum(sum_skip)) * factor
    late_core[1].start()
    early.step(1)
    back = mm(dxb[...], wi[:, 0:E], 1, 1)
    late.step(0)
    back = back + mm(dzb[...], wi[:, E : 2 * E], 1, 1)
    back = back + mm(d_ssm, wpad[...], 1, 1)
    gt[...] = back.astype(BF16)
    early.step(2)
    late.step(1)
    early.step(3)
    late.step(2)
    early.step(4)
    late.step(3)
    early.step(5)
    for who in (fr, fc, gr_, gc_):
        who.drain()
    for copy in ends:
        copy.wait_send()
    late.step(4)
    early.finish(6)
    late.step(5)
    late.step(6)


def unpack(eres, lres, lo_in, gt_in, lo, gt, gi, gs, go, gb, gr, gk, gg):
    lo[...] = lo_in[...]
    gt[...] = gt_in[...]
    for j in range(4):
        gi[:, j * 128 : (j + 1) * 128] = lres[LROW[j] : LROW[j] + 256]
        gi[:, E + j * 128 : E + (j + 1) * 128] = eres[j * 256 : (j + 1) * 256]
        gg[:, j * 128 : (j + 1) * 128] = lres[VROW + j : VROW + j + 1]
    for j in range(2):
        go[:, j * 128 : (j + 1) * 128] = eres[1024 + j * 512 : 1024 + (j + 1) * 512]
        gs[:, j * 128 : (j + 1) * 128] = lres[SROW[j] : SROW[j] + 40]
    gb[...] = lres[VROW + 4 : VROW + 5, 0:HEADS]
    gr[...] = lres[VROW + 5 : VROW + 6, 0:HEADS]
    gk[...] = lres[VROW + 6 : VROW + 7, 0:HEADS]


def local(tokens_in, out_cotangent, w_inner, w_ssm, dt_bias, decay_rate, skip_gain, norm_gain, w_out):
    devices = lax.axis_size("slide") * lax.axis_size("row") * lax.axis_size("col")
    factor = float(devices * T) ** -0.5
    shape = jax.ShapeDtypeStruct
    vmem = pl.BlockSpec(memory_space=pltpu.VMEM)
    lo, gt, eres, lres = pl.pallas_call(
        functools.partial(kernel, factor),
        out_shape=(shape((T, D), BF16), shape((T, D), BF16), shape((EARLY, 128), F32), shape((LATE, 128), F32)),
        in_specs=[pl.BlockSpec(memory_space=pltpu.HBM)] * 9,
        out_specs=(vmem,) * 4,
        scratch_shapes=[kind for _, kind in SCRATCH],
        compiler_params=pltpu.CompilerParams(
            collective_id=0, has_side_effects=True, vmem_limit_bytes=48 * 2**20
        ),
    )(
        *[
            pltpu.with_memory_space_constraint(array, pltpu.HBM)
            for array in (
                tokens_in.reshape(T, D),
                out_cotangent.reshape(T, D),
                w_inner,
                w_ssm.T,
                dt_bias.reshape(1, -1),
                decay_rate.reshape(1, -1),
                skip_gain.reshape(1, -1),
                norm_gain.reshape(1, -1),
                w_out,
            )
        ]
    )
    out = pl.pallas_call(
        unpack,
        out_shape=(
            shape((T, D), BF16),
            shape((T, D), BF16),
            shape(w_inner.shape, F32),
            shape(w_ssm.shape[::-1], F32),
            shape(w_out.shape, F32),
            shape((1, HEADS), F32),
            shape((1, HEADS), F32),
            shape((1, HEADS), F32),
            shape((1, E), F32),
        ),
        in_specs=[vmem] * 4,
        out_specs=(vmem,) * 9,
        compiler_params=pltpu.CompilerParams(vmem_limit_bytes=6 * 2**20),
    )(eres, lres, lo, gt)
    return (
        out[0].reshape(tokens_in.shape),
        out[1].reshape(tokens_in.shape),
        out[2],
        out[3].T,
        out[4],
        out[5].reshape(-1),
        out[6].reshape(-1),
        out[7].reshape(-1),
        out[8].reshape(-1),
    )


def solution(mesh):
    tiles = P("slide", "row", "col", None)
    return jax.shard_map(
        local,
        mesh=mesh,
        in_specs=(tiles, tiles) + (P(),) * 7,
        out_specs=(tiles, tiles) + (P(),) * 7,
        check_vma=False,
    )
```

```python
import functools

import jax
import jax.numpy as jnp
from jax import lax
from jax.experimental import pallas as pl
from jax.experimental.pallas import tpu as pltpu
from jax.sharding import PartitionSpec as P

MESH = pl.DeviceIdType.MESH
F32 = jnp.float32
BF16 = jnp.bfloat16
HEADS = 8
HDIM = 64
STATE = 16
SIDE = 16
T = SIDE * SIDE
E = HEADS * HDIM
D = 256
TILES = 8
SHARE = T // TILES
PARTS = SHARE // STATE
ORDER = (4, 3, 5, 2, 6, 1, 7)
NEG = -1e30
EARLY = 2048
LATE = 1280
LROW = (0, 256, 640, 896)
SROW = (512, 1152)
VROW = 512 + 64


def mm(a, b, ca=1, cb=0):
    return lax.dot_general(a, b, (((ca,), (cb,)), ((), ())), preferred_element_type=F32)


def split(x, terms):
    out = []
    for _ in range(terms - 1):
        hi = x.astype(BF16)
        out.append(hi)
        x = x - hi.astype(F32)
    out.append(x.astype(BF16))
    return out


def pick(mask, x, terms=3):
    return functools.reduce(lambda u, v: u + v, [mm(mask, part) for part in split(x, terms)])


def spread(x, mask, terms=2):
    return functools.reduce(lambda u, v: u + v, [mm(part, mask) for part in split(x, terms)])


def mm3(a, b, ca=1, cb=0):
    (ah, al), (bh, bl) = a, b
    return mm(ah, bh, ca, cb) + (mm(ah, bl, ca, cb) + mm(al, bh, ca, cb))


def keep(pair, where, x):
    hi, lo = split(x, 2)
    pair[(0,) + where] = hi
    pair[(1,) + where] = lo


def both(pair):
    return pair[0], pair[1]


def only(mask, pair):
    nil = jnp.zeros(mask.shape, BF16)
    return jnp.where(mask, pair[0], nil), jnp.where(mask, pair[1], nil)


def ind(cond):
    return jnp.where(cond, 1.0, 0.0).astype(BF16)


def grid2(rows, cols):
    return (
        lax.broadcasted_iota(jnp.int32, (rows, cols), 0),
        lax.broadcasted_iota(jnp.int32, (rows, cols), 1),
    )


def hi4(x):
    return lax.shift_right_logical(x, 4)


def lo4(x):
    return jnp.bitwise_and(x, 15)


def head_spread():
    r, c = grid2(128, E)
    return ind(r == lax.shift_right_logical(c, 6))


def head_sum(x):
    r, c = grid2(E, 128)
    return spread(x, ind(lax.shift_right_logical(r, 6) == c), 2)


def place():
    row, col, slide = lax.axis_index("row"), lax.axis_index("col"), lax.axis_index("slide")
    return dict(y=row // 2, xh=lax.rem(row, 2), z=col // 2, co=lax.rem(col, 2), xl=slide)


def at(pos, **change):
    p = dict(pos, **change)
    return (p["y"] * 2 + p["xh"], p["z"] * 2 + p["co"], p["xl"])


def flip(bit, by):
    return bit + by * (1 - 2 * bit)


def peers(pos, axis):
    out = []
    for d in (1, 2, 3):
        if axis == "x":
            out.append(at(pos, xh=flip(pos["xh"], d // 2), xl=flip(pos["xl"], d % 2)))
        else:
            out.append(at(pos, **{axis: xor4(pos[axis], d)}))
    return out


def xor4(q, d):
    return 2 * flip(q // 2, d // 2) + flip(lax.rem(q, 2), d % 2)


def remote(src, dst, ssem, rsem, to):
    return pltpu.make_async_remote_copy(
        src_ref=src, dst_ref=dst, send_sem=ssem, recv_sem=rsem, device_id=to, device_id_type=MESH
    )


class Scan:
    def __init__(self, pos, axis, back, own, got, out, res, dec, ssem, rsem, slot):
        self.me = lax.axis_index("col" if axis == "r" else "row")
        self.pos, self.axis, self.back = pos, axis, back
        self.head, self.last = (TILES - 1, 0) if back else (0, TILES - 1)
        self.own, self.got, self.out, self.res, self.dec = own, got, out, res, dec
        self.ssem, self.rsem, self.slot = ssem, rsem, slot

    def peer(self, d):
        k = lax.rem(self.me + d, TILES)
        if self.axis == "r":
            return k, (lax.axis_index("row"), k, self.pos["xl"])
        return k, (k, lax.axis_index("col"), self.pos["xl"])

    def lines(self, k, part):
        return pl.ds(pl.multiple_of(k * SHARE + part * STATE, STATE), STATE)

    def copies(self, stage, part):
        out, piece = [], pl.ds(part * STATE, STATE)
        for d in ORDER:
            k, to = self.peer(d)
            sems = self.ssem.at[self.slot, stage, part, d], self.rsem.at[self.slot, stage, part, d]
            if stage == 0:
                out.append(remote(self.own.at[self.lines(k, part)], self.got.at[self.me, piece], *sems, to))
            else:
                out.append(remote(self.out.at[k, piece], self.res.at[self.lines(self.me, part)], *sems, to))
        return out

    def start(self, part):
        @pl.when(self.me != self.last)
        def _():
            for copy in self.copies(0, part):
                copy.start()

        self.got[self.me, pl.ds(part * STATE, STATE)] = self.own[self.lines(self.me, part)]

    def turn(self, part):
        for d, copy in zip(ORDER, self.copies(0, part)):
            pl.when(lax.rem(self.me - d + TILES, TILES) != self.last)(copy.wait_recv)
        state, piece = jnp.zeros((STATE, E), F32), pl.ds(part * STATE, STATE)
        for j in range(TILES - 1, -1, -1) if self.back else range(TILES):
            self.out[j, piece] = state
            if j != self.last:
                state = self.dec[pl.ds(j * SHARE + part * STATE, STATE)] * state + self.got[j, piece]
        for d, copy in zip(ORDER, self.copies(1, part)):
            pl.when(self.peer(d)[0] != self.head)(copy.start)

    def finish(self):
        @pl.when(self.me == self.head)
        def _():
            self.res[...] = jnp.zeros((T, E), F32)

        @pl.when(self.me != self.head)
        def _():
            for part in range(PARTS):
                self.res[self.lines(self.me, part)] = self.out[self.me, pl.ds(part * STATE, STATE)]
                for copy in self.copies(1, part):
                    copy.wait_recv()

    def drain(self):
        for part in range(PARTS):
            @pl.when(self.me != self.last)
            def _():
                for copy in self.copies(0, part):
                    copy.wait_send()

            for d, copy in zip(ORDER, self.copies(1, part)):
                pl.when(self.peer(d)[0] != self.head)(copy.wait_send)


class Total:
    def __init__(self, pos, buf, out, cbuf, xbuf, ybuf, zbuf, ssem, rsem, cuts):
        n = buf.shape[0]
        self.cuts = cuts
        self.pos, self.buf, self.out = pos, buf, out
        self.cbuf, self.xbuf, self.ybuf, self.zbuf = cbuf, xbuf, ybuf, zbuf
        self.ssem, self.rsem = ssem, rsem
        self.nh = n // 2
        self.base = pos["co"] * self.nh
        self.other = at(pos, co=1 - pos["co"])
        index = {"x": pos["xh"] * 2 + pos["xl"], "y": pos["y"], "z": pos["z"]}
        third = -(-self.nh // 384) * 128
        sizes = (third, third, self.nh - 2 * third)
        self.parts, offset = [], 0
        for size, order in zip(sizes, ("xyz", "yzx", "zxy")):
            start = self.base + offset
            first = start + index[order[0]] * (size // 4)
            second = first + index[order[1]] * (size // 16)
            self.parts.append((order, index[order[0]], index[order[1]], size, offset, start, first, second))
            offset += size

    def rows(self, start, size):
        return pl.ds(pl.multiple_of(start, 8), size)

    def copies(self, stage):
        pos = self.pos
        if stage == 0:
            out, offset = [], 0
            for k, size in enumerate(self.cuts):
                src = self.buf.at[self.rows((1 - pos["co"]) * self.nh + offset, size)]
                sems = self.ssem.at[0, k], self.rsem.at[0, k]
                out.append(remote(src, self.cbuf.at[pl.ds(offset, size)], *sems, self.other))
                offset += size
            return out
        if stage == 6:
            own = self.out.at[self.rows(self.base, self.nh)]
            return [remote(own, own, self.ssem.at[6, 0], self.rsem.at[6, 0], self.other)]
        out = []
        for p, (order, g0, g1, size, offset, start, first, second) in enumerate(self.parts):
            n0, n1 = size // 4, size // 16
            axis = order[(0, 1, 2, 1, 0)[stage - 1]]
            for d, to in enumerate(peers(pos, axis)):
                if stage == 1:
                    src = self.buf.at[self.rows(start + xor4(g0, d + 1) * n0, n0)]
                    dst = self.xbuf.at[d, pl.ds(offset // 4, n0)]
                elif stage == 2:
                    src = self.buf.at[self.rows(first + xor4(g1, d + 1) * n1, n1)]
                    dst = self.ybuf.at[d, pl.ds(offset // 16, n1)]
                elif stage == 3:
                    src, dst = self.buf.at[self.rows(second, n1)], self.zbuf.at[d, pl.ds(offset // 16, n1)]
                elif stage == 4:
                    src = dst = self.out.at[self.rows(second, n1)]
                else:
                    src = dst = self.out.at[self.rows(first, n0)]
                k = 3 * p + d
                out.append(remote(src, dst, self.ssem.at[stage, k], self.rsem.at[stage, k], to))
        return out

    def start(self, stage):
        for copy in self.copies(stage):
            copy.start()

    def finish(self, stage):
        for copy in self.copies(stage):
            copy.wait()
        if stage == 0:
            sl = self.rows(self.base, self.nh)
            self.buf[sl] = self.buf[sl] + self.cbuf[...]
        if stage not in (1, 2, 3):
            return
        came = (self.xbuf, self.ybuf, self.zbuf)[stage - 1]
        to = self.out if stage == 3 else self.buf
        for order, g0, g1, size, offset, start, first, second in self.parts:
            share = 4 if stage == 1 else 16
            sl = self.rows(first if stage == 1 else second, size // share)
            at_ = pl.ds(offset // share, size // share)
            to[sl] = (self.buf[sl] + came[0, at_]) + (came[1, at_] + came[2, at_])

    def step(self, stage):
        self.finish(stage)
        if stage < 6:
            self.start(stage + 1)


def kernel(factor, *refs):
    names_in = ["tok", "cot", "wi", "ws", "bias", "rate", "skip", "gain", "wo"]
    names_in = [name + "_h" for name in names_in]
    names_out = ["lo", "gt", "eres", "lres"]
    n_io = len(names_in) + len(names_out)
    k = dict(zip(names_in + names_out, refs[:n_io]))
    k.update(zip([name for name, _ in SCRATCH], refs[n_io:]))
    body(factor, **k)


def vm(*shape, dtype=F32):
    return pltpu.VMEM(shape, dtype)


BIG = (T, E)
SCRATCH = [
    ("x", vm(*BIG)), ("z", vm(*BIG)), ("ub", vm(2, *BIG, dtype=BF16)), ("stepe", vm(*BIG)),
    ("bt", vm(2, T, T, dtype=BF16)), ("ct", vm(2, T, T, dtype=BF16)), ("s", vm(T, T)), ("ds", vm(T, T)),
    ("wsel", vm(D, 640, dtype=BF16)), ("wpad", vm(D, 128, dtype=BF16)), ("vecs", vm(8, 128)),
    ("step", vm(T, 128)), ("sig", vm(T, 128)),
    ("cumr", vm(T, 128)), ("cumc", vm(T, 128)), ("cumrt", vm(128, T)), ("cumct", vm(128, T)),
    ("er", vm(*BIG)), ("ec", vm(*BIG)), ("wr", vm(*BIG)), ("wc", vm(*BIG)), ("dr", vm(*BIG)), ("dc", vm(*BIG)),
    ("dxr", vm(*BIG)), ("dxc", vm(*BIG)),
    ("finr", vm(SIDE, 128)), ("finc", vm(SIDE, 128)), ("allr", vm(128, 128)), ("allc", vm(128, 128)),
    ("wur", vm(2, *BIG, dtype=BF16)), ("wuc", vm(2, *BIG, dtype=BF16)),
    ("edr", vm(2, *BIG, dtype=BF16)), ("edc", vm(2, *BIG, dtype=BF16)),
    ("mr", vm(2, HEADS, T, T, dtype=BF16)), ("mc", vm(2, HEADS, T, T, dtype=BF16)), ("ls", vm(HEADS, T, T)),
    ("yr", vm(*BIG)), ("yc", vm(*BIG)), ("car", vm(*BIG)), ("cac", vm(*BIG)), ("dn", vm(*BIG)),
    ("dy", vm(*BIG)), ("dyb", vm(2, *BIG, dtype=BF16)), ("dzb", vm(*BIG, dtype=BF16)), ("nb", vm(*BIG, dtype=BF16)),
    ("qr", vm(*BIG)), ("qc", vm(*BIG)), ("dxb", vm(*BIG, dtype=BF16)), ("act", vm(*BIG)), ("hd", vm(T, 128)), ("dux", vm(*BIG)),
    ("dbe", vm(T, T)), ("dce", vm(T, T)),
    ("own", pltpu.VMEM((4, T, E), F32)), ("got", pltpu.VMEM((4, TILES, SHARE, E), F32)),
    ("out", pltpu.VMEM((4, TILES, SHARE, E), F32)), ("res", pltpu.VMEM((4, T, E), F32)),
    ("ebuf", vm(EARLY, 128)), ("ecb", vm(EARLY // 2, 128)), ("exb", vm(3, EARLY // 8, 128)),
    ("eyb", vm(3, EARLY // 32, 128)), ("ezb", vm(3, EARLY // 32, 128)),
    ("lbuf", vm(LATE, 128)), ("lcb", vm(LATE // 2, 128)), ("lxb", vm(3, LATE // 8, 128)),
    ("lyb", vm(3, LATE // 32, 128)), ("lzb", vm(3, LATE // 32, 128)),
    ("fsem", pltpu.SemaphoreType.DMA((2, 2, TILES))),
    ("cs", pltpu.SemaphoreType.DMA((4, 2, PARTS, TILES))), ("cr", pltpu.SemaphoreType.DMA((4, 2, PARTS, TILES))),
    ("es", pltpu.SemaphoreType.DMA((7, 9))), ("erv", pltpu.SemaphoreType.DMA((7, 9))),
    ("lsm", pltpu.SemaphoreType.DMA((7, 9))), ("lrv", pltpu.SemaphoreType.DMA((7, 9))),
]
SCRATCH += [
    ("tok", vm(T, D, dtype=BF16)), ("cot", vm(T, D, dtype=BF16)), ("wi", vm(D, 2 * E, dtype=BF16)),
    ("ws", vm(2 * STATE + HEADS, D, dtype=BF16)), ("bias", vm(1, HEADS)), ("rate", vm(1, HEADS)),
    ("skip", vm(1, HEADS)), ("gain", vm(1, E)), ("wo", vm(E, D, dtype=BF16)),
    ("isem", pltpu.SemaphoreType.DMA((9,))),
]
RB = 128


def loop(rows, fn, init=0):
    def step(i, carry):
        return fn(pl.ds(pl.multiple_of(i * RB, RB), RB), i, carry)

    return lax.fori_loop(0, rows // RB, step, init)


def body(factor, tok_h, cot_h, wi_h, ws_h, bias_h, rate_h, skip_h, gain_h, wo_h, lo, gt, eres, lres,
         x, z, ub, stepe, bt, ct, s, ds, wsel, wpad, vecs, step, sig, cumr, cumc, cumrt, cumct,
         er, ec, wr, wc, dr, dc, dxr, dxc, finr, finc, allr, allc, wur, wuc, edr, edc, mr, mc, ls,
         yr, yc, car, cac, dn, dy, dyb, dzb, nb, qr, qc, dxb, act, hd, dux, dbe, dce,
         own, got, out, res, ebuf, ecb, exb, eyb, ezb, lbuf, lcb, lxb, lyb, lzb,
         fsem, cs, cr, es, erv, lsm, lrv, tok, cot, wi, ws, bias, rate, skip, gain, wo, isem):
    pos = place()
    given = (ws_h, ws), (bias_h, bias), (rate_h, rate), (skip_h, skip), (tok_h, tok), (wi_h, wi), (cot_h, cot), (wo_h, wo), (gain_h, gain)
    fetch = [pltpu.make_async_copy(src, dst, isem.at[j]) for j, (src, dst) in enumerate(given)]
    for copy in fetch:
        copy.start()
    barrier = pltpu.get_barrier_semaphore()

    def scan(slot, axis, back):
        return Scan(pos, axis, back, own.at[slot], got.at[slot], out.at[slot], res.at[slot], (dxr, dxc)[slot % 2],
                    cs, cr, slot)

    fr, fc, gr_, gc_ = scan(0, "r", False), scan(1, "c", False), scan(2, "r", True), scan(3, "c", True)
    near = [who.peer(d)[1] for who in (fr, fc) for d in range(1, TILES)]
    near += [at(pos, xl=1 - pos["xl"]), at(pos, xl=1 - pos["xl"], xh=1 - pos["xh"])]
    for to in near:
        pl.semaphore_signal(barrier, inc=1, device_id=to, device_id_type=MESH)
    early = Total(pos, ebuf, eres, ecb, exb, eyb, ezb, es, erv, (EARLY // 2,))
    late = Total(pos, lbuf, lres, lcb, lxb, lyb, lzb, lsm, lrv, (512, 128))

    for copy in fetch[:5]:
        copy.wait()
    r, c = grid2(2 * STATE + HEADS, 640)
    sel = ((c < 256) & (r == lo4(c))) | ((c >= 256) & (c < 512) & (r == 16 + lo4(c))) | ((c >= 512) & (r == c - 480))
    wsel[...] = mm(ws[...], ind(sel), 0, 0).astype(BF16)
    r, c = grid2(2 * STATE + HEADS, 128)
    wpad[...] = mm(ws[...], ind(r == c), 0, 0).astype(BF16)
    vecs[...] = jnp.zeros((8, 128), F32)
    vecs[0:1, 0:HEADS] = bias[...]
    vecs[1:2, 0:HEADS] = rate[...]
    vecs[2:3, 0:HEADS] = skip[...]
    raw = mm(tok[...], wsel[:, 512:640]) + vecs[0:1, :]
    tail = jnp.exp(-jnp.abs(raw))
    stp = jnp.maximum(raw, 0.0) + jnp.log1p(tail)
    step[...] = stp
    sig[...] = jnp.where(raw >= 0, 1.0, tail) / (1.0 + tail)
    a = -stp * vecs[1:2, :]
    t, u = grid2(T, T)
    same_r, same_c = hi4(t) == hi4(u), lo4(t) == lo4(u)
    aft_r = pick(ind(same_r & (u > t)), a)
    aft_c = pick(ind(same_c & (u > t)), a)
    r, c = grid2(SIDE, T)
    finr[...] = jnp.exp(pick(ind(r == hi4(c)), a))
    finc[...] = jnp.exp(pick(ind(r == lo4(c)), a))
    hx = head_spread()
    stepe[...] = spread(stp, hx, 3)
    wr[...] = spread(jnp.exp(aft_r), hx)
    wc[...] = spread(jnp.exp(aft_c), hx)
    fetch[5].wait()
    x[...] = mm(tok[...], wi[:, 0:E])
    keep(bt, (), mm(tok[...], wsel[:, 0:256]))

    def drive(sl, i, carry):
        u_ = stepe[sl] * x[sl]
        keep(ub, (sl,), u_)
        keep(wur, (sl,), wr[sl] * u_)
        keep(wuc, (sl,), wc[sl] * u_)
        return carry

    loop(T, drive)
    line_r, line_c = hi4(t) == hi4(u), lo4(t) == hi4(u)
    own[1] = mm3(only(line_c, bt), both(wuc), 0, 0)
    own[0] = mm3(only(line_r, bt), both(wur), 0, 0)
    pl.semaphore_wait(barrier, len(near))
    ends = []
    for a_, (who, mine, all_) in enumerate(((fc, finc, allc), (fr, finr, allr))):
        place_ = pl.ds(pl.multiple_of(who.me * SIDE, SIDE), SIDE)
        all_[place_] = mine[...]
        for d in range(1, TILES):
            ends.append(remote(mine, all_.at[place_], fsem.at[a_, 0, d], fsem.at[a_, 1, d], who.peer(d)[1]))
            ends[-1].start()
    for part in range(PARTS):
        fc.start(part)
        fr.start(part)

    cumr[...] = pick(ind(same_r & (u <= t)), a)
    cumc[...] = pick(ind(same_c & (u <= t)), a)

    def lines(rows, first, ends):
        k, l = grid2(rows, SIDE)
        return pick(ind(hi4(k) + first == l), spread(ends, hx), 2)

    dr[...] = lines(T, 0, finr[...])
    dc[...] = lines(T, 0, finc[...])

    z[...] = mm(tok[...], wi[:, E : 2 * E])
    keep(ct, (), mm(tok[...], wsel[:, 256:512]))
    s[...] = mm3(both(ct), both(bt), 1, 1) * (1.0 / 16.0)
    er[...] = spread(jnp.exp(cumr[...]), hx)
    ec[...] = spread(jnp.exp(cumc[...]), hx)
    cumrt[...] = cumr[...].T
    cumct[...] = cumc[...].T

    def masks(sl, i, carry):
        t_, u_ = grid2(RB, T)
        t_ = t_ + i * RB
        in_r = (hi4(t_) == hi4(u_)) & (u_ <= t_)
        in_c = (lo4(t_) == lo4(u_)) & (u_ <= t_)
        s_ = s[sl]
        c_r, c_c = cumr[sl], cumc[sl]
        for h in range(HEADS):
            l_r = jnp.exp(jnp.where(in_r, c_r[:, h : h + 1] - cumrt[h : h + 1, :], NEG))
            l_c = jnp.exp(jnp.where(in_c, c_c[:, h : h + 1] - cumct[h : h + 1, :], NEG))
            keep(mr, (h, sl), l_r * s_)
            keep(mc, (h, sl), l_c * s_)
            ls[h, sl] = l_r + l_c
        return carry

    loop(T, masks)
    low = lax.broadcasted_iota(jnp.int32, (T, 128), 1) < HDIM

    def heads(m, hp, pair, dim):
        wide = jnp.concatenate(pair, axis=1)
        part = []
        for h in (2 * hp, 2 * hp + 1):
            full = mm(m[0, h], wide, dim, 0)
            part.append(full[:, :128] + full[:, 128:] + mm(m[1, h], pair[0], dim, 0))
        return jnp.where(low, part[0], part[1])

    def within(hp, carry):
        sl = pl.ds(pl.multiple_of(hp * 128, 128), 128)
        u_ = (ub[0, :, sl], ub[1, :, sl])
        yr[:, sl] = heads(mr, hp, u_, 1)
        yc[:, sl] = heads(mc, hp, u_, 1)
        return carry

    for copy in fetch[6:]:
        copy.wait()

    for copy in ends:
        copy.wait_recv()
    k, l = grid2(T, 128)
    line = lax.shift_right_logical(k, 5) * SIDE + jnp.bitwise_and(hi4(k), 1)
    for who, all_ in ((fr, allr), (fc, allc)):
        who.dec[...] = spread(pick(ind(l == line + 2 * who.me), all_[...], 2), hx)
    for part in range(PARTS):
        fr.turn(part)
        fc.turn(part)
    lax.fori_loop(0, HEADS // 2, within, 0)
    dn[...] = mm(cot[...], wo[...], 1, 1)

    def gate(sl, i, carry):
        z_ = z[sl]
        sg = 1.0 / (1.0 + jnp.exp(-z_))
        act[sl] = z_ * sg
        z[sl] = sg * (1.0 + z_ * (1.0 - sg))
        return carry

    loop(T, gate)
    fr.finish()
    car[...] = mm3(only(line_r, ct), split(res[0], 2))
    fc.finish()
    cac[...] = mm3(only(line_c, ct), split(res[1], 2))

    skipe = spread(vecs[...], hx, 3)[2:3, :]
    gain_ = gain[...]

    def middle(sl, i, carry):
        sum_gain, sum_skip = carry
        x_, act_ = x[sl], act[sl]
        c_r, c_c = er[sl] * car[sl], ec[sl] * cac[sl]
        w_r, w_c = yr[sl], yc[sl]
        y = (w_r + w_c) + (c_r + c_c) + skipe * x_
        gated = y * act_
        inv = lax.rsqrt(jnp.mean(gated * gated, axis=-1, keepdims=True) + 1e-05)
        unit = gated * inv
        nb[sl] = (unit * gain_).astype(BF16)
        d_n = dn[sl]
        g1 = d_n * gain_
        dg = inv * (g1 - unit * jnp.mean(g1 * unit, axis=-1, keepdims=True))
        d_y = dg * act_
        dzb[sl] = (dg * y * z[sl]).astype(BF16)
        dy[sl] = d_y
        keep(dyb, (sl,), d_y)
        keep(edr, (sl,), er[sl] * d_y)
        keep(edc, (sl,), ec[sl] * d_y)
        qr[sl] = d_y * (c_r + w_r)
        qc[sl] = d_y * (c_c + w_c)
        fold = lambda v: functools.reduce(lambda p, q: p + q, [v[8 * j : 8 * j + 8] for j in range(RB // 8)])
        return sum_gain + fold(d_n * unit), sum_skip + fold(d_y * x_)

    nil = jnp.zeros((8, E), F32)
    sum_gain, sum_skip = loop(T, middle, (nil, nil))
    own[3] = mm3(only(line_c, ct), both(edc), 0, 0)
    for part in range(PARTS):
        gc_.start(part)
    own[2] = mm3(only(line_r, ct), both(edr), 0, 0)
    for part in range(PARTS):
        gr_.start(part)

    lg = mm(tok[...], dzb[...], 0, 0) * factor
    for j in range(4):
        ebuf[j * 256 : (j + 1) * 256] = lg[:, j * 128 : (j + 1) * 128]
    lg = mm(nb[...], cot[...], 0, 0) * factor
    for j in range(2):
        ebuf[1024 + j * 512 : 1024 + (j + 1) * 512] = lg[:, j * 128 : (j + 1) * 128]
    early.start(0)
    def within_back(hp, carry):
        sl = pl.ds(pl.multiple_of(hp * 128, 128), 128)
        d_ = (dyb[0, :, sl], dyb[1, :, sl])
        yr[:, sl] = heads(mr, hp, d_, 0)
        yc[:, sl] = heads(mc, hp, d_, 0)
        return carry


    def scores_back(hp, carry):
        sl = pl.ds(pl.multiple_of(hp * 128, 128), 128)
        u_h, u_l = ub[0, :, sl], ub[1, :, sl]
        twice = jnp.concatenate((u_h, u_h), axis=1)
        total = ds[...]
        for j in (0, 1):
            d_h, d_l = only(low if j == 0 else ~low, (dyb[0, :, sl], dyb[1, :, sl]))
            pairs = mm(jnp.concatenate((d_h, d_l), axis=1), twice, 1, 1) + mm(d_h, u_l, 1, 1)
            total = total + ls[2 * hp + j] * pairs
        ds[...] = total
        return carry

    lax.fori_loop(0, HEADS // 2, within_back, 0)
    for part in range(PARTS):
        gr_.turn(part)
        gc_.turn(part)
    ds[...] = jnp.zeros((T, T), F32)
    lax.fori_loop(0, HEADS // 2, scores_back, 0)
    head = u < STATE
    d_s = split(ds[...], 2)
    dce[...] = (
        jnp.where(line_r, mm3(both(edr), split(res[0], 2), 1, 1), 0.0)
        + jnp.where(line_c, mm3(both(edc), split(res[1], 2), 1, 1), 0.0)
        + jnp.where(head, mm3(d_s, both(bt)), 0.0)
    )
    dbe[...] = jnp.where(head, mm3(d_s, both(ct), 0, 0), 0.0)
    lo[...] = mm(nb[...], wo[...]).astype(BF16)

    def ahead(sl, i, carry):
        x_, se = x[sl], stepe[sl]
        u_ = se * x_
        w_r, w_c = yr[sl], yc[sl]
        w_ = w_r + w_c
        qr[sl] = qr[sl] - u_ * w_r
        qc[sl] = qc[sl] - u_ * w_c
        dux[sl] = w_ * x_
        dy[sl] = se * w_ + skipe * dy[sl]
        res[0, sl] = own[0, sl] + dr[sl] * res[0, sl]
        res[1, sl] = own[1, sl] + dc[sl] * res[1, sl]
        return carry

    loop(T, ahead)
    cumr[...] = head_sum(qr[...])
    cumc[...] = head_sum(qc[...])
    hd[...] = head_sum(dux[...])
    early.step(0)
    gr_.finish()
    g_r = split(res[2], 2)
    car[...] = mm3(only(line_r, bt), g_r)
    dbe[...] = dbe[...] + jnp.where(line_r, mm3(both(wur), g_r, 1, 1), 0.0)
    gc_.finish()
    g_c = split(res[3], 2)
    cac[...] = mm3(only(line_c, bt), g_c)
    dbe[...] = dbe[...] + jnp.where(line_c, mm3(both(wuc), g_c, 1, 1), 0.0)

    def last(sl, i, carry):
        x_ = x[sl]
        v_r, v_c = wr[sl] * car[sl], wc[sl] * cac[sl]
        qr[sl] = x_ * v_r
        qc[sl] = x_ * v_c
        dxb[sl] = (dy[sl] + stepe[sl] * (v_r + v_c)).astype(BF16)
        res[0, sl] = res[2, sl] * res[0, sl]
        res[1, sl] = res[3, sl] * res[1, sl]
        return carry

    loop(T, last)
    lg = mm(tok[...], dxb[...], 0, 0) * factor
    for j in range(4):
        lbuf[LROW[j] : LROW[j] + 256] = lg[:, j * 128 : (j + 1) * 128]
    late_core = late.copies(0)
    late_core[0].start()
    h_r, h_c = head_sum(qr[...]), head_sum(qc[...])
    d_a = (
        pick(ind(same_r & (u >= t)), cumr[...] - step[...] * h_r)
        + pick(ind(same_c & (u >= t)), cumc[...] - step[...] * h_c)
        + pick(ind(line_r), head_sum(res[0]))
        + pick(ind(line_c), head_sum(res[1]))
    )
    d_step = hd[...] + (h_r + h_c) - vecs[1:2, :] * d_a
    d_raw = d_step * sig[...]
    r, c = grid2(T, 128)
    d_ssm = (
        spread(dbe[...], ind(c == lo4(r)))
        + spread(dce[...], ind(c == 16 + lo4(r)))
        + spread(d_raw, ind(grid2(128, 128)[1] == 32 + grid2(128, 128)[0]), 3)
    )
    d_ssm = d_ssm.astype(BF16)
    lg = mm(d_ssm, tok[...], 0, 0) * factor
    for j in range(2):
        lbuf[SROW[j] : SROW[j] + 128] = lg[:, j * 128 : (j + 1) * 128]
    total_of = lambda v: jnp.sum(v, axis=0, keepdims=True)
    sum_gain = total_of(sum_gain) * factor
    for j in range(4):
        lbuf[VROW + j : VROW + j + 1] = sum_gain[:, j * 128 : (j + 1) * 128]
    lbuf[VROW + 4 : VROW + 5] = total_of(d_raw) * factor
    lbuf[VROW + 5 : VROW + 6] = -total_of(step[...] * d_a) * factor
    lbuf[VROW + 6 : VROW + 7] = total_of(head_sum(sum_skip)) * factor
    late_core[1].start()
    early.step(1)
    back = mm(dxb[...], wi[:, 0:E], 1, 1)
    late.step(0)
    back = back + mm(dzb[...], wi[:, E : 2 * E], 1, 1)
    back = back + mm(d_ssm, wpad[...], 1, 1)
    gt[...] = back.astype(BF16)
    early.step(2)
    late.step(1)
    early.step(3)
    late.step(2)
    early.step(4)
    late.step(3)
    early.step(5)
    for who in (fr, fc, gr_, gc_):
        who.drain()
    for copy in ends:
        copy.wait_send()
    late.step(4)
    early.finish(6)
    late.step(5)
    late.step(6)


def unpack(eres, lres, lo_in, gt_in, lo, gt, gi, gs, go, gb, gr, gk, gg):
    lo[...] = lo_in[...]
    gt[...] = gt_in[...]
    for j in range(4):
        gi[:, j * 128 : (j + 1) * 128] = lres[LROW[j] : LROW[j] + 256]
        gi[:, E + j * 128 : E + (j + 1) * 128] = eres[j * 256 : (j + 1) * 256]
        gg[:, j * 128 : (j + 1) * 128] = lres[VROW + j : VROW + j + 1]
    for j in range(2):
        go[:, j * 128 : (j + 1) * 128] = eres[1024 + j * 512 : 1024 + (j + 1) * 512]
        gs[:, j * 128 : (j + 1) * 128] = lres[SROW[j] : SROW[j] + 40]
    gb[...] = lres[VROW + 4 : VROW + 5, 0:HEADS]
    gr[...] = lres[VROW + 5 : VROW + 6, 0:HEADS]
    gk[...] = lres[VROW + 6 : VROW + 7, 0:HEADS]


def local(tokens_in, out_cotangent, w_inner, w_ssm, dt_bias, decay_rate, skip_gain, norm_gain, w_out):
    devices = lax.axis_size("slide") * lax.axis_size("row") * lax.axis_size("col")
    factor = float(devices * T) ** -0.5
    shape = jax.ShapeDtypeStruct
    vmem = pl.BlockSpec(memory_space=pltpu.VMEM)
    lo, gt, eres, lres = pl.pallas_call(
        functools.partial(kernel, factor),
        out_shape=(shape((T, D), BF16), shape((T, D), BF16), shape((EARLY, 128), F32), shape((LATE, 128), F32)),
        in_specs=[pl.BlockSpec(memory_space=pltpu.HBM)] * 9,
        out_specs=(vmem,) * 4,
        scratch_shapes=[kind for _, kind in SCRATCH],
        compiler_params=pltpu.CompilerParams(
            collective_id=0, has_side_effects=True, vmem_limit_bytes=48 * 2**20
        ),
    )(
        *[
            pltpu.with_memory_space_constraint(array, pltpu.HBM)
            for array in (
                tokens_in.reshape(T, D),
                out_cotangent.reshape(T, D),
                w_inner,
                w_ssm.T,
                dt_bias.reshape(1, -1),
                decay_rate.reshape(1, -1),
                skip_gain.reshape(1, -1),
                norm_gain.reshape(1, -1),
                w_out,
            )
        ]
    )
    out = pl.pallas_call(
        unpack,
        out_shape=(
            shape((T, D), BF16),
            shape((T, D), BF16),
            shape(w_inner.shape, F32),
            shape(w_ssm.shape[::-1], F32),
            shape(w_out.shape, F32),
            shape((1, HEADS), F32),
            shape((1, HEADS), F32),
            shape((1, HEADS), F32),
            shape((1, E), F32),
        ),
        in_specs=[vmem] * 4,
        out_specs=(vmem,) * 9,
        compiler_params=pltpu.CompilerParams(vmem_limit_bytes=6 * 2**20),
    )(eres, lres, lo, gt)
    return (
        out[0].reshape(tokens_in.shape),
        out[1].reshape(tokens_in.shape),
        out[2],
        out[3].T,
        out[4],
        out[5].reshape(-1),
        out[6].reshape(-1),
        out[7].reshape(-1),
        out[8].reshape(-1),
    )


def solution(mesh):
    tiles = P("slide", "row", "col", None)
    return jax.shard_map(
        local,
        mesh=mesh,
        in_specs=(tiles, tiles) + (P(),) * 7,
        out_specs=(tiles, tiles) + (P(),) * 7,
        check_vma=False,
    )
```

```python
import functools

import jax
import jax.numpy as jnp
from jax import lax
from jax.experimental import pallas as pl
from jax.experimental.pallas import tpu as pltpu
from jax.sharding import PartitionSpec as P

MESH = pl.DeviceIdType.MESH
F32 = jnp.float32
BF16 = jnp.bfloat16
HEADS = 8
HDIM = 64
STATE = 16
SIDE = 16
T = SIDE * SIDE
E = HEADS * HDIM
D = 256
TILES = 8
SHARE = T // TILES
PARTS = SHARE // STATE
ORDER = (4, 3, 5, 2, 6, 1, 7)
NEG = -1e30
EARLY = 2048
LATE = 1280
LROW = (0, 256, 640, 896)
SROW = (512, 1152)
VROW = 512 + 64


def mm(a, b, ca=1, cb=0):
    return lax.dot_general(a, b, (((ca,), (cb,)), ((), ())), preferred_element_type=F32)


def split(x, terms):
    out = []
    for _ in range(terms - 1):
        hi = x.astype(BF16)
        out.append(hi)
        x = x - hi.astype(F32)
    out.append(x.astype(BF16))
    return out


def pick(mask, x, terms=3):
    return functools.reduce(lambda u, v: u + v, [mm(mask, part) for part in split(x, terms)])


def spread(x, mask, terms=2):
    return functools.reduce(lambda u, v: u + v, [mm(part, mask) for part in split(x, terms)])


def mm3(a, b, ca=1, cb=0):
    (ah, al), (bh, bl) = a, b
    return mm(ah, bh, ca, cb) + (mm(ah, bl, ca, cb) + mm(al, bh, ca, cb))


def keep(pair, where, x):
    hi, lo = split(x, 2)
    pair[(0,) + where] = hi
    pair[(1,) + where] = lo


def both(pair):
    return pair[0], pair[1]


def only(mask, pair):
    nil = jnp.zeros(mask.shape, BF16)
    return jnp.where(mask, pair[0], nil), jnp.where(mask, pair[1], nil)


def ind(cond):
    return jnp.where(cond, 1.0, 0.0).astype(BF16)


def grid2(rows, cols):
    return (
        lax.broadcasted_iota(jnp.int32, (rows, cols), 0),
        lax.broadcasted_iota(jnp.int32, (rows, cols), 1),
    )


def hi4(x):
    return lax.shift_right_logical(x, 4)


def lo4(x):
    return jnp.bitwise_and(x, 15)


def head_spread():
    r, c = grid2(128, E)
    return ind(r == lax.shift_right_logical(c, 6))


def head_sum(x):
    r, c = grid2(E, 128)
    return spread(x, ind(lax.shift_right_logical(r, 6) == c), 2)


def place():
    row, col, slide = lax.axis_index("row"), lax.axis_index("col"), lax.axis_index("slide")
    return dict(y=row // 2, xh=lax.rem(row, 2), z=col // 2, co=lax.rem(col, 2), xl=slide)


def at(pos, **change):
    p = dict(pos, **change)
    return (p["y"] * 2 + p["xh"], p["z"] * 2 + p["co"], p["xl"])


def flip(bit, by):
    return bit + by * (1 - 2 * bit)


def peers(pos, axis):
    out = []
    for d in (1, 2, 3):
        if axis == "x":
            out.append(at(pos, xh=flip(pos["xh"], d // 2), xl=flip(pos["xl"], d % 2)))
        else:
            out.append(at(pos, **{axis: xor4(pos[axis], d)}))
    return out


def xor4(q, d):
    return 2 * flip(q // 2, d // 2) + flip(lax.rem(q, 2), d % 2)


def remote(src, dst, ssem, rsem, to):
    return pltpu.make_async_remote_copy(
        src_ref=src, dst_ref=dst, send_sem=ssem, recv_sem=rsem, device_id=to, device_id_type=MESH
    )


class Scan:
    def __init__(self, pos, axis, back, own, got, out, res, dec, ssem, rsem, slot):
        self.me = lax.axis_index("col" if axis == "r" else "row")
        self.pos, self.axis, self.back = pos, axis, back
        self.head, self.last = (TILES - 1, 0) if back else (0, TILES - 1)
        self.own, self.got, self.out, self.res, self.dec = own, got, out, res, dec
        self.ssem, self.rsem, self.slot = ssem, rsem, slot

    def peer(self, d):
        k = lax.rem(self.me + d, TILES)
        if self.axis == "r":
            return k, (lax.axis_index("row"), k, self.pos["xl"])
        return k, (k, lax.axis_index("col"), self.pos["xl"])

    def lines(self, k, part):
        return pl.ds(pl.multiple_of(k * SHARE + part * STATE, STATE), STATE)

    def copies(self, stage, part):
        out, piece = [], pl.ds(part * STATE, STATE)
        for d in ORDER:
            k, to = self.peer(d)
            sems = self.ssem.at[self.slot, stage, part, d], self.rsem.at[self.slot, stage, part, d]
            if stage == 0:
                out.append(remote(self.own.at[self.lines(k, part)], self.got.at[self.me, piece], *sems, to))
            else:
                out.append(remote(self.out.at[k, piece], self.res.at[self.lines(self.me, part)], *sems, to))
        return out

    def start(self, part):
        @pl.when(self.me != self.last)
        def _():
            for copy in self.copies(0, part):
                copy.start()

        self.got[self.me, pl.ds(part * STATE, STATE)] = self.own[self.lines(self.me, part)]

    def turn(self, part):
        for d, copy in zip(ORDER, self.copies(0, part)):
            pl.when(lax.rem(self.me - d + TILES, TILES) != self.last)(copy.wait_recv)
        state, piece = jnp.zeros((STATE, E), F32), pl.ds(part * STATE, STATE)
        for j in range(TILES - 1, -1, -1) if self.back else range(TILES):
            self.out[j, piece] = state
            if j != self.last:
                state = self.dec[pl.ds(j * SHARE + part * STATE, STATE)] * state + self.got[j, piece]
        for d, copy in zip(ORDER, self.copies(1, part)):
            pl.when(self.peer(d)[0] != self.head)(copy.start)

    def finish(self):
        @pl.when(self.me == self.head)
        def _():
            self.res[...] = jnp.zeros((T, E), F32)

        @pl.when(self.me != self.head)
        def _():
            for part in range(PARTS):
                self.res[self.lines(self.me, part)] = self.out[self.me, pl.ds(part * STATE, STATE)]
                for copy in self.copies(1, part):
                    copy.wait_recv()

    def drain(self):
        for part in range(PARTS):
            @pl.when(self.me != self.last)
            def _():
                for copy in self.copies(0, part):
                    copy.wait_send()

            for d, copy in zip(ORDER, self.copies(1, part)):
                pl.when(self.peer(d)[0] != self.head)(copy.wait_send)


class Total:
    def __init__(self, pos, buf, out, cbuf, xbuf, ybuf, zbuf, ssem, rsem, cuts):
        n = buf.shape[0]
        self.cuts = cuts
        self.pos, self.buf, self.out = pos, buf, out
        self.cbuf, self.xbuf, self.ybuf, self.zbuf = cbuf, xbuf, ybuf, zbuf
        self.ssem, self.rsem = ssem, rsem
        self.nh = n // 2
        self.base = pos["co"] * self.nh
        self.other = at(pos, co=1 - pos["co"])
        index = {"x": pos["xh"] * 2 + pos["xl"], "y": pos["y"], "z": pos["z"]}
        third = -(-self.nh // 384) * 128
        sizes = (third, third, self.nh - 2 * third)
        self.parts, offset = [], 0
        for size, order in zip(sizes, ("xyz", "yzx", "zxy")):
            start = self.base + offset
            first = start + index[order[0]] * (size // 4)
            second = first + index[order[1]] * (size // 16)
            self.parts.append((order, index[order[0]], index[order[1]], size, offset, start, first, second))
            offset += size

    def rows(self, start, size):
        return pl.ds(pl.multiple_of(start, 8), size)

    def copies(self, stage):
        pos = self.pos
        if stage == 0:
            out, offset = [], 0
            for k, size in enumerate(self.cuts):
                src = self.buf.at[self.rows((1 - pos["co"]) * self.nh + offset, size)]
                sems = self.ssem.at[0, k], self.rsem.at[0, k]
                out.append(remote(src, self.cbuf.at[pl.ds(offset, size)], *sems, self.other))
                offset += size
            return out
        if stage == 6:
            own = self.out.at[self.rows(self.base, self.nh)]
            return [remote(own, own, self.ssem.at[6, 0], self.rsem.at[6, 0], self.other)]
        out = []
        for p, (order, g0, g1, size, offset, start, first, second) in enumerate(self.parts):
            n0, n1 = size // 4, size // 16
            axis = order[(0, 1, 2, 1, 0)[stage - 1]]
            for d, to in enumerate(peers(pos, axis)):
                if stage == 1:
                    src = self.buf.at[self.rows(start + xor4(g0, d + 1) * n0, n0)]
                    dst = self.xbuf.at[d, pl.ds(offset // 4, n0)]
                elif stage == 2:
                    src = self.buf.at[self.rows(first + xor4(g1, d + 1) * n1, n1)]
                    dst = self.ybuf.at[d, pl.ds(offset // 16, n1)]
                elif stage == 3:
                    src, dst = self.buf.at[self.rows(second, n1)], self.zbuf.at[d, pl.ds(offset // 16, n1)]
                elif stage == 4:
                    src = dst = self.out.at[self.rows(second, n1)]
                else:
                    src = dst = self.out.at[self.rows(first, n0)]
                k = 3 * p + d
                out.append(remote(src, dst, self.ssem.at[stage, k], self.rsem.at[stage, k], to))
        return out

    def start(self, stage):
        for copy in self.copies(stage):
            copy.start()

    def finish(self, stage):
        for copy in self.copies(stage):
            copy.wait()
        if stage == 0:
            sl = self.rows(self.base, self.nh)
            self.buf[sl] = self.buf[sl] + self.cbuf[...]
        if stage not in (1, 2, 3):
            return
        came = (self.xbuf, self.ybuf, self.zbuf)[stage - 1]
        to = self.out if stage == 3 else self.buf
        for order, g0, g1, size, offset, start, first, second in self.parts:
            share = 4 if stage == 1 else 16
            sl = self.rows(first if stage == 1 else second, size // share)
            at_ = pl.ds(offset // share, size // share)
            to[sl] = (self.buf[sl] + came[0, at_]) + (came[1, at_] + came[2, at_])

    def step(self, stage):
        self.finish(stage)
        if stage < 6:
            self.start(stage + 1)


def kernel(factor, *refs):
    names_in = ["tok", "cot", "wi", "ws", "bias", "rate", "skip", "gain", "wo"]
    names_in = [name + "_h" for name in names_in]
    names_out = ["lo", "gt", "eres", "lres"]
    n_io = len(names_in) + len(names_out)
    k = dict(zip(names_in + names_out, refs[:n_io]))
    k.update(zip([name for name, _ in SCRATCH], refs[n_io:]))
    body(factor, **k)


def vm(*shape, dtype=F32):
    return pltpu.VMEM(shape, dtype)


BIG = (T, E)
SCRATCH = [
    ("x", vm(*BIG)), ("z", vm(*BIG)), ("ub", vm(2, *BIG, dtype=BF16)), ("stepe", vm(*BIG)),
    ("bt", vm(2, T, T, dtype=BF16)), ("ct", vm(2, T, T, dtype=BF16)), ("s", vm(T, T)), ("ds", vm(T, T)),
    ("wsel", vm(D, 640, dtype=BF16)), ("wpad", vm(D, 128, dtype=BF16)), ("vecs", vm(8, 128)),
    ("step", vm(T, 128)), ("sig", vm(T, 128)),
    ("cumr", vm(T, 128)), ("cumc", vm(T, 128)), ("cumrt", vm(128, T)), ("cumct", vm(128, T)),
    ("er", vm(*BIG)), ("ec", vm(*BIG)), ("wr", vm(*BIG)), ("wc", vm(*BIG)), ("dr", vm(*BIG)), ("dc", vm(*BIG)),
    ("dxr", vm(*BIG)), ("dxc", vm(*BIG)),
    ("finr", vm(SIDE, 128)), ("finc", vm(SIDE, 128)), ("allr", vm(128, 128)), ("allc", vm(128, 128)),
    ("wur", vm(2, *BIG, dtype=BF16)), ("wuc", vm(2, *BIG, dtype=BF16)),
    ("edr", vm(2, *BIG, dtype=BF16)), ("edc", vm(2, *BIG, dtype=BF16)),
    ("mr", vm(2, HEADS, T, T, dtype=BF16)), ("mc", vm(2, HEADS, T, T, dtype=BF16)), ("ls", vm(HEADS, T, T)),
    ("yr", vm(*BIG)), ("yc", vm(*BIG)), ("car", vm(*BIG)), ("cac", vm(*BIG)), ("dn", vm(*BIG)),
    ("dy", vm(*BIG)), ("dyb", vm(2, *BIG, dtype=BF16)), ("dzb", vm(*BIG, dtype=BF16)), ("nb", vm(*BIG, dtype=BF16)),
    ("qr", vm(*BIG)), ("qc", vm(*BIG)), ("dxb", vm(*BIG, dtype=BF16)), ("act", vm(*BIG)), ("hd", vm(T, 128)), ("dux", vm(*BIG)),
    ("dbe", vm(T, T)), ("dce", vm(T, T)),
    ("own", pltpu.VMEM((4, T, E), F32)), ("got", pltpu.VMEM((4, TILES, SHARE, E), F32)),
    ("out", pltpu.VMEM((4, TILES, SHARE, E), F32)), ("res", pltpu.VMEM((4, T, E), F32)),
    ("ebuf", vm(EARLY, 128)), ("ecb", vm(EARLY // 2, 128)), ("exb", vm(3, EARLY // 8, 128)),
    ("eyb", vm(3, EARLY // 32, 128)), ("ezb", vm(3, EARLY // 32, 128)),
    ("lbuf", vm(LATE, 128)), ("lcb", vm(LATE // 2, 128)), ("lxb", vm(3, LATE // 8, 128)),
    ("lyb", vm(3, LATE // 32, 128)), ("lzb", vm(3, LATE // 32, 128)),
    ("fsem", pltpu.SemaphoreType.DMA((2, 2, TILES))),
    ("cs", pltpu.SemaphoreType.DMA((4, 2, PARTS, TILES))), ("cr", pltpu.SemaphoreType.DMA((4, 2, PARTS, TILES))),
    ("es", pltpu.SemaphoreType.DMA((7, 9))), ("erv", pltpu.SemaphoreType.DMA((7, 9))),
    ("lsm", pltpu.SemaphoreType.DMA((7, 9))), ("lrv", pltpu.SemaphoreType.DMA((7, 9))),
]
SCRATCH += [
    ("tok", vm(T, D, dtype=BF16)), ("cot", vm(T, D, dtype=BF16)), ("wi", vm(D, 2 * E, dtype=BF16)),
    ("ws", vm(2 * STATE + HEADS, D, dtype=BF16)), ("bias", vm(1, HEADS)), ("rate", vm(1, HEADS)),
    ("skip", vm(1, HEADS)), ("gain", vm(1, E)), ("wo", vm(E, D, dtype=BF16)),
    ("isem", pltpu.SemaphoreType.DMA((9,))),
]
RB = 256


def loop(rows, fn, init=0):
    def step(i, carry):
        return fn(pl.ds(pl.multiple_of(i * RB, RB), RB), i, carry)

    return lax.fori_loop(0, rows // RB, step, init)


def body(factor, tok_h, cot_h, wi_h, ws_h, bias_h, rate_h, skip_h, gain_h, wo_h, lo, gt, eres, lres,
         x, z, ub, stepe, bt, ct, s, ds, wsel, wpad, vecs, step, sig, cumr, cumc, cumrt, cumct,
         er, ec, wr, wc, dr, dc, dxr, dxc, finr, finc, allr, allc, wur, wuc, edr, edc, mr, mc, ls,
         yr, yc, car, cac, dn, dy, dyb, dzb, nb, qr, qc, dxb, act, hd, dux, dbe, dce,
         own, got, out, res, ebuf, ecb, exb, eyb, ezb, lbuf, lcb, lxb, lyb, lzb,
         fsem, cs, cr, es, erv, lsm, lrv, tok, cot, wi, ws, bias, rate, skip, gain, wo, isem):
    pos = place()
    given = (ws_h, ws), (bias_h, bias), (rate_h, rate), (skip_h, skip), (tok_h, tok), (wi_h, wi), (cot_h, cot), (wo_h, wo), (gain_h, gain)
    fetch = [pltpu.make_async_copy(src, dst, isem.at[j]) for j, (src, dst) in enumerate(given)]
    for copy in fetch:
        copy.start()
    barrier = pltpu.get_barrier_semaphore()

    def scan(slot, axis, back):
        return Scan(pos, axis, back, own.at[slot], got.at[slot], out.at[slot], res.at[slot], (dxr, dxc)[slot % 2],
                    cs, cr, slot)

    fr, fc, gr_, gc_ = scan(0, "r", False), scan(1, "c", False), scan(2, "r", True), scan(3, "c", True)
    near = [who.peer(d)[1] for who in (fr, fc) for d in range(1, TILES)]
    near += [at(pos, xl=1 - pos["xl"]), at(pos, xl=1 - pos["xl"], xh=1 - pos["xh"])]
    for to in near:
        pl.semaphore_signal(barrier, inc=1, device_id=to, device_id_type=MESH)
    early = Total(pos, ebuf, eres, ecb, exb, eyb, ezb, es, erv, (EARLY // 2,))
    late = Total(pos, lbuf, lres, lcb, lxb, lyb, lzb, lsm, lrv, (512, 128))

    for copy in fetch[:5]:
        copy.wait()
    r, c = grid2(2 * STATE + HEADS, 640)
    sel = ((c < 256) & (r == lo4(c))) | ((c >= 256) & (c < 512) & (r == 16 + lo4(c))) | ((c >= 512) & (r == c - 480))
    wsel[...] = mm(ws[...], ind(sel), 0, 0).astype(BF16)
    r, c = grid2(2 * STATE + HEADS, 128)
    wpad[...] = mm(ws[...], ind(r == c), 0, 0).astype(BF16)
    vecs[...] = jnp.zeros((8, 128), F32)
    vecs[0:1, 0:HEADS] = bias[...]
    vecs[1:2, 0:HEADS] = rate[...]
    vecs[2:3, 0:HEADS] = skip[...]
    raw = mm(tok[...], wsel[:, 512:640]) + vecs[0:1, :]
    tail = jnp.exp(-jnp.abs(raw))
    stp = jnp.maximum(raw, 0.0) + jnp.log1p(tail)
    step[...] = stp
    sig[...] = jnp.where(raw >= 0, 1.0, tail) / (1.0 + tail)
    a = -stp * vecs[1:2, :]
    t, u = grid2(T, T)
    same_r, same_c = hi4(t) == hi4(u), lo4(t) == lo4(u)
    aft_r = pick(ind(same_r & (u > t)), a)
    aft_c = pick(ind(same_c & (u > t)), a)
    r, c = grid2(SIDE, T)
    finr[...] = jnp.exp(pick(ind(r == hi4(c)), a))
    finc[...] = jnp.exp(pick(ind(r == lo4(c)), a))
    hx = head_spread()
    stepe[...] = spread(stp, hx, 3)
    wr[...] = spread(jnp.exp(aft_r), hx)
    wc[...] = spread(jnp.exp(aft_c), hx)
    fetch[5].wait()
    x[...] = mm(tok[...], wi[:, 0:E])
    keep(bt, (), mm(tok[...], wsel[:, 0:256]))

    def drive(sl, i, carry):
        u_ = stepe[sl] * x[sl]
        keep(ub, (sl,), u_)
        keep(wur, (sl,), wr[sl] * u_)
        keep(wuc, (sl,), wc[sl] * u_)
        return carry

    loop(T, drive)
    line_r, line_c = hi4(t) == hi4(u), lo4(t) == hi4(u)
    own[1] = mm3(only(line_c, bt), both(wuc), 0, 0)
    own[0] = mm3(only(line_r, bt), both(wur), 0, 0)
    pl.semaphore_wait(barrier, len(near))
    ends = []
    for a_, (who, mine, all_) in enumerate(((fc, finc, allc), (fr, finr, allr))):
        place_ = pl.ds(pl.multiple_of(who.me * SIDE, SIDE), SIDE)
        all_[place_] = mine[...]
        for d in range(1, TILES):
            ends.append(remote(mine, all_.at[place_], fsem.at[a_, 0, d], fsem.at[a_, 1, d], who.peer(d)[1]))
            ends[-1].start()
    for part in range(PARTS):
        fc.start(part)
        fr.start(part)

    cumr[...] = pick(ind(same_r & (u <= t)), a)
    cumc[...] = pick(ind(same_c & (u <= t)), a)

    def lines(rows, first, ends):
        k, l = grid2(rows, SIDE)
        return pick(ind(hi4(k) + first == l), spread(ends, hx), 2)

    dr[...] = lines(T, 0, finr[...])
    dc[...] = lines(T, 0, finc[...])

    z[...] = mm(tok[...], wi[:, E : 2 * E])
    keep(ct, (), mm(tok[...], wsel[:, 256:512]))
    s[...] = mm3(both(ct), both(bt), 1, 1) * (1.0 / 16.0)
    er[...] = spread(jnp.exp(cumr[...]), hx)
    ec[...] = spread(jnp.exp(cumc[...]), hx)
    cumrt[...] = cumr[...].T
    cumct[...] = cumc[...].T

    def masks(sl, i, carry):
        t_, u_ = grid2(RB, T)
        t_ = t_ + i * RB
        in_r = (hi4(t_) == hi4(u_)) & (u_ <= t_)
        in_c = (lo4(t_) == lo4(u_)) & (u_ <= t_)
        s_ = s[sl]
        c_r, c_c = cumr[sl], cumc[sl]
        for h in range(HEADS):
            l_r = jnp.exp(jnp.where(in_r, c_r[:, h : h + 1] - cumrt[h : h + 1, :], NEG))
            l_c = jnp.exp(jnp.where(in_c, c_c[:, h : h + 1] - cumct[h : h + 1, :], NEG))
            keep(mr, (h, sl), l_r * s_)
            keep(mc, (h, sl), l_c * s_)
            ls[h, sl] = l_r + l_c
        return carry

    loop(T, masks)
    low = lax.broadcasted_iota(jnp.int32, (T, 128), 1) < HDIM

    def heads(m, hp, pair, dim):
        wide = jnp.concatenate(pair, axis=1)
        part = []
        for h in (2 * hp, 2 * hp + 1):
            full = mm(m[0, h], wide, dim, 0)
            part.append(full[:, :128] + full[:, 128:] + mm(m[1, h], pair[0], dim, 0))
        return jnp.where(low, part[0], part[1])

    def within(hp, carry):
        sl = pl.ds(pl.multiple_of(hp * 128, 128), 128)
        u_ = (ub[0, :, sl], ub[1, :, sl])
        yr[:, sl] = heads(mr, hp, u_, 1)
        yc[:, sl] = heads(mc, hp, u_, 1)
        return carry

    for copy in fetch[6:]:
        copy.wait()

    for copy in ends:
        copy.wait_recv()
    k, l = grid2(T, 128)
    line = lax.shift_right_logical(k, 5) * SIDE + jnp.bitwise_and(hi4(k), 1)
    for who, all_ in ((fr, allr), (fc, allc)):
        who.dec[...] = spread(pick(ind(l == line + 2 * who.me), all_[...], 2), hx)
    for part in range(PARTS):
        fr.turn(part)
        fc.turn(part)
    lax.fori_loop(0, HEADS // 2, within, 0)
    dn[...] = mm(cot[...], wo[...], 1, 1)

    def gate(sl, i, carry):
        z_ = z[sl]
        sg = 1.0 / (1.0 + jnp.exp(-z_))
        act[sl] = z_ * sg
        z[sl] = sg * (1.0 + z_ * (1.0 - sg))
        return carry

    loop(T, gate)
    fr.finish()
    car[...] = mm3(only(line_r, ct), split(res[0], 2))
    fc.finish()
    cac[...] = mm3(only(line_c, ct), split(res[1], 2))

    skipe = spread(vecs[...], hx, 3)[2:3, :]
    gain_ = gain[...]

    def middle(sl, i, carry):
        sum_gain, sum_skip = carry
        x_, act_ = x[sl], act[sl]
        c_r, c_c = er[sl] * car[sl], ec[sl] * cac[sl]
        w_r, w_c = yr[sl], yc[sl]
        y = (w_r + w_c) + (c_r + c_c) + skipe * x_
        gated = y * act_
        inv = lax.rsqrt(jnp.mean(gated * gated, axis=-1, keepdims=True) + 1e-05)
        unit = gated * inv
        nb[sl] = (unit * gain_).astype(BF16)
        d_n = dn[sl]
        g1 = d_n * gain_
        dg = inv * (g1 - unit * jnp.mean(g1 * unit, axis=-1, keepdims=True))
        d_y = dg * act_
        dzb[sl] = (dg * y * z[sl]).astype(BF16)
        dy[sl] = d_y
        keep(dyb, (sl,), d_y)
        keep(edr, (sl,), er[sl] * d_y)
        keep(edc, (sl,), ec[sl] * d_y)
        qr[sl] = d_y * (c_r + w_r)
        qc[sl] = d_y * (c_c + w_c)
        fold = lambda v: functools.reduce(lambda p, q: p + q, [v[8 * j : 8 * j + 8] for j in range(RB // 8)])
        return sum_gain + fold(d_n * unit), sum_skip + fold(d_y * x_)

    nil = jnp.zeros((8, E), F32)
    sum_gain, sum_skip = loop(T, middle, (nil, nil))
    own[3] = mm3(only(line_c, ct), both(edc), 0, 0)
    for part in range(PARTS):
        gc_.start(part)
    own[2] = mm3(only(line_r, ct), both(edr), 0, 0)
    for part in range(PARTS):
        gr_.start(part)

    lg = mm(tok[...], dzb[...], 0, 0) * factor
    for j in range(4):
        ebuf[j * 256 : (j + 1) * 256] = lg[:, j * 128 : (j + 1) * 128]
    lg = mm(nb[...], cot[...], 0, 0) * factor
    for j in range(2):
        ebuf[1024 + j * 512 : 1024 + (j + 1) * 512] = lg[:, j * 128 : (j + 1) * 128]
    early.start(0)
    def within_back(hp, carry):
        sl = pl.ds(pl.multiple_of(hp * 128, 128), 128)
        d_ = (dyb[0, :, sl], dyb[1, :, sl])
        yr[:, sl] = heads(mr, hp, d_, 0)
        yc[:, sl] = heads(mc, hp, d_, 0)
        return carry


    def scores_back(hp, carry):
        sl = pl.ds(pl.multiple_of(hp * 128, 128), 128)
        u_h, u_l = ub[0, :, sl], ub[1, :, sl]
        twice = jnp.concatenate((u_h, u_h), axis=1)
        total = ds[...]
        for j in (0, 1):
            d_h, d_l = only(low if j == 0 else ~low, (dyb[0, :, sl], dyb[1, :, sl]))
            pairs = mm(jnp.concatenate((d_h, d_l), axis=1), twice, 1, 1) + mm(d_h, u_l, 1, 1)
            total = total + ls[2 * hp + j] * pairs
        ds[...] = total
        return carry

    lax.fori_loop(0, HEADS // 2, within_back, 0)
    for part in range(PARTS):
        gr_.turn(part)
        gc_.turn(part)
    ds[...] = jnp.zeros((T, T), F32)
    lax.fori_loop(0, HEADS // 2, scores_back, 0)
    head = u < STATE
    d_s = split(ds[...], 2)
    dce[...] = (
        jnp.where(line_r, mm3(both(edr), split(res[0], 2), 1, 1), 0.0)
        + jnp.where(line_c, mm3(both(edc), split(res[1], 2), 1, 1), 0.0)
        + jnp.where(head, mm3(d_s, both(bt)), 0.0)
    )
    dbe[...] = jnp.where(head, mm3(d_s, both(ct), 0, 0), 0.0)
    lo[...] = mm(nb[...], wo[...]).astype(BF16)

    def ahead(sl, i, carry):
        x_, se = x[sl], stepe[sl]
        u_ = se * x_
        w_r, w_c = yr[sl], yc[sl]
        w_ = w_r + w_c
        qr[sl] = qr[sl] - u_ * w_r
        qc[sl] = qc[sl] - u_ * w_c
        dux[sl] = w_ * x_
        dy[sl] = se * w_ + skipe * dy[sl]
        res[0, sl] = own[0, sl] + dr[sl] * res[0, sl]
        res[1, sl] = own[1, sl] + dc[sl] * res[1, sl]
        return carry

    loop(T, ahead)
    cumr[...] = head_sum(qr[...])
    cumc[...] = head_sum(qc[...])
    hd[...] = head_sum(dux[...])
    early.step(0)
    gr_.finish()
    g_r = split(res[2], 2)
    car[...] = mm3(only(line_r, bt), g_r)
    dbe[...] = dbe[...] + jnp.where(line_r, mm3(both(wur), g_r, 1, 1), 0.0)
    gc_.finish()
    g_c = split(res[3], 2)
    cac[...] = mm3(only(line_c, bt), g_c)
    dbe[...] = dbe[...] + jnp.where(line_c, mm3(both(wuc), g_c, 1, 1), 0.0)

    def last(sl, i, carry):
        x_ = x[sl]
        v_r, v_c = wr[sl] * car[sl], wc[sl] * cac[sl]
        qr[sl] = x_ * v_r
        qc[sl] = x_ * v_c
        dxb[sl] = (dy[sl] + stepe[sl] * (v_r + v_c)).astype(BF16)
        res[0, sl] = res[2, sl] * res[0, sl]
        res[1, sl] = res[3, sl] * res[1, sl]
        return carry

    loop(T, last)
    lg = mm(tok[...], dxb[...], 0, 0) * factor
    for j in range(4):
        lbuf[LROW[j] : LROW[j] + 256] = lg[:, j * 128 : (j + 1) * 128]
    late_core = late.copies(0)
    late_core[0].start()
    h_r, h_c = head_sum(qr[...]), head_sum(qc[...])
    d_a = (
        pick(ind(same_r & (u >= t)), cumr[...] - step[...] * h_r)
        + pick(ind(same_c & (u >= t)), cumc[...] - step[...] * h_c)
        + pick(ind(line_r), head_sum(res[0]))
        + pick(ind(line_c), head_sum(res[1]))
    )
    d_step = hd[...] + (h_r + h_c) - vecs[1:2, :] * d_a
    d_raw = d_step * sig[...]
    r, c = grid2(T, 128)
    d_ssm = (
        spread(dbe[...], ind(c == lo4(r)))
        + spread(dce[...], ind(c == 16 + lo4(r)))
        + spread(d_raw, ind(grid2(128, 128)[1] == 32 + grid2(128, 128)[0]), 3)
    )
    d_ssm = d_ssm.astype(BF16)
    lg = mm(d_ssm, tok[...], 0, 0) * factor
    for j in range(2):
        lbuf[SROW[j] : SROW[j] + 128] = lg[:, j * 128 : (j + 1) * 128]
    total_of = lambda v: jnp.sum(v, axis=0, keepdims=True)
    sum_gain = total_of(sum_gain) * factor
    for j in range(4):
        lbuf[VROW + j : VROW + j + 1] = sum_gain[:, j * 128 : (j + 1) * 128]
    lbuf[VROW + 4 : VROW + 5] = total_of(d_raw) * factor
    lbuf[VROW + 5 : VROW + 6] = -total_of(step[...] * d_a) * factor
    lbuf[VROW + 6 : VROW + 7] = total_of(head_sum(sum_skip)) * factor
    late_core[1].start()
    early.step(1)
    back = mm(dxb[...], wi[:, 0:E], 1, 1)
    late.step(0)
    back = back + mm(dzb[...], wi[:, E : 2 * E], 1, 1)
    back = back + mm(d_ssm, wpad[...], 1, 1)
    gt[...] = back.astype(BF16)
    early.step(2)
    late.step(1)
    early.step(3)
    late.step(2)
    early.step(4)
    late.step(3)
    early.step(5)
    for who in (fr, fc, gr_, gc_):
        who.drain()
    for copy in ends:
        copy.wait_send()
    late.step(4)
    early.finish(6)
    late.step(5)
    late.step(6)


def unpack(eres, lres, lo_in, gt_in, lo, gt, gi, gs, go, gb, gr, gk, gg):
    lo[...] = lo_in[...]
    gt[...] = gt_in[...]
    for j in range(4):
        gi[:, j * 128 : (j + 1) * 128] = lres[LROW[j] : LROW[j] + 256]
        gi[:, E + j * 128 : E + (j + 1) * 128] = eres[j * 256 : (j + 1) * 256]
        gg[:, j * 128 : (j + 1) * 128] = lres[VROW + j : VROW + j + 1]
    for j in range(2):
        go[:, j * 128 : (j + 1) * 128] = eres[1024 + j * 512 : 1024 + (j + 1) * 512]
        gs[:, j * 128 : (j + 1) * 128] = lres[SROW[j] : SROW[j] + 40]
    gb[...] = lres[VROW + 4 : VROW + 5, 0:HEADS]
    gr[...] = lres[VROW + 5 : VROW + 6, 0:HEADS]
    gk[...] = lres[VROW + 6 : VROW + 7, 0:HEADS]


def local(tokens_in, out_cotangent, w_inner, w_ssm, dt_bias, decay_rate, skip_gain, norm_gain, w_out):
    devices = lax.axis_size("slide") * lax.axis_size("row") * lax.axis_size("col")
    factor = float(devices * T) ** -0.5
    shape = jax.ShapeDtypeStruct
    vmem = pl.BlockSpec(memory_space=pltpu.VMEM)
    lo, gt, eres, lres = pl.pallas_call(
        functools.partial(kernel, factor),
        out_shape=(shape((T, D), BF16), shape((T, D), BF16), shape((EARLY, 128), F32), shape((LATE, 128), F32)),
        in_specs=[pl.BlockSpec(memory_space=pltpu.HBM)] * 9,
        out_specs=(vmem,) * 4,
        scratch_shapes=[kind for _, kind in SCRATCH],
        compiler_params=pltpu.CompilerParams(
            collective_id=0, has_side_effects=True, vmem_limit_bytes=48 * 2**20
        ),
    )(
        *[
            pltpu.with_memory_space_constraint(array, pltpu.HBM)
            for array in (
                tokens_in.reshape(T, D),
                out_cotangent.reshape(T, D),
                w_inner,
                w_ssm.T,
                dt_bias.reshape(1, -1),
                decay_rate.reshape(1, -1),
                skip_gain.reshape(1, -1),
                norm_gain.reshape(1, -1),
                w_out,
            )
        ]
    )
    out = pl.pallas_call(
        unpack,
        out_shape=(
            shape((T, D), BF16),
            shape((T, D), BF16),
            shape(w_inner.shape, F32),
            shape(w_ssm.shape[::-1], F32),
            shape(w_out.shape, F32),
            shape((1, HEADS), F32),
            shape((1, HEADS), F32),
            shape((1, HEADS), F32),
            shape((1, E), F32),
        ),
        in_specs=[vmem] * 4,
        out_specs=(vmem,) * 9,
        compiler_params=pltpu.CompilerParams(vmem_limit_bytes=6 * 2**20),
    )(eres, lres, lo, gt)
    return (
        out[0].reshape(tokens_in.shape),
        out[1].reshape(tokens_in.shape),
        out[2],
        out[3].T,
        out[4],
        out[5].reshape(-1),
        out[6].reshape(-1),
        out[7].reshape(-1),
        out[8].reshape(-1),
    )


def solution(mesh):
    tiles = P("slide", "row", "col", None)
    return jax.shard_map(
        local,
        mesh=mesh,
        in_specs=(tiles, tiles) + (P(),) * 7,
        out_specs=(tiles, tiles) + (P(),) * 7,
        check_vma=False,
    )
```
